32 devices in a mesh: batch: 4 (over y, x), head: 8 (over z, core).
Axes of the slice: x: 2, y: 2, z: 4, core: 2. Of those that a mesh axis runs over, the one named last changes fastest.
Arguments:
- tokens: bfloat16 [8192, 2048], P(('batch', 'head')), may hold values from -6 to 6
- cotangent: bfloat16 [8192, 2048], P(('batch', 'head')), may hold values from -6 to 6
- doc_starts: int32 [4, 4], P('batch'), may hold values from 1 to 2048, as said below
- owner: int32 [16], replicated, may hold values from 0 to 15, each once
- vectors: float32 [6, 2048], replicated, may hold values from -1 to 2
- bias_query: float32 [2048], P('head'), may hold values from -1.75 to 1.75
- bias_value: float32 [128], replicated, may hold values from -1.75 to 1.75
- bias_up: float32 [8192], P('head'), may hold values from -1.75 to 1.75
- w_query: bfloat16 [2048, 2048], P(None, 'head'), may hold values from -0.1875 to 0.1875
- w_key: bfloat16 [2048, 128], replicated, may hold values from -0.125 to 0.125
- w_value: bfloat16 [2048, 128], replicated, may hold values from -0.125 to 0.125
- w_out: bfloat16 [2048, 2048], P('head'), may hold values from -2 to 2
- w_up: bfloat16 [2048, 8192], P(None, 'head'), may hold values from -0.125 to 0.125
- w_down: bfloat16 [8192, 2048], P('head'), may hold values from -0.0625 to 0.0625
- attn_left: float32 [2, 16, 16, 128, 128], P(None, 'batch', 'head')
- attn_right: float32 [2, 16, 16, 128, 128], P(None, 'batch', 'head')
- attn_root_left: float32 [2, 16, 16, 128, 128], P(None, 'batch', 'head')
- attn_root_right: float32 [2, 16, 16, 128, 128], P(None, 'batch', 'head')
- mixer_left: float32 [2, 16, 64, 128, 128], P(None, 'batch', 'head')
- mixer_right: float32 [2, 16, 64, 128, 128], P(None, 'batch', 'head')
- mixer_root_left: float32 [2, 16, 64, 128, 128], P(None, 'batch', 'head')
- mixer_root_right: float32 [2, 16, 64, 128, 128], P(None, 'batch', 'head')
- kv_left: float32 [2, 16, 1, 128, 128], P(None, 'head')
- kv_right: float32 [2, 16, 1, 128, 128], P(None, 'head')
- kv_root_left: float32 [2, 16, 1, 128, 128], P(None, 'head')
- kv_root_right: float32 [2, 16, 1, 128, 128], P(None, 'head')
- vector_second: float32 [6, 2048], replicated
- query_second: float32 [2048], P('head')
- value_second: float32 [128], replicated
- up_second: float32 [8192], P('head')
Outputs:
- output: float32 [8192, 2048], P(('batch', 'head'))
- grad_tokens: float32 [8192, 2048], P(('batch', 'head'))
- vector_grad: float32 [6, 2048], replicated
- vector_second_new: float32 [4, 2048], replicated
- first_norm_second: float32 [2, 2048], replicated
- vector_new: float32 [6, 2048], replicated
- query_bias_grad: float32 [2048], P('head')
- query_second_new: float32 [2048], P('head')
- query_bias_new: float32 [2048], P('head')
- value_bias_grad: float32 [128], replicated
- value_second_new: float32 [128], replicated
- value_bias_new: float32 [128], replicated
- up_bias_grad: float32 [8192], P('head')
- up_second_new: float32 [8192], P('head')
- up_bias_new: float32 [8192], P('head')
- attn_grad: float32 [2, 16, 16, 128, 128], P(None, 'batch', 'head')
- attn_left_new: float32 [2, 16, 16, 128, 128], P(None, 'batch', 'head')
- attn_right_new: float32 [2, 16, 16, 128, 128], P(None, 'batch', 'head')
- attn_weight_new: float32 [2, 16, 16, 128, 128], P(None, 'batch', 'head')
- mixer_grad: float32 [2, 16, 64, 128, 128], P(None, 'batch', 'head')
- mixer_left_new: float32 [2, 16, 64, 128, 128], P(None, 'batch', 'head')
- mixer_right_new: float32 [2, 16, 64, 128, 128], P(None, 'batch', 'head')
- mixer_weight_new: float32 [2, 16, 64, 128, 128], P(None, 'batch', 'head')
- kv_grad: float32 [2, 16, 1, 128, 128], P(None, 'head')
- kv_left_new: float32 [2, 16, 1, 128, 128], P(None, 'head')
- kv_right_new: float32 [2, 16, 1, 128, 128], P(None, 'head')
- kv_weight_new: float32 [2, 16, 1, 128, 128], P(None, 'head')
The draws below stay inside these ranges and needn't reach their ends.
Inputs may be any that keep to these rules, and one draw needn't show every extreme that they name: `doc_starts`: in every draw one sequence has all its entries equal to 2048, so that it is one document; entries need not be sorted.
All inputs are finite; a program needn't handle non-finite values.
Results may differ from the reference program's by a relative error of at most 0.013.
Values may be sent and summed in bfloat16 or wider, within the bound.
A program may use at most 384 MiB of HBM per device.

```python
import math
from functools import partial
import jax
import jax.numpy as jnp
from jax import lax

WIDTH = 2048
HEADS = 16
HEAD_DIM = 128
HIDDEN_SIZE = 8192
DOC_SLOTS = 4
TILE = 128
QUERY_ROWS = 512
SEQ_LEN = 2048
SEQUENCES = 4
TOKENS = 8192
WIDTH_TILES = 16
QUERY_TILES = 16
HIDDEN_TILES = 64
HEAD_TILES = 1
OUT_FAN = 10
N_HEAD = 8


MATRIX_RATE = 0.01


def gradient_size(factor):
    return factor * math.sqrt(TOKENS)


def dominant_tiles(key, lead_shape, low_end, high_end):
    key_diag, key_off = jax.random.split(key)
    diagonal = jax.random.uniform(key_diag, lead_shape + (TILE,), jnp.float32, low_end, high_end)
    spread = jax.random.uniform(key_off, lead_shape + (TILE, TILE), jnp.float32, -1.0, 1.0) * (0.9 / TILE)
    index_row = jnp.arange(TILE)[:, None]
    index_col = jnp.arange(TILE)[None, :]
    upper = spread * (index_col > index_row).astype(jnp.float32)
    eye_tile = (index_col == index_row).astype(jnp.float32)
    return upper + jnp.swapaxes(upper, -1, -2) + diagonal[..., None] * eye_tile


def kind_column(first_value, second_value):
    return jnp.array([first_value, second_value], jnp.float32).reshape(2, 1, 1, 1, 1)


def stat_draw(key, lead_shape, grad_sizes):
    tile_stack = dominant_tiles(key, lead_shape, 1.0, 4.0)
    return tile_stack * kind_column(TILE * grad_sizes[0] ** 2, TILE * grad_sizes[1] ** 2)


def root_draw(key, lead_shape, grad_sizes, spreads):
    tile_stack = dominant_tiles(key, lead_shape, 1.0, 2.0)
    first_scale = math.sqrt(spreads[0] / (2.0 * MATRIX_RATE * grad_sizes[0]))
    second_scale = math.sqrt(spreads[1] / (2.0 * MATRIX_RATE * grad_sizes[1]))
    return tile_stack * kind_column(first_scale, second_scale)


def attn_sizes():
    return (gradient_size(0.7), gradient_size(math.sqrt(OUT_FAN / (HEADS * HEAD_DIM))))


def attn_spreads():
    return (math.sqrt(2.0 / WIDTH), math.sqrt(1.0 / OUT_FAN))


def mixer_sizes():
    return (gradient_size(0.3), gradient_size(0.6))


def mixer_spreads():
    return (math.sqrt(1.0 / WIDTH), math.sqrt(1.0 / HIDDEN_SIZE))


def kv_sizes():
    kv_factor = 2.0 * math.sqrt(WIDTH / OUT_FAN)
    return (gradient_size(kv_factor), gradient_size(kv_factor))


def kv_spreads():
    return (math.sqrt(1.0 / WIDTH), math.sqrt(1.0 / WIDTH))


def draw_attn_left(key, part):
    key = jax.random.fold_in(key, 21)
    return stat_draw(key, (2, WIDTH_TILES, QUERY_TILES), attn_sizes())


def draw_attn_right(key, part):
    key = jax.random.fold_in(key, 22)
    return stat_draw(key, (2, WIDTH_TILES, QUERY_TILES), attn_sizes())


def draw_attn_root_left(key, part):
    key = jax.random.fold_in(key, 23)
    return root_draw(key, (2, WIDTH_TILES, QUERY_TILES), attn_sizes(), attn_spreads())


def draw_attn_root_right(key, part):
    key = jax.random.fold_in(key, 24)
    return root_draw(key, (2, WIDTH_TILES, QUERY_TILES), attn_sizes(), attn_spreads())


def draw_mixer_left(key, part):
    key = jax.random.fold_in(key, 31)
    return stat_draw(key, (2, WIDTH_TILES, HIDDEN_TILES), mixer_sizes())


def draw_mixer_right(key, part):
    key = jax.random.fold_in(key, 32)
    return stat_draw(key, (2, WIDTH_TILES, HIDDEN_TILES), mixer_sizes())


def draw_mixer_root_left(key, part):
    key = jax.random.fold_in(key, 33)
    return root_draw(key, (2, WIDTH_TILES, HIDDEN_TILES), mixer_sizes(), mixer_spreads())


def draw_mixer_root_right(key, part):
    key = jax.random.fold_in(key, 34)
    return root_draw(key, (2, WIDTH_TILES, HIDDEN_TILES), mixer_sizes(), mixer_spreads())


def draw_kv_left(key, part):
    key = jax.random.fold_in(key, 41)
    return stat_draw(key, (2, WIDTH_TILES, HEAD_TILES), kv_sizes())


def draw_kv_right(key, part):
    key = jax.random.fold_in(key, 42)
    return stat_draw(key, (2, WIDTH_TILES, HEAD_TILES), kv_sizes())


def draw_kv_root_left(key, part):
    key = jax.random.fold_in(key, 43)
    return root_draw(key, (2, WIDTH_TILES, HEAD_TILES), kv_sizes(), kv_spreads())


def draw_kv_root_right(key, part):
    key = jax.random.fold_in(key, 44)
    return root_draw(key, (2, WIDTH_TILES, HEAD_TILES), kv_sizes(), kv_spreads())


def draw_vectors(key, part):
    key = jax.random.fold_in(key, 51)
    key_gain, key_shift = jax.random.split(key)
    gains = jax.random.uniform(key_gain, (6, WIDTH), jnp.float32, 0.7, 1.3)
    shifts = jax.random.uniform(key_shift, (6, WIDTH), jnp.float32, -0.5, 0.5)
    row_ids = jnp.arange(6)
    is_gain = (row_ids % 2 == 0) & (row_ids < 4)
    return jnp.where(is_gain[:, None], gains, shifts)


def draw_vector_second(key, part):
    key = jax.random.fold_in(key, 52)
    factors = jnp.array([1.5, 1.5, 0.6, 0.6, 1.2, 1.0], jnp.float32)[:, None] * math.sqrt(TOKENS)
    return factors * factors * jax.random.uniform(key, (6, WIDTH), jnp.float32, 1.0, 4.0)


def draw_query_second(key, part):
    key = jax.random.fold_in(key, 53)
    return gradient_size(1.0) ** 2 * jax.random.uniform(key, (HEADS * HEAD_DIM,), jnp.float32, 1.0, 4.0)


def draw_value_second(key, part):
    key = jax.random.fold_in(key, 54)
    return gradient_size(4.0) ** 2 * jax.random.uniform(key, (HEAD_DIM,), jnp.float32, 1.0, 4.0)


def draw_up_second(key, part):
    key = jax.random.fold_in(key, 55)
    return gradient_size(0.3) ** 2 * jax.random.uniform(key, (HIDDEN_SIZE,), jnp.float32, 1.0, 4.0)


def draw_doc_starts(key, part):
    key = jax.random.fold_in(key, 61)
    key_starts, key_whole = jax.random.split(key)
    starts = jax.random.randint(key_starts, (SEQUENCES, DOC_SLOTS), 1, SEQ_LEN + 1)
    whole_row = jax.random.randint(key_whole, (), 0, SEQUENCES)
    row_ids = jnp.arange(SEQUENCES)[:, None]
    return jnp.where(row_ids == whole_row, SEQ_LEN, starts).astype(jnp.int32)


def shard_levels(key, dims, cuts, least, high):
    factor_of = 1.0
    for axis_at, parts in cuts:
        draws = jax.random.uniform(jax.random.fold_in(jax.random.fold_in(key, 6), axis_at), (parts,), jnp.float32, least / len(cuts), high / len(cuts))
        factor_of = factor_of * jnp.repeat(jnp.exp(draws), dims[axis_at] // parts).reshape((-1,) + (1,) * (len(dims) - 1 - axis_at))
    return factor_of


def gaussian(stream_key, extent, width, limit, pieces=(), held_as=jnp.bfloat16):
    values = jax.random.normal(stream_key, extent, jnp.float32) * width
    if len(pieces) > 0:
        values = shard_levels(stream_key, extent, pieces, -0.22, 0.18) * values
    return jnp.clip(values, min=-limit, max=limit).astype(held_as)


def setup_inputs(seed: int = 0) -> dict:
    seeds = jax.random.split(jax.random.key(seed), 31)
    return {
        "tokens": gaussian(seeds[0], (TOKENS, WIDTH), 1.0, 6.0, ((0, 32),)),
        "cotangent": gaussian(seeds[1], (TOKENS, WIDTH), 1.0, 6.0, ((0, 32),)),
        "doc_starts": draw_doc_starts(jax.random.fold_in(seeds[30], 71), 0),
        "owner": jax.random.permutation(seeds[3], WIDTH_TILES).astype(jnp.int32),
        "vectors": draw_vectors(jax.random.fold_in(seeds[30], 71), 0),
        "bias_query": gaussian(seeds[5], (HEADS * HEAD_DIM,), 0.3, 1.75, ((0, 8),), jnp.float32),
        "bias_value": gaussian(seeds[6], (HEAD_DIM,), 0.3, 1.75, (), jnp.float32),
        "bias_up": gaussian(seeds[7], (HIDDEN_SIZE,), 0.3, 1.75, ((0, 8),), jnp.float32),
        "w_query": gaussian(seeds[8], (WIDTH, HEADS * HEAD_DIM), (WIDTH // 2) ** -0.5, 0.1875, ((1, 8),)),
        "w_key": gaussian(seeds[9], (WIDTH, HEAD_DIM), WIDTH ** -0.5, 0.125),
        "w_value": gaussian(seeds[10], (WIDTH, HEAD_DIM), WIDTH ** -0.5, 0.125),
        "w_out": gaussian(seeds[11], (HEADS * HEAD_DIM, WIDTH), OUT_FAN ** -0.5, 2.0, ((0, 8),)),
        "w_up": gaussian(seeds[12], (WIDTH, HIDDEN_SIZE), WIDTH ** -0.5, 0.125, ((1, 8),)),
        "w_down": gaussian(seeds[13], (HIDDEN_SIZE, WIDTH), HIDDEN_SIZE ** -0.5, 0.0625, ((0, 8),)),
        "attn_left": draw_attn_left(jax.random.fold_in(seeds[30], 71), 0),
        "attn_right": draw_attn_right(jax.random.fold_in(seeds[30], 71), 0),
        "attn_root_left": draw_attn_root_left(jax.random.fold_in(seeds[30], 71), 0),
        "attn_root_right": draw_attn_root_right(jax.random.fold_in(seeds[30], 71), 0),
        "mixer_left": draw_mixer_left(jax.random.fold_in(seeds[30], 71), 0),
        "mixer_right": draw_mixer_right(jax.random.fold_in(seeds[30], 71), 0),
        "mixer_root_left": draw_mixer_root_left(jax.random.fold_in(seeds[30], 71), 0),
        "mixer_root_right": draw_mixer_root_right(jax.random.fold_in(seeds[30], 71), 0),
        "kv_left": draw_kv_left(jax.random.fold_in(seeds[30], 71), 0),
        "kv_right": draw_kv_right(jax.random.fold_in(seeds[30], 71), 0),
        "kv_root_left": draw_kv_root_left(jax.random.fold_in(seeds[30], 71), 0),
        "kv_root_right": draw_kv_root_right(jax.random.fold_in(seeds[30], 71), 0),
        "vector_second": draw_vector_second(jax.random.fold_in(seeds[30], 71), 0),
        "query_second": draw_query_second(jax.random.fold_in(seeds[30], 71), 0),
        "value_second": draw_value_second(jax.random.fold_in(seeds[30], 71), 0),
        "up_second": draw_up_second(jax.random.fold_in(seeds[30], 71), 0),
    }


EPSILON = 1e-05
DECAY_RATE = 0.5
MATRIX_RATE = 0.01
VECTOR_RATE = 0.1
SAFE_ADD = 1e-08
PRECISE = lax.Precision.HIGHEST

@jax.custom_vjp
def low(v):
    return lax.optimization_barrier(v.astype(jnp.bfloat16)).astype(jnp.float32)

@jax.custom_vjp
def low_back(v):
    return v

def low_keep(v):
    return (low(v), None)

def low_pass(kept, grad):
    return (grad,)

def back_keep(v):
    return (v, None)

def back_low(kept, grad):
    return (low(grad),)
low.defvjp(low_keep, low_pass)
low_back.defvjp(back_keep, back_low)

def product(first_op, second_op):
    return jnp.dot(first_op, second_op, precision=PRECISE, preferred_element_type=jnp.float32)

def layer_norm(rows_in, gain, shift):
    mean_row = lax.optimization_barrier(jnp.mean(rows_in, axis=-1, keepdims=True))
    centered = rows_in - mean_row
    variance = lax.optimization_barrier(jnp.mean(centered * centered, axis=-1, keepdims=True))
    return centered * lax.rsqrt(variance + EPSILON) * gain + shift

def document_ids(starts):
    positions = jnp.arange(SEQ_LEN, dtype=jnp.int32)
    return lax.optimization_barrier(jnp.sum((starts[None, :] <= positions[:, None]).astype(jnp.int32), axis=1))

def attend_tile(query_tile, first_row, key_groups, value_groups, documents):
    positions = jnp.arange(SEQ_LEN, dtype=jnp.int32)
    row_ids = first_row + jnp.arange(QUERY_ROWS, dtype=jnp.int32)
    row_docs = lax.dynamic_slice_in_dim(documents, first_row, QUERY_ROWS, 0)
    allowed = (row_docs[:, None] == documents[None, :]) & (positions[None, :] <= row_ids[:, None])
    scores = jnp.einsum('qghd,gkd->ghqk', query_tile, key_groups, precision=PRECISE) * (1.0 / math.sqrt(HEAD_DIM))
    scores = low_back(scores)
    scores = jnp.where(allowed, scores, -1e+30)
    highest = lax.optimization_barrier(jnp.max(scores, axis=-1, keepdims=True))
    raised = jnp.exp(scores - highest)
    attention = raised / lax.optimization_barrier(jnp.sum(raised, axis=-1, keepdims=True))
    return jnp.einsum('ghqk,gkd->qghd', low(attention), value_groups, precision=PRECISE)

def forward_pass(params, rows_in, documents):
    vectors, bias_query, bias_value, bias_up, w_query, w_key, w_value, w_out, w_up, w_down = params
    normed_in = low(layer_norm(rows_in, vectors[0], vectors[1]))
    queries = low_back(low(product(normed_in, w_query) + bias_query))
    key_rows = low(product(normed_in, w_key))
    value_rows = low(product(normed_in, w_value) + bias_value)
    key_groups = low_back(jnp.broadcast_to(key_rows[None], (N_HEAD, SEQ_LEN, HEAD_DIM)))
    value_groups = low_back(jnp.broadcast_to(value_rows[None], (N_HEAD, SEQ_LEN, HEAD_DIM)))
    tile_count = SEQ_LEN // QUERY_ROWS
    query_tiles = queries.reshape(tile_count, QUERY_ROWS, N_HEAD, HEADS // N_HEAD, HEAD_DIM)
    first_rows = jnp.arange(tile_count, dtype=jnp.int32) * QUERY_ROWS
    tile_step = jax.checkpoint(attend_tile)

    def one_tile(element):
        return tile_step(element[0], element[1], key_groups, value_groups, documents)
    attended = lax.map(one_tile, (query_tiles, first_rows)).reshape(SEQ_LEN, HEADS * HEAD_DIM)
    attended = low_back(low(attended))
    resid = rows_in + low_back(product(attended, w_out) + vectors[4])
    mixer_in = low(layer_norm(resid, vectors[2], vectors[3]))
    pre_act = low_back(product(mixer_in, w_up) + bias_up)
    hidden = low(jax.nn.gelu(pre_act, approximate=True))
    return resid + low_back(product(hidden, w_down) + vectors[5])

def row_tiles(matrix):
    return matrix.reshape(matrix.shape[0] // TILE, TILE, matrix.shape[1] // TILE, TILE).transpose(0, 2, 1, 3)

def col_tiles(matrix):
    return matrix.reshape(matrix.shape[0] // TILE, TILE, matrix.shape[1] // TILE, TILE).transpose(2, 0, 1, 3)

def shampoo_update(grad_tiles, left_old, right_old, root_left, root_right, weight_tiles):
    outer_left = jnp.einsum('...ij,...kj->...ik', grad_tiles, grad_tiles, precision=PRECISE)
    outer_right = jnp.einsum('...ji,...jk->...ik', grad_tiles, grad_tiles, precision=PRECISE)
    left_new = DECAY_RATE * left_old + (1.0 - DECAY_RATE) * outer_left
    right_new = DECAY_RATE * right_old + (1.0 - DECAY_RATE) * outer_right
    stepped = jnp.einsum('...ij,...jk->...ik', root_left, grad_tiles, precision=PRECISE)
    stepped = jnp.einsum('...ij,...jk->...ik', stepped, root_right, precision=PRECISE)
    return (grad_tiles, left_new, right_new, weight_tiles - MATRIX_RATE * stepped)

def diagonal_update(gradient, second, current):
    second_new = DECAY_RATE * second + (1.0 - DECAY_RATE) * gradient * gradient
    return (gradient, second_new, current - VECTOR_RATE * gradient / (jnp.sqrt(second_new) + SAFE_ADD))

def reference(tokens, cotangent, doc_starts, owner, vectors, bias_query, bias_value, bias_up, w_query, w_key, w_value, w_out, w_up, w_down, attn_left, attn_right, attn_root_left, attn_root_right, mixer_left, mixer_right, mixer_root_left, mixer_root_right, kv_left, kv_right, kv_root_left, kv_root_right, vector_second, query_second, value_second, up_second):
    params = tuple((item.astype(jnp.float32) for item in (vectors, bias_query, bias_value, bias_up, w_query, w_key, w_value, w_out, w_up, w_down)))
    rows_all = tokens.astype(jnp.float32).reshape(SEQUENCES, SEQ_LEN, WIDTH)
    cot_all = cotangent.astype(jnp.float32).reshape(SEQUENCES, SEQ_LEN, WIDTH)

    def sequence_step(totals, element):
        seq_rows, seq_cot, starts = element
        documents = document_ids(starts)
        seq_out, pull = jax.vjp(partial(forward_pass, documents=documents), params, seq_rows)
        grad_params, grad_rows = pull(seq_cot)
        return (jax.tree.map(jnp.add, totals, grad_params), (seq_out, grad_rows))
    zeros = jax.tree.map(jnp.zeros_like, params)
    grads, (outputs, grad_rows) = lax.scan(sequence_step, zeros, (rows_all, cot_all, doc_starts))
    output = outputs.reshape(TOKENS, WIDTH)
    grad_tokens = grad_rows.reshape(TOKENS, WIDTH)
    vec_out = diagonal_update(grads[0], vector_second, params[0])
    query_out = diagonal_update(grads[1], query_second, params[1])
    value_out = diagonal_update(grads[2], value_second, params[2])
    up_out = diagonal_update(grads[3], up_second, params[3])
    attn_grad = jnp.stack([jnp.take(row_tiles(grads[4]), owner, axis=0), jnp.take(col_tiles(grads[7]), owner, axis=0)])
    attn_weight = jnp.stack([jnp.take(row_tiles(params[4]), owner, axis=0), jnp.take(col_tiles(params[7]), owner, axis=0)])
    mixer_grad = jnp.stack([jnp.take(row_tiles(grads[8]), owner, axis=0), jnp.take(col_tiles(grads[9]), owner, axis=0)])
    mixer_weight = jnp.stack([jnp.take(row_tiles(params[8]), owner, axis=0), jnp.take(col_tiles(params[9]), owner, axis=0)])
    kv_grad = jnp.stack([row_tiles(grads[5]), row_tiles(grads[6])])
    kv_weight = jnp.stack([row_tiles(params[5]), row_tiles(params[6])])
    attn_out = shampoo_update(attn_grad, attn_left, attn_right, attn_root_left, attn_root_right, attn_weight)
    mixer_out = shampoo_update(mixer_grad, mixer_left, mixer_right, mixer_root_left, mixer_root_right, mixer_weight)
    kv_out = shampoo_update(kv_grad, kv_left, kv_right, kv_root_left, kv_root_right, kv_weight)
    return (output, grad_tokens, vec_out[0], vec_out[1][2:], vec_out[1][:2], vec_out[2], query_out[0], query_out[1], query_out[2], value_out[0], value_out[1], value_out[2], up_out[0], up_out[1], up_out[2], attn_out[0], attn_out[1], attn_out[2], attn_out[3], mixer_out[0], mixer_out[1], mixer_out[2], mixer_out[3], kv_out[0], kv_out[1], kv_out[2], kv_out[3])
```

```python
from functools import partial
import math

import jax
import jax.numpy as jnp
from jax import lax
from jax.experimental import pallas as pl
from jax.experimental.pallas import tpu as pltpu
from jax.sharding import PartitionSpec as P

EPSILON = 1e-05
DECAY_RATE = 0.5
MATRIX_RATE = 0.01
VECTOR_RATE = 0.1
SAFE_ADD = 1e-08
PRECISE = lax.Precision.HIGHEST
LOG2E = math.log2(math.e)
MASKED = -1e30
TILE = 128
MESH = pl.DeviceIdType.MESH
BF16 = jnp.bfloat16
F32 = jnp.float32
VMEM_LIMIT = 56 * 1024 * 1024
ANY = pl.BlockSpec(memory_space=pl.ANY)
WHOLE = pl.BlockSpec(memory_space=pltpu.VMEM)


def matmul(first_op, second_op):
    return jnp.dot(first_op, second_op, preferred_element_type=F32)


def matmul_t(first_op, second_op):
    return lax.dot_general(
        first_op, second_op, (((0,), (0,)), ((), ())), preferred_element_type=F32
    )


def matmul_nt(first_op, second_op):
    return lax.dot_general(
        first_op, second_op, (((1,), (1,)), ((), ())), preferred_element_type=F32
    )


def norm_stats(rows_in):
    mean_row = jnp.mean(rows_in, axis=-1, keepdims=True)
    centered = rows_in - mean_row
    variance = jnp.mean(centered * centered, axis=-1, keepdims=True)
    inverse = lax.rsqrt(variance + EPSILON)
    return (centered * inverse, inverse)


def norm_back(grad_out, normed, inverse, gain):
    scaled = grad_out * gain
    mean_one = jnp.mean(scaled, axis=-1, keepdims=True)
    mean_two = jnp.mean(scaled * normed, axis=-1, keepdims=True)
    return inverse * (scaled - mean_one - normed * mean_two)


def lanes(start, size, unit):
    return pl.ds(pl.multiple_of(start, unit), size)


def greet(targets):
    barrier = pltpu.get_barrier_semaphore()
    for target in targets:
        pl.semaphore_signal(barrier, inc=1, device_id=target, device_id_type=MESH)
    pl.semaphore_wait(barrier, len(targets))


def gather_weights(w_query, w_out, bias_local, batch_size, head_count):
    rows, cols = w_query.shape
    chips = head_count // 2
    ring = batch_size == 4

    def kernel(
        q_ref, w_ref, bias_ref, q_all, w_all, bias_all, loc, zs, zr, xs, xr, fs, fr, cs, cr, bs, br
    ):
        b = lax.axis_index("batch")
        h = lax.axis_index("head")
        z = h // 2
        c = h % 2
        sibling = {"head": h + 1 - 2 * c}

        def at_chip(r):
            return {"head": lax.rem(z + r, chips) * 2 + c}

        def other(d):
            return {"head": lax.rem(h + d, head_count)}

        def peer(k):
            return {"batch": b ^ k}

        def source(r):
            return lax.rem(z - r + chips, chips) * 2 + c

        def remote(src, dst, send, recv, target):
            copy = pltpu.make_async_remote_copy(
                src_ref=src,
                dst_ref=dst,
                send_sem=send,
                recv_sem=recv,
                device_id=target,
                device_id_type=MESH,
            )
            copy.start()
            return copy

        def place_query(quarter, head, half=None):
            part = rows // batch_size
            if half is not None:
                part = part // 2
                quarter = quarter * 2 + half
            return q_all.at[lanes(quarter * part, part, part), lanes(head * cols, cols, cols)]

        def place_out(quarter, head, half=None):
            part = cols // batch_size
            if half is not None:
                part = part // 2
                quarter = quarter * 2 + half
            return w_all.at[lanes(head * cols + quarter * part, part, part), :]

        greet([other(d) for d in range(1, head_count)] + [peer(k) for k in range(1, batch_size)])
        places = (place_query, place_out)
        own = (q_all.at[:, lanes(h * cols, cols, cols)], w_all.at[lanes(h * cols, cols, cols), :])
        q_part, w_part = rows // batch_size, cols // batch_size
        mine = (
            q_ref.at[lanes(b * q_part, q_part, q_part), :],
            w_ref.at[lanes(b * w_part, w_part, w_part), :],
        )
        sent = []
        received = []

        def z_start(m):
            return [
                remote(mine[m], places[m](b, h), zs.at[m, r], zr.at[m, r], at_chip(r))
                for r in range(1, chips)
            ]

        z_copies = [z_start(0), None]
        locals_ = []
        for m, src in enumerate((q_ref, w_ref)):
            local = pltpu.make_async_copy(src, own[m], loc.at[m])
            local.start()
            locals_.append(local)
            last = remote(src, own[m], cs.at[m, batch_size, 0], cr.at[m, batch_size, 0], sibling)
            sent.append(last)
            received.append(last)
        for d in range(1, head_count):
            copy = remote(bias_ref, bias_all.at[h], bs.at[d], br.at[d], other(d))
            sent.append(copy)
            received.append(copy)
        bias_own = pltpu.make_async_copy(bias_ref, bias_all.at[h], bs.at[0])
        bias_own.start()

        direct = (1, 2) if ring else tuple(range(1, batch_size))
        for m in range(2):
            if m == 1:
                z_copies[1] = z_start(1)
            place = places[m]
            hops = {}
            for r in range(1, chips):
                z_copies[m][r - 1].wait_recv()
                spot = place(b, source(r))
                for k in direct:
                    hops[k, r] = remote(spot, spot, xs.at[m, k, r], xr.at[m, k, r], peer(k))
                    sent.append(hops[k, r])
                copy = remote(spot, spot, cs.at[m, 0, r], cr.at[m, 0, r], sibling)
                sent.append(copy)
                received.append(copy)
            halves = {}
            for r in range(1, chips):
                for k in direct:
                    hops[k, r].wait_recv()
                    if ring:
                        spot = place(b ^ k, source(r), k - 1)
                        halves[k, r] = remote(
                            spot, spot, fs.at[m, k, r], fr.at[m, k, r], peer(3 - k)
                        )
                        sent.append(halves[k, r])
                    spot = place(b ^ k, source(r))
                    copy = remote(spot, spot, cs.at[m, k, r], cr.at[m, k, r], sibling)
                    sent.append(copy)
                    received.append(copy)
            if ring:
                for r in range(1, chips):
                    for k in direct:
                        halves[k, r].wait_recv()
                    spot = place(b ^ 3, source(r))
                    copy = remote(spot, spot, cs.at[m, 3, r], cr.at[m, 3, r], sibling)
                    sent.append(copy)
                    received.append(copy)
            sent.extend(z_copies[m])
        for copy in received:
            copy.wait_recv()
        for copy in sent:
            copy.wait_send()
        for local in locals_:
            local.wait()
        bias_own.wait()

    dma = pltpu.SemaphoreType.DMA
    hop = dma((2, batch_size, chips))
    return pl.pallas_call(
        kernel,
        out_shape=(
            jax.ShapeDtypeStruct((rows, cols * head_count), w_query.dtype),
            jax.ShapeDtypeStruct((cols * head_count, w_out.shape[1]), w_out.dtype),
            jax.ShapeDtypeStruct((head_count, 1, cols), F32),
        ),
        in_specs=[ANY] * 3,
        out_specs=(ANY,) * 3,
        scratch_shapes=[
            dma((2,)),
            dma((2, chips)),
            dma((2, chips)),
            hop,
            hop,
            hop,
            hop,
            dma((2, batch_size + 1, chips)),
            dma((2, batch_size + 1, chips)),
            dma((head_count,)),
            dma((head_count,)),
        ],
        compiler_params=pltpu.CompilerParams(collective_id=0, has_side_effects=True),
        cost_estimate=pl.CostEstimate(
            flops=0, bytes_accessed=200 * 1024 * 1024, transcendentals=0
        ),
        name="gather_weights",
    )(w_query, w_out, bias_local)


def project_out(attended, weight, tokens, vectors):
    tok, width = attended.shape

    def kernel(att_ref, tok_ref, vec_ref, w_ref, resid_ref, mixer_ref, normed_ref, inverse_ref):
        resid = matmul(att_ref[...], w_ref[...]) + vec_ref[4:5, :] + tok_ref[...].astype(F32)
        normed, inverse = norm_stats(resid)
        resid_ref[...] = resid
        normed_ref[...] = normed
        inverse_ref[...] = jnp.broadcast_to(inverse, inverse_ref.shape)
        mixer_ref[...] = (normed * vec_ref[2:3, :] + vec_ref[3:4, :]).astype(BF16)

    return pl.pallas_call(
        kernel,
        out_shape=(
            jax.ShapeDtypeStruct((tok, width), F32),
            jax.ShapeDtypeStruct((tok, width), BF16),
            jax.ShapeDtypeStruct((tok, width), F32),
            jax.ShapeDtypeStruct((tok, TILE), F32),
        ),
        in_specs=[WHOLE] * 4,
        out_specs=(WHOLE,) * 4,
        compiler_params=pltpu.CompilerParams(vmem_limit_bytes=VMEM_LIMIT),
        cost_estimate=pl.CostEstimate(
            flops=2 * tok * width * width, bytes_accessed=14 * width * width, transcendentals=0
        ),
        name="project_out",
    )(attended, tokens, vectors, weight)


def attention_forward(queries, key_rows, value_turned, mask, slabs):
    tok, width = queries.shape
    seq_len, head_size = key_rows.shape
    slab = width // slabs
    heads = slab // head_size
    scale = LOG2E / math.sqrt(head_size)

    def kernel(q_ref, k_ref, v_ref, mask_ref, o_ref, log_ref):
        for j in range(heads):
            spot = slice(j * head_size, (j + 1) * head_size)
            scores = matmul_nt(k_ref[...], q_ref[:, spot]) * scale + mask_ref[...]
            highest = jnp.max(scores, axis=0, keepdims=True)
            raised = jnp.exp2(scores - highest)
            total = jnp.sum(raised, axis=0, keepdims=True)
            out = matmul(v_ref[...], raised.astype(BF16)) / total
            o_ref[:, spot] = out.T.astype(BF16)
            log_ref[0, j : j + 1, :] = highest + jnp.log2(total)

    return pl.pallas_call(
        kernel,
        grid=(slabs,),
        out_shape=(
            jax.ShapeDtypeStruct((tok, width), BF16),
            jax.ShapeDtypeStruct((slabs, heads, tok), F32),
        ),
        in_specs=[
            pl.BlockSpec((tok, slab), lambda i: (0, i)),
            pl.BlockSpec((seq_len, head_size), lambda i: (0, 0)),
            pl.BlockSpec((head_size, seq_len), lambda i: (0, 0)),
            pl.BlockSpec((seq_len, tok), lambda i: (0, 0)),
        ],
        out_specs=(
            pl.BlockSpec((tok, slab), lambda i: (0, i)),
            pl.BlockSpec((1, heads, tok), lambda i: (i, 0, 0)),
        ),
        compiler_params=pltpu.CompilerParams(vmem_limit_bytes=VMEM_LIMIT),
        cost_estimate=pl.CostEstimate(
            flops=8 * tok * seq_len * width,
            bytes_accessed=4 * tok * width,
            transcendentals=tok * seq_len * slabs * heads,
        ),
        name="attention_forward",
    )(queries, key_rows, value_turned, mask)


def attention_backward(
    queries, key_rows, key_turned, value_rows, mask, log_totals, attended, grad_attended, slabs
):
    tok, width = queries.shape
    seq_len, head_size = key_rows.shape
    slab = width // slabs
    heads = slab // head_size
    scale = LOG2E / math.sqrt(head_size)
    plain_scale = 1.0 / math.sqrt(head_size)
    block = 512 if seq_len % 512 == 0 else seq_len

    def kernel(
        q_ref, k_ref, kt_ref, v_ref, mask_ref, log_ref, o_ref, g_ref, dq_ref, dkv_ref, dk, dv
    ):
        step = pl.program_id(0)

        @pl.when(step == 0)
        def _():
            dk[...] = jnp.zeros_like(dk)
            dv[...] = jnp.zeros_like(dv)

        for j in range(heads):
            spot = slice(j * head_size, (j + 1) * head_size)
            query = q_ref[:, spot]
            grad = g_ref[:, spot]
            joint = grad.astype(F32) * o_ref[:, spot].astype(F32)
            delta = jnp.sum(joint.T, axis=0, keepdims=True)
            logs = log_ref[0, j : j + 1, :]
            total = jnp.zeros((head_size, tok), F32)
            for start in range(0, seq_len, block):
                part = slice(start, start + block)
                scores = matmul_nt(k_ref[part, :], query) * scale + mask_ref[part, :]
                probs = jnp.exp2(scores - logs)
                grad_probs = matmul_nt(v_ref[part, :], grad)
                grad_scores = (probs * (grad_probs - delta)).astype(BF16)
                dv[part, :] += matmul(probs.astype(BF16), grad)
                dk[part, :] += matmul(grad_scores, query)
                total += matmul(kt_ref[:, part], grad_scores)
            dq_ref[:, spot] = (total * plain_scale).T.astype(BF16)

        @pl.when(step == slabs - 1)
        def _():
            dkv_ref[:, :head_size] = (dk[...] * plain_scale).astype(BF16)
            dkv_ref[:, head_size:] = dv[...].astype(BF16)

    whole = lambda *shape: pl.BlockSpec(shape, lambda i: (0,) * len(shape))
    part = pl.BlockSpec((tok, slab), lambda i: (0, i))
    return pl.pallas_call(
        kernel,
        grid=(slabs,),
        out_shape=(
            jax.ShapeDtypeStruct((tok, width), BF16),
            jax.ShapeDtypeStruct((seq_len, 2 * head_size), BF16),
        ),
        in_specs=[
            part,
            whole(seq_len, head_size),
            whole(head_size, seq_len),
            whole(seq_len, head_size),
            whole(seq_len, tok),
            pl.BlockSpec((1, heads, tok), lambda i: (i, 0, 0)),
            part,
            part,
        ],
        out_specs=(part, whole(seq_len, 2 * head_size)),
        scratch_shapes=[
            pltpu.VMEM((seq_len, head_size), F32),
            pltpu.VMEM((seq_len, head_size), F32),
        ],
        compiler_params=pltpu.CompilerParams(vmem_limit_bytes=VMEM_LIMIT),
        cost_estimate=pl.CostEstimate(
            flops=20 * tok * seq_len * width,
            bytes_accessed=8 * tok * width,
            transcendentals=tok * seq_len * slabs * heads,
        ),
        name="attention_backward",
    )(queries, key_rows, key_turned, value_rows, mask, log_totals, attended, grad_attended)


def tiled_gradient(wide, narrow, owner, batch_size, pieces):
    tok, width = wide.shape
    columns = narrow.shape[1]
    per_step = width // TILE // batch_size
    piece = columns // pieces

    def kernel(owner_ref, *refs):
        del owner_ref
        wide_refs, n_ref, o_ref = refs[:per_step], refs[per_step], refs[per_step + 1]
        left = jnp.concatenate([ref[...] for ref in wide_refs], axis=1)
        result = matmul_t(left, n_ref[...])
        for i in range(pieces):
            o_ref[0, i] = result[:, i * piece : (i + 1) * piece].astype(BF16)

    def pick(j):
        return pl.BlockSpec((tok, TILE), lambda i, ids: (0, ids[i * per_step + j]))

    return pl.pallas_call(
        kernel,
        grid_spec=pltpu.PrefetchScalarGridSpec(
            num_scalar_prefetch=1,
            grid=(batch_size,),
            in_specs=[pick(j) for j in range(per_step)]
            + [pl.BlockSpec((tok, columns), lambda i, ids: (0, 0))],
            out_specs=pl.BlockSpec(
                (1, pieces, per_step * TILE, piece), lambda i, ids: (i, 0, 0, 0)
            ),
        ),
        out_shape=jax.ShapeDtypeStruct((batch_size, pieces, per_step * TILE, piece), BF16),
        compiler_params=pltpu.CompilerParams(vmem_limit_bytes=VMEM_LIMIT),
        cost_estimate=pl.CostEstimate(
            flops=2 * tok * width * columns,
            bytes_accessed=2 * (tok * width + tok * columns + width * columns),
            transcendentals=0,
        ),
        name="tiled_gradient",
    )(owner, *([wide] * per_step), narrow)


def exchange_batch(chunks, batch_size):
    b = lax.axis_index("batch")
    kept = lax.dynamic_index_in_dim(chunks, b, 0, keepdims=False)
    arrived = [
        lax.ppermute(
            lax.dynamic_index_in_dim(chunks, b ^ k, 0, keepdims=False),
            "batch",
            [(i, i ^ k) for i in range(batch_size)],
        )
        for k in range(1, batch_size)
    ]
    return [kept] + arrived


def flush(chunks, batch_size, head_count):
    chips = head_count // 2
    h = lax.axis_index("head")
    z = h // 2
    c = h % 2
    _, _, rows, cols = chunks.shape
    split = chunks.reshape(batch_size, chips, 2, rows, cols)
    keep = lax.dynamic_index_in_dim(split, c, 2, keepdims=False)
    give = lax.dynamic_index_in_dim(split, 1 - c, 2, keepdims=False)
    got = lax.ppermute(give, "head", [(i, i ^ 1) for i in range(head_count)])
    paired = (keep.astype(F32) + got.astype(F32)).astype(BF16)
    parts = exchange_batch(paired, batch_size)
    summed = sum(part.astype(F32) for part in parts).astype(BF16)
    total = lax.dynamic_index_in_dim(summed, z, 0, keepdims=False).astype(F32)
    for r in range(1, chips):
        there = lax.rem(z + r, chips)
        total += lax.ppermute(
            lax.dynamic_index_in_dim(summed, there, 0, keepdims=False),
            "head",
            [(i, (i + 2 * r) % head_count) for i in range(head_count)],
        ).astype(F32)
    return total


def scatter_rows(partial_rows, head_count):
    rows, cols = partial_rows.shape
    own = rows // head_count
    chips = head_count // 2
    stacked = partial_rows.reshape(chips, 2, own, cols)

    def kernel(x_ref, o_ref, here, pair, land, cs, cr, zs, zr):
        h = lax.axis_index("head")
        z = h // 2
        c = h % 2
        sibling = {"head": h + 1 - 2 * c}

        def at_chip(r):
            return {"head": lax.rem(z + r, chips) * 2 + c}

        greet([sibling] + [at_chip(r) for r in range(1, chips)])
        swaps = []
        for r in range(chips):
            there = lax.rem(z + chips - 1 - r, chips)
            copy = pltpu.make_async_remote_copy(
                src_ref=x_ref.at[there, 1 - c],
                dst_ref=pair.at[r],
                send_sem=cs.at[r],
                recv_sem=cr.at[r],
                device_id=sibling,
                device_id_type=MESH,
            )
            copy.start()
            swaps.append(copy)
        sends = []
        for r in range(chips - 1):
            step = chips - 1 - r
            there = lax.rem(z + step, chips)
            swaps[r].wait_recv()
            here[r] = (x_ref[there, c].astype(F32) + pair[r].astype(F32)).astype(BF16)
            copy = pltpu.make_async_remote_copy(
                src_ref=here.at[r],
                dst_ref=land.at[r],
                send_sem=zs.at[r],
                recv_sem=zr.at[r],
                device_id=at_chip(step),
                device_id_type=MESH,
            )
            copy.start()
            sends.append(copy)
        swaps[chips - 1].wait_recv()
        total = x_ref[z, c].astype(F32) + pair[chips - 1].astype(F32)
        for r in range(chips - 1):
            sends[r].wait_recv()
            total += land[r].astype(F32)
        o_ref[...] = total
        for copy in swaps + sends:
            copy.wait_send()

    dma = pltpu.SemaphoreType.DMA
    return pl.pallas_call(
        kernel,
        out_shape=jax.ShapeDtypeStruct((own, cols), F32),
        in_specs=[WHOLE],
        out_specs=WHOLE,
        scratch_shapes=[
            pltpu.VMEM((chips, own, cols), BF16),
            pltpu.VMEM((chips, own, cols), BF16),
            pltpu.VMEM((chips, own, cols), BF16),
            dma((chips,)),
            dma((chips,)),
            dma((chips,)),
            dma((chips,)),
        ],
        compiler_params=pltpu.CompilerParams(
            collective_id=1, has_side_effects=True, vmem_limit_bytes=VMEM_LIMIT
        ),
        name="scatter_rows",
    )(stacked)


def small_sums(kv_parts, vector_parts, up_parts, batch_size, head_count):
    _, chips, _, rows, cols = kv_parts.shape
    _, vrows, vcols = vector_parts.shape

    def kernel(
        kv_ref, vec_ref, up_ref, kv_out, vec_out, up_out,
        kv_pair, kv_sum, kv_land, kv_half, kv_zland, kv_own, kv_all,
        vec_land, vec_sum, vec_bland, vec_total, up_land,
        s_pair, r_pair, s_kvb, r_kvb, s_kvz, r_kvz, s_kva, r_kva,
        s_vh, r_vh, s_vb, r_vb, s_va, r_va, s_up, r_up,
    ):
        b = lax.axis_index("batch")
        h = lax.axis_index("head")
        z = h // 2
        c = h % 2
        sibling = {"head": h + 1 - 2 * c}

        def at_chip(r):
            return {"head": lax.rem(z + r, chips) * 2 + c}

        def other(d):
            return {"head": lax.rem(h + d, head_count)}

        def peer(k):
            return {"batch": b ^ k}

        def remote(src, dst, send, recv, target):
            copy = pltpu.make_async_remote_copy(
                src_ref=src, dst_ref=dst, send_sem=send, recv_sem=recv,
                device_id=target, device_id_type=MESH,
            )
            copy.start()
            return copy

        greet([other(d) for d in range(1, head_count)] + [peer(k) for k in range(1, batch_size)])
        done = []
        pair_copy = remote(kv_ref.at[1 - c], kv_pair, s_pair, r_pair, sibling)
        up_copies = [
            remote(up_ref, up_land.at[k], s_up.at[k], r_up.at[k], peer(k))
            for k in range(1, batch_size)
        ]
        vec_copies = [
            remote(
                vec_ref.at[lax.rem(h + d, head_count)], vec_land.at[d], s_vh.at[d], r_vh.at[d],
                other(d),
            )
            for d in range(1, head_count)
        ]
        pair_copy.wait_recv()
        kv_sum[...] = (kv_ref[c].astype(F32) + kv_pair[...].astype(F32)).astype(BF16)
        kv_copies = [
            remote(kv_sum.at[b ^ k], kv_land.at[k], s_kvb.at[k], r_kvb.at[k], peer(k))
            for k in range(1, batch_size)
        ]
        total = vec_ref[h]
        for copy in vec_copies:
            copy.wait_recv()
        for d in range(1, head_count):
            total += vec_land[d]
        vec_sum[...] = total
        vec_bcopies = [
            remote(vec_sum, vec_bland.at[k], s_vb.at[k], r_vb.at[k], peer(k))
            for k in range(1, batch_size)
        ]
        for copy in kv_copies:
            copy.wait_recv()
        kv_total = kv_sum[b].astype(F32)
        for k in range(1, batch_size):
            kv_total += kv_land[k].astype(F32)
        kv_half[...] = kv_total.astype(BF16)
        kv_zcopies = [
            remote(
                kv_half.at[lax.rem(z + r, chips)], kv_zland.at[r], s_kvz.at[r], r_kvz.at[r],
                at_chip(r),
            )
            for r in range(1, chips)
        ]
        for copy in vec_bcopies:
            copy.wait_recv()
        total = vec_sum[...]
        for k in range(1, batch_size):
            total += vec_bland[k]
        vec_total[h] = total
        vec_acopies = [
            remote(vec_total.at[h], vec_total.at[h], s_va.at[d], r_va.at[d], other(d))
            for d in range(1, head_count)
        ]
        up_total = up_ref[...]
        for copy in up_copies:
            copy.wait_recv()
        for k in range(1, batch_size):
            up_total += up_land[k]
        up_out[...] = up_total
        for copy in kv_zcopies:
            copy.wait_recv()
        kv_mine = kv_half[z].astype(F32)
        for r in range(1, chips):
            kv_mine += kv_zland[r].astype(F32)
        kv_all[b] = kv_mine
        kv_acopies = [
            remote(kv_all.at[b], kv_all.at[b], s_kva.at[k], r_kva.at[k], peer(k))
            for k in range(1, batch_size)
        ]
        for copy in vec_acopies + kv_acopies:
            copy.wait_recv()
        kv_out[...] = kv_all[...]
        vec_out[...] = vec_total[...]
        del kv_own
        done = [pair_copy] + up_copies + vec_copies + kv_copies + vec_bcopies
        for copy in done + kv_zcopies + vec_acopies + kv_acopies:
            copy.wait_send()

    dma = pltpu.SemaphoreType.DMA
    vm = pltpu.VMEM
    nb, nh = batch_size, head_count
    return pl.pallas_call(
        kernel,
        out_shape=(
            jax.ShapeDtypeStruct((nb, rows, cols), F32),
            jax.ShapeDtypeStruct((nh, vrows, vcols), F32),
            jax.ShapeDtypeStruct(up_parts.shape, F32),
        ),
        in_specs=[WHOLE] * 3,
        out_specs=(WHOLE,) * 3,
        scratch_shapes=[
            vm((nb, chips, rows, cols), BF16),
            vm((nb, chips, rows, cols), BF16),
            vm((nb, chips, rows, cols), BF16),
            vm((chips, rows, cols), BF16),
            vm((chips, rows, cols), BF16),
            vm((8, 128), F32),
            vm((nb, rows, cols), F32),
            vm((nh, vrows, vcols), F32),
            vm((vrows, vcols), F32),
            vm((nb, vrows, vcols), F32),
            vm((nh, vrows, vcols), F32),
            vm((nb,) + up_parts.shape, F32),
            dma, dma, dma((nb,)), dma((nb,)), dma((chips,)), dma((chips,)), dma((nb,)), dma((nb,)),
            dma((nh,)), dma((nh,)), dma((nb,)), dma((nb,)), dma((nh,)), dma((nh,)),
            dma((nb,)), dma((nb,)),
        ],
        compiler_params=pltpu.CompilerParams(
            collective_id=2, has_side_effects=True, vmem_limit_bytes=VMEM_LIMIT
        ),
        name="small_sums",
    )(kv_parts.transpose(2, 0, 1, 3, 4), vector_parts, up_parts)


def split_high(value):
    high = value.astype(BF16)
    return high, (value - high.astype(F32)).astype(BF16)


def matmul_three(first_op, second_op):
    first_high, first_low = split_high(first_op)
    second_high, second_low = split_high(second_op)
    return (
        matmul(first_high, second_high)
        + matmul(first_high, second_low)
        + matmul(first_low, second_high)
    )


def shampoo(first, second, first_weight, second_weight, owned, left, right, root_left, root_right):
    _, owned_count, columns, _, _ = left.shape
    shares = len(first)

    def kernel(ids_ref, *refs):
        del ids_ref
        one, two = refs[:shares], refs[shares : 2 * shares]
        w_one, w_two, l_ref, r_ref, p_ref, q_ref, g_out, l_out, r_out, w_out = refs[2 * shares :]

        def update(turned):
            for t in range(columns):
                spot = slice(t * TILE, (t + 1) * TILE)
                share_refs = two if turned else one
                grad = share_refs[0][:, spot].astype(F32)
                for ref in share_refs[1:]:
                    grad += ref[:, spot].astype(F32)
                if turned:
                    grad = grad.T
                    weight = w_two[spot, :].astype(F32)
                else:
                    weight = w_one[:, spot].astype(F32)
                high = grad.astype(BF16)
                g_out[0, 0, t] = grad
                l_out[0, 0, t] = DECAY_RATE * l_ref[0, 0, t] + (1.0 - DECAY_RATE) * matmul_nt(
                    high, high
                )
                r_out[0, 0, t] = DECAY_RATE * r_ref[0, 0, t] + (1.0 - DECAY_RATE) * matmul_t(
                    high, high
                )
                stepped = matmul_three(p_ref[0, 0, t], grad)
                stepped = matmul_three(stepped, q_ref[0, 0, t])
                w_out[0, 0, t] = weight - MATRIX_RATE * stepped

        @pl.when(pl.program_id(0) == 0)
        def _():
            update(False)

        @pl.when(pl.program_id(0) == 1)
        def _():
            update(True)

    last = owned_count - 1
    share_one = pl.BlockSpec(
        (TILE, columns * TILE), lambda m, p, ids: (jnp.where(m == 0, p, last), 0)
    )
    share_two = pl.BlockSpec((TILE, columns * TILE), lambda m, p, ids: (jnp.where(m == 1, p, 0), 0))
    weight_one = pl.BlockSpec(
        (TILE, columns * TILE), lambda m, p, ids: (ids[jnp.where(m == 0, p, last)], 0)
    )
    weight_two = pl.BlockSpec(
        (columns * TILE, TILE), lambda m, p, ids: (0, ids[jnp.where(m == 1, p, 0)])
    )
    stat = pl.BlockSpec((1, 1, columns, TILE, TILE), lambda m, p, ids: (m, p, 0, 0, 0))
    shape = jax.ShapeDtypeStruct(left.shape, F32)
    return pl.pallas_call(
        kernel,
        grid_spec=pltpu.PrefetchScalarGridSpec(
            num_scalar_prefetch=1,
            grid=(2, owned_count),
            in_specs=[share_one] * shares
            + [share_two] * shares
            + [weight_one, weight_two]
            + [stat] * 4,
            out_specs=[stat] * 4,
        ),
        out_shape=[shape] * 4,
        compiler_params=pltpu.CompilerParams(vmem_limit_bytes=VMEM_LIMIT),
        cost_estimate=pl.CostEstimate(
            flops=left.size * TILE * 16, bytes_accessed=left.size * 40, transcendentals=0
        ),
        name="shampoo",
    )(owned, *first, *second, first_weight, second_weight, left, right, root_left, root_right)


def shampoo_update(grad_tiles, left_old, right_old, root_left, root_right, weight_tiles):
    outer_left = jnp.einsum("...ij,...kj->...ik", grad_tiles, grad_tiles, precision=PRECISE)
    outer_right = jnp.einsum("...ji,...jk->...ik", grad_tiles, grad_tiles, precision=PRECISE)
    left_new = DECAY_RATE * left_old + (1.0 - DECAY_RATE) * outer_left
    right_new = DECAY_RATE * right_old + (1.0 - DECAY_RATE) * outer_right
    stepped = jnp.einsum("...ij,...jk->...ik", root_left, grad_tiles, precision=PRECISE)
    stepped = jnp.einsum("...ij,...jk->...ik", stepped, root_right, precision=PRECISE)
    return (grad_tiles, left_new, right_new, weight_tiles - MATRIX_RATE * stepped)


def diagonal_update(gradient, second, current):
    second_new = DECAY_RATE * second + (1.0 - DECAY_RATE) * gradient * gradient
    return (
        gradient,
        second_new,
        current - VECTOR_RATE * gradient / (jnp.sqrt(second_new) + SAFE_ADD),
    )


def gelu_pair(u):
    root = math.sqrt(2.0 / math.pi)
    square = u * u
    turn = jnp.tanh(root * u * (1.0 + 0.044715 * square))
    half = 0.5 * (1.0 + turn)
    slope = half + 0.5 * u * (1.0 - turn * turn) * root * (1.0 + 3.0 * 0.044715 * square)
    return u * half, slope


def body(
    tokens,
    cotangent,
    doc_starts,
    owner,
    vectors,
    bias_query,
    bias_value,
    bias_up,
    w_query,
    w_key,
    w_value,
    w_out,
    w_up,
    w_down,
    attn_left,
    attn_right,
    attn_root_left,
    attn_root_right,
    mixer_left,
    mixer_right,
    mixer_root_left,
    mixer_root_right,
    kv_left,
    kv_right,
    kv_root_left,
    kv_root_right,
    vector_second,
    query_second,
    value_second,
    up_second,
):
    batch_size = lax.axis_size("batch")
    head_count = lax.axis_size("head")
    batch_index = lax.axis_index("batch")
    head_index = lax.axis_index("head")
    tok_dev, width = tokens.shape
    seq_len = tok_dev * head_count
    row_start = head_index * tok_dev
    head_size = w_key.shape[1]
    slab = w_query.shape[1]
    chips = head_count // 2
    gain_one = vectors[0]
    shift_one = vectors[1]
    gain_two = vectors[2]
    bias_down = vectors[5]

    positions = jnp.arange(seq_len, dtype=jnp.int32)
    documents = jnp.sum((doc_starts[0][None, :] <= positions[:, None]).astype(jnp.int32), axis=1)
    row_ids = row_start + jnp.arange(tok_dev, dtype=jnp.int32)
    row_docs = lax.dynamic_slice_in_dim(documents, row_start, tok_dev, 0)
    allowed = (documents[:, None] == row_docs[None, :]) & (positions[:, None] <= row_ids[None, :])
    mask = jnp.where(allowed, 0.0, MASKED).astype(F32)

    rows_own = tokens.astype(F32)
    normed_one, inverse_one = norm_stats(rows_own)
    normed_in = (normed_one * gain_one + shift_one).astype(BF16)
    w_kv = jnp.concatenate([w_key, w_value], axis=1)
    kv_bias = jnp.concatenate([jnp.zeros_like(bias_value), bias_value])
    kv_own = (matmul(normed_in, w_kv) + kv_bias).astype(BF16)
    kv_all = lax.all_gather(kv_own, "head", axis=0, tiled=True)
    key_rows = kv_all[:, :head_size]
    value_rows = kv_all[:, head_size:]

    w_query_all, w_out_all, bias_all = gather_weights(
        w_query, w_out, bias_query.reshape(1, slab), batch_size, head_count
    )
    cot_all = lax.all_gather(cotangent, "head", axis=0, tiled=True)

    queries = (matmul(normed_in, w_query_all) + bias_all.reshape(1, width)).astype(BF16)
    attended, log_totals = attention_forward(queries, key_rows, value_rows.T, mask, head_count)
    attended, cot_all = lax.optimization_barrier((attended, cot_all))
    resid, mixer_in, normed_two, inverse_wide = project_out(
        attended, w_out_all, tokens, vectors
    )
    inverse_two = inverse_wide[:, :1]

    mixer_all = lax.all_gather(mixer_in, "head", axis=0, tiled=True)
    grad_hidden = matmul_nt(cot_all, w_down).astype(BF16)
    pre_act = matmul(mixer_all, w_up) + bias_up
    hidden_f, slope = gelu_pair(pre_act)
    hidden = hidden_f.astype(BF16)
    grad_pre = (grad_hidden.astype(F32) * slope).astype(BF16)
    grad_mixer_in = lax.psum_scatter(
        matmul_nt(grad_pre, w_up).astype(BF16), "head", scatter_dimension=0, tiled=True
    ).astype(F32)
    grad_down = tiled_gradient(cot_all, hidden, owner, batch_size, 1)[:, 0]
    down_shares = exchange_batch(grad_down, batch_size)
    grad_up = tiled_gradient(mixer_all, grad_pre, owner, batch_size, 1)[:, 0]
    up_shares = exchange_batch(grad_up, batch_size)
    mix_one = lax.psum_scatter(
        matmul(hidden, w_down).astype(BF16), "head", scatter_dimension=0, tiled=True
    )
    grad_up_bias = jnp.sum(grad_pre.astype(F32), axis=0)

    cot_one = cotangent.astype(F32)
    grad_resid = cot_one + norm_back(grad_mixer_in, normed_two, inverse_two, gain_two)
    grad_branch = grad_resid.astype(BF16)
    grad_attended = matmul_nt(grad_branch, w_out_all).astype(BF16)
    grad_out = tiled_gradient(grad_branch, attended, owner, batch_size, head_count)
    out_total = flush(grad_out, batch_size, head_count).astype(BF16)
    grad_q, grad_kv_part = attention_backward(
        queries,
        key_rows,
        key_rows.T,
        value_rows,
        mask,
        log_totals,
        attended,
        grad_attended,
        head_count,
    )
    grad_q, down_shares, up_shares, mix_one = lax.optimization_barrier(
        (grad_q, down_shares, up_shares, mix_one)
    )
    output = resid + mix_one.astype(F32) + bias_down
    grad_query = tiled_gradient(normed_in, grad_q, owner, batch_size, head_count)
    query_total = flush(grad_query, batch_size, head_count).astype(BF16)
    grad_kv = scatter_rows(grad_kv_part, head_count)
    grad_kv_low = grad_kv.astype(BF16)
    grad_normed_in = matmul_nt(grad_q, w_query_all) + matmul_nt(grad_kv_low, w_kv)
    grad_tokens = grad_resid + norm_back(grad_normed_in, normed_one, inverse_one, gain_one)

    kv_part = matmul_t(normed_in, grad_kv_low).astype(BF16)
    kv_rows = width // head_count // batch_size
    kv_parts = kv_part.reshape(chips, 2, batch_size, kv_rows, 2 * head_size).transpose(
        2, 0, 1, 3, 4
    )
    value_bias_row = jnp.concatenate(
        [
            jnp.sum(grad_kv_low[:, head_size:].astype(F32), axis=0),
            jnp.zeros((width - head_size,), F32),
        ]
    )
    vector_part = jnp.stack(
        [
            jnp.sum(grad_normed_in * normed_one, axis=0),
            jnp.sum(grad_normed_in, axis=0),
            jnp.sum(grad_mixer_in * normed_two, axis=0),
            jnp.sum(grad_mixer_in, axis=0),
            jnp.sum(grad_branch.astype(F32), axis=0),
            jnp.sum(cot_one, axis=0),
            jnp.sum(grad_q.astype(F32), axis=0),
            value_bias_row,
        ]
    )
    kv_total, vector_wide, up_bias_total = small_sums(
        kv_parts,
        vector_part.reshape(8, head_count, width // head_count).transpose(1, 0, 2),
        grad_up_bias.reshape(8, -1),
        batch_size,
        head_count,
    )
    kv_total = kv_total.reshape(batch_size * kv_rows, 2 * head_size)
    up_bias_total = up_bias_total.reshape(-1)
    vector_all = vector_wide.transpose(1, 0, 2).reshape(8, width)
    vector_total = vector_all[:6]
    query_bias_total = lax.dynamic_slice_in_dim(vector_all[6], head_index * slab, slab, 0)
    value_bias_total = vector_all[7, :head_size]

    owned_count = attn_left.shape[1]
    owned = lax.dynamic_slice_in_dim(owner, batch_index * owned_count, owned_count, 0)
    mixer_out = shampoo(
        up_shares,
        down_shares,
        w_up,
        w_down,
        owned,
        mixer_left,
        mixer_right,
        mixer_root_left,
        mixer_root_right,
    )
    attn_out = shampoo(
        [query_total],
        [out_total],
        w_query,
        w_out,
        owned,
        attn_left,
        attn_right,
        attn_root_left,
        attn_root_right,
    )
    kv_count = width // head_count

    def kv_tiles(matrix):
        return matrix.reshape(kv_count // TILE, TILE, head_size // TILE, TILE).transpose(0, 2, 1, 3)

    kv_slab = lax.dynamic_slice_in_dim(w_kv, head_index * kv_count, kv_count, 0).astype(F32)
    kv_out = shampoo_update(
        jnp.stack([kv_tiles(kv_total[:, :head_size]), kv_tiles(kv_total[:, head_size:])]),
        kv_left,
        kv_right,
        kv_root_left,
        kv_root_right,
        jnp.stack([kv_tiles(kv_slab[:, :head_size]), kv_tiles(kv_slab[:, head_size:])]),
    )
    vec_out = diagonal_update(vector_total, vector_second, vectors)
    query_out = diagonal_update(query_bias_total, query_second, bias_query)
    value_out = diagonal_update(value_bias_total, value_second, bias_value)
    up_out = diagonal_update(up_bias_total, up_second, bias_up)
    return (
        output,
        grad_tokens,
        vec_out[0],
        vec_out[1][2:],
        vec_out[1][:2],
        vec_out[2],
        query_out[0],
        query_out[1],
        query_out[2],
        value_out[0],
        value_out[1],
        value_out[2],
        up_out[0],
        up_out[1],
        up_out[2],
        attn_out[0],
        attn_out[1],
        attn_out[2],
        attn_out[3],
        mixer_out[0],
        mixer_out[1],
        mixer_out[2],
        mixer_out[3],
        kv_out[0],
        kv_out[1],
        kv_out[2],
        kv_out[3],
    )


def solution(mesh):
    rows = P(("batch", "head"), None)
    whole = P()
    head = P("head")
    tiles = P(None, "batch", "head", None, None)
    kv_tiles = P(None, "head", None, None, None)
    in_specs = (
        rows,
        rows,
        P("batch", None),
        whole,
        whole,
        head,
        whole,
        head,
        P(None, "head"),
        whole,
        whole,
        P("head", None),
        P(None, "head"),
        P("head", None),
        *([tiles] * 8),
        *([kv_tiles] * 4),
        whole,
        head,
        whole,
        head,
    )
    out_specs = (
        rows,
        rows,
        *([whole] * 4),
        *([head] * 3),
        *([whole] * 3),
        *([head] * 3),
        *([tiles] * 8),
        *([kv_tiles] * 4),
    )
    return jax.shard_map(body, mesh=mesh, in_specs=in_specs, out_specs=out_specs, check_vma=False)
```

```python
from functools import partial
import math

import jax
import jax.numpy as jnp
from jax import lax
from jax.experimental import pallas as pl
from jax.experimental.pallas import tpu as pltpu
from jax.sharding import PartitionSpec as P

EPSILON = 1e-05
DECAY_RATE = 0.5
MATRIX_RATE = 0.01
VECTOR_RATE = 0.1
SAFE_ADD = 1e-08
PRECISE = lax.Precision.HIGHEST
LOG2E = math.log2(math.e)
MASKED = -1e30
TILE = 128
MESH = pl.DeviceIdType.MESH
BF16 = jnp.bfloat16
F32 = jnp.float32
VMEM_LIMIT = 60 * 1024 * 1024
ANY = pl.BlockSpec(memory_space=pl.ANY)
WHOLE = pl.BlockSpec(memory_space=pltpu.VMEM)


def matmul(first_op, second_op):
    return jnp.dot(first_op, second_op, preferred_element_type=F32)


def matmul_t(first_op, second_op):
    return lax.dot_general(
        first_op, second_op, (((0,), (0,)), ((), ())), preferred_element_type=F32
    )


def matmul_nt(first_op, second_op):
    return lax.dot_general(
        first_op, second_op, (((1,), (1,)), ((), ())), preferred_element_type=F32
    )


def norm_stats(rows_in):
    mean_row = jnp.mean(rows_in, axis=-1, keepdims=True)
    centered = rows_in - mean_row
    variance = jnp.mean(centered * centered, axis=-1, keepdims=True)
    inverse = lax.rsqrt(variance + EPSILON)
    return (centered * inverse, inverse)


def norm_back(grad_out, normed, inverse, gain):
    scaled = grad_out * gain
    mean_one = jnp.mean(scaled, axis=-1, keepdims=True)
    mean_two = jnp.mean(scaled * normed, axis=-1, keepdims=True)
    return inverse * (scaled - mean_one - normed * mean_two)


def lanes(start, size, unit):
    return pl.ds(pl.multiple_of(start, unit), size)


def greet(targets):
    barrier = pltpu.get_barrier_semaphore()
    for target in targets:
        pl.semaphore_signal(barrier, inc=1, device_id=target, device_id_type=MESH)
    pl.semaphore_wait(barrier, len(targets))


def gather_weights(w_query, w_out, bias_local, batch_size, head_count):
    rows, cols = w_query.shape
    chips = head_count // 2
    ring = batch_size == 4

    def kernel(
        q_ref, w_ref, bias_ref, q_all, w_all, bias_all, loc, zs, zr, xs, xr, fs, fr, cs, cr, bs, br
    ):
        b = lax.axis_index("batch")
        h = lax.axis_index("head")
        z = h // 2
        c = h % 2
        sibling = {"head": h + 1 - 2 * c}

        def at_chip(r):
            return {"head": lax.rem(z + r, chips) * 2 + c}

        def other(d):
            return {"head": lax.rem(h + d, head_count)}

        def peer(k):
            return {"batch": b ^ k}

        def source(r):
            return lax.rem(z - r + chips, chips) * 2 + c

        def remote(src, dst, send, recv, target):
            copy = pltpu.make_async_remote_copy(
                src_ref=src,
                dst_ref=dst,
                send_sem=send,
                recv_sem=recv,
                device_id=target,
                device_id_type=MESH,
            )
            copy.start()
            return copy

        def place_query(quarter, head, half=None):
            part = rows // batch_size
            if half is not None:
                part = part // 2
                quarter = quarter * 2 + half
            return q_all.at[lanes(quarter * part, part, part), lanes(head * cols, cols, cols)]

        def place_out(quarter, head, half=None):
            part = cols // batch_size
            if half is not None:
                part = part // 2
                quarter = quarter * 2 + half
            return w_all.at[lanes(head * cols + quarter * part, part, part), :]

        greet([other(d) for d in range(1, head_count)] + [peer(k) for k in range(1, batch_size)])
        places = (place_query, place_out)
        own = (q_all.at[:, lanes(h * cols, cols, cols)], w_all.at[lanes(h * cols, cols, cols), :])
        q_part, w_part = rows // batch_size, cols // batch_size
        mine = (
            q_ref.at[lanes(b * q_part, q_part, q_part), :],
            w_ref.at[lanes(b * w_part, w_part, w_part), :],
        )
        sent = []
        received = []

        def z_start(m):
            return [
                remote(mine[m], places[m](b, h), zs.at[m, r], zr.at[m, r], at_chip(r))
                for r in range(1, chips)
            ]

        z_copies = [z_start(0), None]
        locals_ = []
        for m, src in enumerate((q_ref, w_ref)):
            local = pltpu.make_async_copy(src, own[m], loc.at[m])
            local.start()
            locals_.append(local)
            last = remote(src, own[m], cs.at[m, batch_size, 0], cr.at[m, batch_size, 0], sibling)
            sent.append(last)
            received.append(last)
        for d in range(1, head_count):
            copy = remote(bias_ref, bias_all.at[h], bs.at[d], br.at[d], other(d))
            sent.append(copy)
            received.append(copy)
        bias_own = pltpu.make_async_copy(bias_ref, bias_all.at[h], bs.at[0])
        bias_own.start()

        direct = (1, 2) if ring else tuple(range(1, batch_size))
        for m in range(2):
            if m == 1:
                z_copies[1] = z_start(1)
            place = places[m]
            hops = {}
            for r in range(1, chips):
                z_copies[m][r - 1].wait_recv()
                spot = place(b, source(r))
                for k in direct:
                    hops[k, r] = remote(spot, spot, xs.at[m, k, r], xr.at[m, k, r], peer(k))
                    sent.append(hops[k, r])
                copy = remote(spot, spot, cs.at[m, 0, r], cr.at[m, 0, r], sibling)
                sent.append(copy)
                received.append(copy)
            halves = {}
            for r in range(1, chips):
                for k in direct:
                    hops[k, r].wait_recv()
                    if ring:
                        spot = place(b ^ k, source(r), k - 1)
                        halves[k, r] = remote(
                            spot, spot, fs.at[m, k, r], fr.at[m, k, r], peer(3 - k)
                        )
                        sent.append(halves[k, r])
                    spot = place(b ^ k, source(r))
                    copy = remote(spot, spot, cs.at[m, k, r], cr.at[m, k, r], sibling)
                    sent.append(copy)
                    received.append(copy)
            if ring:
                for r in range(1, chips):
                    for k in direct:
                        halves[k, r].wait_recv()
                    spot = place(b ^ 3, source(r))
                    copy = remote(spot, spot, cs.at[m, 3, r], cr.at[m, 3, r], sibling)
                    sent.append(copy)
                    received.append(copy)
            sent.extend(z_copies[m])
        for copy in received:
            copy.wait_recv()
        for copy in sent:
            copy.wait_send()
        for local in locals_:
            local.wait()
        bias_own.wait()

    dma = pltpu.SemaphoreType.DMA
    hop = dma((2, batch_size, chips))
    return pl.pallas_call(
        kernel,
        out_shape=(
            jax.ShapeDtypeStruct((rows, cols * head_count), w_query.dtype),
            jax.ShapeDtypeStruct((cols * head_count, w_out.shape[1]), w_out.dtype),
            jax.ShapeDtypeStruct((head_count, 1, cols), F32),
        ),
        in_specs=[WHOLE] * 3,
        out_specs=(ANY,) * 3,
        scratch_shapes=[
            dma((2,)),
            dma((2, chips)),
            dma((2, chips)),
            hop,
            hop,
            hop,
            hop,
            dma((2, batch_size + 1, chips)),
            dma((2, batch_size + 1, chips)),
            dma((head_count,)),
            dma((head_count,)),
        ],
        compiler_params=pltpu.CompilerParams(collective_id=0, has_side_effects=True),
        cost_estimate=pl.CostEstimate(
            flops=0, bytes_accessed=200 * 1024 * 1024, transcendentals=0
        ),
        name="gather_weights",
    )(w_query, w_out, bias_local)


def project_out(attended, weight, tokens, vectors):
    tok, width = attended.shape

    def kernel(att_ref, tok_ref, vec_ref, w_ref, resid_ref, mixer_ref, normed_ref, inverse_ref):
        resid = matmul(att_ref[...], w_ref[...]) + vec_ref[4:5, :] + tok_ref[...].astype(F32)
        normed, inverse = norm_stats(resid)
        resid_ref[...] = resid
        normed_ref[...] = normed
        inverse_ref[...] = jnp.broadcast_to(inverse, inverse_ref.shape)
        mixer_ref[...] = (normed * vec_ref[2:3, :] + vec_ref[3:4, :]).astype(BF16)

    return pl.pallas_call(
        kernel,
        out_shape=(
            jax.ShapeDtypeStruct((tok, width), F32),
            jax.ShapeDtypeStruct((tok, width), BF16),
            jax.ShapeDtypeStruct((tok, width), F32),
            jax.ShapeDtypeStruct((tok, TILE), F32),
        ),
        in_specs=[WHOLE] * 4,
        out_specs=(WHOLE,) * 4,
        compiler_params=pltpu.CompilerParams(vmem_limit_bytes=VMEM_LIMIT),
        cost_estimate=pl.CostEstimate(
            flops=2 * tok * width * width, bytes_accessed=14 * width * width, transcendentals=0
        ),
        name="project_out",
    )(attended, tokens, vectors, weight)


def mixer_pass(mixer_in, cot_all, w_up, w_down, bias_up, owner, batch_size, head_count, cuts):
    tok, width = mixer_in.shape
    hid = w_up.shape[1]
    n = head_count // 2
    sub = tok // cuts
    block = (n, 2, cuts, sub)
    tiles = width // TILE
    owned = tiles // batch_size
    total_events = n * cuts

    def kernel(
        owner_ref, x_ref, cot_ref, up_ref, down_ref, bias_ref,
        all_ref, hid_ref, pre_ref, mix_ref, grad_up_ref, grad_down_ref, out_ref, sum_ref,
        x_buf, cot_buf, hid_buf, pre_buf, mine, give, pair_in, chain_in, right_in,
        up_acc, down_acc, stage,
        own_sem, x_sem, cot_sem, hid_sem, pre_sem, mix_sem,
        right_send, left_send, side_send, side_recv, line_recv,
        pair_send, pair_recv, chain_send, chain_recv, last_recv,
    ):
        h = lax.axis_index("head")
        z = h // 2
        c = h % 2
        has_left = z > 0
        has_right = z < n - 1

        def at(chip):
            return {"head": chip * 2 + c}

        sibling = {"head": h + 1 - 2 * c}

        def remote(src, dst, send, recv, target):
            return pltpu.make_async_remote_copy(
                src_ref=src, dst_ref=dst, send_sem=send, recv_sem=recv,
                device_id=target, device_id_type=MESH,
            )

        def row_copy(chip, g, way):
            spot = all_ref.at[chip, c, g]
            if way == 0:
                return remote(spot, spot, right_send.at[chip, g], line_recv.at[chip, g], at(z + 1))
            if way == 1:
                return remote(spot, spot, left_send.at[chip, g], line_recv.at[chip, g], at(z - 1))
            return remote(spot, spot, side_send.at[chip, g], side_recv.at[chip, g], sibling)

        def pair_copy(chip, g):
            return remote(
                give.at[chip, g], pair_in.at[chip, g], pair_send.at[chip, g],
                pair_recv.at[chip, g], sibling,
            )

        def chain_copy(chip, g, target):
            return remote(
                mine.at[chip, g], chain_in.at[chip, g], chain_send.at[chip, g],
                chain_recv.at[chip, g], at(target),
            )

        def last_copy(chip, g):
            return remote(
                mine.at[chip, g], right_in.at[g], chain_send.at[chip, g], last_recv.at[g],
                at(z - 1),
            )

        barrier = pltpu.get_barrier_semaphore()
        pl.semaphore_signal(barrier, inc=1, device_id=sibling, device_id_type=MESH)

        @pl.when(has_left)
        def _():
            pl.semaphore_signal(barrier, inc=1, device_id=at(z - 1), device_id_type=MESH)

        @pl.when(has_right)
        def _():
            pl.semaphore_signal(barrier, inc=1, device_id=at(z + 1), device_id_type=MESH)

        own = pltpu.make_async_copy(x_ref, all_ref.at[z, c], own_sem)
        own.start()
        sum_ref[...] = jnp.zeros_like(sum_ref)
        up_acc[...] = jnp.zeros_like(up_acc)
        down_acc[...] = jnp.zeros_like(down_acc)
        pl.semaphore_wait(
            barrier, 1 + has_left.astype(jnp.int32) + has_right.astype(jnp.int32)
        )
        own.wait()

        def pass_on(chip, g):
            @pl.when((chip <= z) & has_right)
            def _():
                row_copy(chip, g, 0).start()

            @pl.when((chip >= z) & has_left)
            def _():
                row_copy(chip, g, 1).start()

            row_copy(chip, g, 2).start()

        for g in range(cuts):
            pass_on(z, g)

        def compute(chip, g):
            cot_load = pltpu.make_async_copy(cot_ref.at[chip, :, g], cot_buf, cot_sem)
            cot_load.start()
            row_copy(chip, g, 2).wait_recv()
            x_load = pltpu.make_async_copy(all_ref.at[chip, :, g], x_buf, x_sem)
            x_load.start()
            cot_load.wait()
            grad_hidden = matmul_nt(cot_buf[...].reshape(2 * sub, width), down_ref[...])
            x_load.wait()
            pre_act = matmul(x_buf[...].reshape(2 * sub, width), up_ref[...]) + bias_ref[...]
            hidden, slope = gelu_pair(pre_act)
            hid_buf[...] = hidden.astype(BF16).reshape(2, sub, hid)
            hid_store = pltpu.make_async_copy(hid_buf, hid_ref.at[chip, :, g], hid_sem)
            hid_store.start()
            grad_pre = (grad_hidden * slope).astype(BF16)
            pre_buf[...] = grad_pre.reshape(2, sub, hid)
            pre_store = pltpu.make_async_copy(pre_buf, pre_ref.at[chip, :, g], pre_sem)
            pre_store.start()
            sum_ref[...] += jnp.sum(
                grad_pre.astype(F32).reshape(2 * sub // 8, 8, hid), axis=0
            )
            share = matmul_nt(grad_pre, up_ref[...]).astype(BF16).reshape(2, sub, width)

            @pl.when(c == 0)
            def _():
                mine[chip, g] = share[0]
                give[chip, g] = share[1]

            @pl.when(c == 1)
            def _():
                mine[chip, g] = share[1]
                give[chip, g] = share[0]

            pair_copy(chip, g).start()
            hid_store.wait()
            pre_store.wait()

        def nearest(i):
            edge = jnp.minimum(z, n - 1 - z)
            near = (i + 1) // 2
            inner = jnp.where(i % 2 == 1, z - near, z + near)
            far = i - edge
            outer = jnp.where(z < n - 1 - z, z + far, z - far)
            return jnp.where(i <= 2 * edge, inner, outer)

        def compute_rest(index):
            chip = nearest(index // cuts)
            g = index % cuts
            loads = [
                pltpu.make_async_copy(cot_ref.at[chip, :, g], cot_buf, cot_sem),
                pltpu.make_async_copy(hid_ref.at[chip, :, g], hid_buf, hid_sem),
                pltpu.make_async_copy(all_ref.at[chip, :, g], x_buf, x_sem),
                pltpu.make_async_copy(pre_ref.at[chip, :, g], pre_buf, pre_sem),
            ]
            for load in loads:
                load.start()
            loads[1].wait()
            hidden = hid_buf[...].reshape(2 * sub, hid)
            stage[...] = matmul(hidden, down_ref[...]).astype(BF16).reshape(2, sub, width)
            mix_store = pltpu.make_async_copy(stage, mix_ref.at[chip, :, g], mix_sem)
            mix_store.start()
            loads[0].wait()
            down_acc[...] += matmul_t(cot_buf[...].reshape(2 * sub, width), hidden).reshape(
                tiles, TILE, hid
            )
            loads[2].wait()
            loads[3].wait()
            up_acc[...] += matmul_t(
                x_buf[...].reshape(2 * sub, width), pre_buf[...].reshape(2 * sub, hid)
            ).reshape(tiles, TILE, hid)
            mix_store.wait()

        def add_up(chip, g, more):
            pair_copy(chip, g).wait_recv()
            total = mine[chip, g].astype(F32) + pair_in[chip, g].astype(F32)

            @pl.when(more)
            def _():
                chain_copy(chip, g, z).wait_recv()
                mine[chip, g] = (total + chain_in[chip, g].astype(F32)).astype(BF16)

            @pl.when(jnp.logical_not(more))
            def _():
                mine[chip, g] = total.astype(BF16)

        def step(t, carry):
            d = t // cuts
            g = t % cuts

            @pl.when((d > 0) & (z >= d))
            def _():
                row_copy(z - d, g, 0).wait_recv()
                pass_on(z - d, g)

            @pl.when((d > 0) & (z + d < n))
            def _():
                row_copy(z + d, g, 1).wait_recv()
                pass_on(z + d, g)

            def one_side(side, inner):
                chip = z + d * (2 * side - 1)

                @pl.when((chip >= 0) & (chip < n) & (d < n) & ((d > 0) | (side == 0)))
                def _():
                    compute(chip, g)

                return inner

            lax.fori_loop(0, 2, one_side, 0)

            from_left = jnp.maximum(t - z, 0)
            chip_right = from_left // cuts
            g_right = from_left % cuts

            @pl.when((t >= z) & (chip_right > z) & (chip_right < n))
            def _():
                add_up(chip_right, g_right, has_left)
                chain_copy(chip_right, g_right, z + 1).start()

            from_right = jnp.maximum(t - (n - 1 - z), 0)
            chip_left = n - 1 - from_right // cuts
            g_left = from_right % cuts

            @pl.when((t >= n - 1 - z) & (chip_left < z) & (chip_left >= 0))
            def _():
                add_up(chip_left, g_left, has_right)

                @pl.when(chip_left == z - 1)
                def _():
                    last_copy(chip_left, g_left).start()

                @pl.when(chip_left < z - 1)
                def _():
                    chain_copy(chip_left, g_left, z - 1).start()

            events = (z >= d).astype(jnp.int32) + (z + d < n).astype(jnp.int32)
            events = jnp.where((d == 0) | (d >= n), 1, events)
            ready = (events < 2) & (carry < total_events)

            @pl.when(ready)
            def _():
                compute_rest(carry)

            return carry + ready.astype(jnp.int32)

        done = lax.fori_loop(0, n * cuts + n - 1, step, 0)

        def left_over(index, carry):
            @pl.when(index >= done)
            def _():
                compute_rest(index)

            return carry

        lax.fori_loop(0, total_events, left_over, 0)

        def put_tile(p, carry):
            grad_up_ref[p] = up_acc[owner_ref[p]].astype(BF16)
            grad_down_ref[p] = down_acc[owner_ref[p]].astype(BF16)
            return carry

        lax.fori_loop(0, tiles, put_tile, 0)

        for g in range(cuts):
            pair_copy(z, g).wait_recv()
            out_ref[g] = mine[z, g].astype(F32) + pair_in[z, g].astype(F32)

            @pl.when(has_left)
            def _():
                chain_copy(z, g, z).wait_recv()
                out_ref[g] += chain_in[z, g].astype(F32)

            @pl.when(has_right)
            def _():
                last_copy(z, g).wait_recv()
                out_ref[g] += right_in[g].astype(F32)

        def finish(chip, carry):
            for g in range(cuts):

                @pl.when((chip <= z) & has_right)
                def _():
                    row_copy(chip, g, 0).wait_send()

                @pl.when((chip >= z) & has_left)
                def _():
                    row_copy(chip, g, 1).wait_send()

                row_copy(chip, g, 2).wait_send()
                pair_copy(chip, g).wait_send()

                @pl.when(chip != z)
                def _():
                    chain_copy(chip, g, z).wait_send()

            return carry

        lax.fori_loop(0, n, finish, 0)

    dma = pltpu.SemaphoreType.DMA
    vm = pltpu.VMEM
    each = dma((n, cuts))
    shares = vm((n, cuts, sub, width), BF16)
    outs = pl.pallas_call(
        kernel,
        out_shape=(
            jax.ShapeDtypeStruct(block + (width,), BF16),
            jax.ShapeDtypeStruct(block + (hid,), BF16),
            jax.ShapeDtypeStruct(block + (hid,), BF16),
            jax.ShapeDtypeStruct(block + (width,), BF16),
            jax.ShapeDtypeStruct((tiles, TILE, hid), BF16),
            jax.ShapeDtypeStruct((tiles, TILE, hid), BF16),
            jax.ShapeDtypeStruct((cuts, sub, width), F32),
            jax.ShapeDtypeStruct((8, hid), F32),
        ),
        in_specs=[pl.BlockSpec(memory_space=pltpu.SMEM), WHOLE, ANY, WHOLE, WHOLE, WHOLE],
        out_specs=(ANY, ANY, ANY, ANY, WHOLE, WHOLE, WHOLE, WHOLE),
        scratch_shapes=[
            vm((2, sub, width), BF16),
            vm((2, sub, width), BF16),
            vm((2, sub, hid), BF16),
            vm((2, sub, hid), BF16),
            shares, shares, shares, shares,
            vm((cuts, sub, width), BF16),
            vm((tiles, TILE, hid), F32),
            vm((tiles, TILE, hid), F32),
            vm((2, sub, width), BF16),
            dma, dma, dma, dma, dma, dma,
            each, each, each, each, each,
            each, each, each, each,
            dma((cuts,)),
        ],
        compiler_params=pltpu.CompilerParams(
            collective_id=3, has_side_effects=True, vmem_limit_bytes=VMEM_LIMIT
        ),
        cost_estimate=pl.CostEstimate(
            flops=12 * n * 2 * tok * width * hid, bytes_accessed=300 * 1024 * 1024, transcendentals=0
        ),
        name="mixer_pass",
    )(
        owner,
        mixer_in.reshape(cuts, sub, width),
        cot_all.reshape(block + (width,)),
        w_up,
        w_down,
        bias_up.reshape(1, hid),
    )
    _, _, _, mix_part, grad_up, grad_down, grad_in, bias_sum = outs
    return (
        mix_part.reshape(2 * n * tok, width),
        grad_up.reshape(batch_size, owned * TILE, hid),
        grad_down.reshape(batch_size, owned * TILE, hid),
        grad_in.reshape(tok, width),
        jnp.sum(bias_sum, axis=0),
    )


def attention_forward(queries, key_rows, value_turned, mask, slabs):
    tok, width = queries.shape
    seq_len, head_size = key_rows.shape
    slab = width // slabs
    heads = slab // head_size
    scale = LOG2E / math.sqrt(head_size)

    def kernel(q_ref, k_ref, v_ref, mask_ref, o_ref, log_ref):
        for j in range(heads):
            spot = slice(j * head_size, (j + 1) * head_size)
            scores = matmul_nt(k_ref[...], q_ref[:, spot]) * scale + mask_ref[...]
            highest = jnp.max(scores, axis=0, keepdims=True)
            raised = jnp.exp2(scores - highest)
            total = jnp.sum(raised, axis=0, keepdims=True)
            out = matmul(v_ref[...], raised.astype(BF16)) / total
            o_ref[:, spot] = out.T.astype(BF16)
            log_ref[0, j : j + 1, :] = highest + jnp.log2(total)

    return pl.pallas_call(
        kernel,
        grid=(slabs,),
        out_shape=(
            jax.ShapeDtypeStruct((tok, width), BF16),
            jax.ShapeDtypeStruct((slabs, heads, tok), F32),
        ),
        in_specs=[
            pl.BlockSpec((tok, slab), lambda i: (0, i)),
            pl.BlockSpec((seq_len, head_size), lambda i: (0, 0)),
            pl.BlockSpec((head_size, seq_len), lambda i: (0, 0)),
            pl.BlockSpec((seq_len, tok), lambda i: (0, 0)),
        ],
        out_specs=(
            pl.BlockSpec((tok, slab), lambda i: (0, i)),
            pl.BlockSpec((1, heads, tok), lambda i: (i, 0, 0)),
        ),
        compiler_params=pltpu.CompilerParams(vmem_limit_bytes=VMEM_LIMIT),
        cost_estimate=pl.CostEstimate(
            flops=8 * tok * seq_len * width,
            bytes_accessed=4 * tok * width,
            transcendentals=tok * seq_len * slabs * heads,
        ),
        name="attention_forward",
    )(queries, key_rows, value_turned, mask)


def attention_backward(
    queries, key_rows, key_turned, value_rows, mask, log_totals, attended, grad_attended, slabs
):
    tok, width = queries.shape
    seq_len, head_size = key_rows.shape
    slab = width // slabs
    heads = slab // head_size
    scale = LOG2E / math.sqrt(head_size)
    plain_scale = 1.0 / math.sqrt(head_size)
    block = 512 if seq_len % 512 == 0 else seq_len

    def kernel(
        q_ref, k_ref, kt_ref, v_ref, mask_ref, log_ref, o_ref, g_ref, dq_ref, dkv_ref, dk, dv
    ):
        step = pl.program_id(0)

        @pl.when(step == 0)
        def _():
            dk[...] = jnp.zeros_like(dk)
            dv[...] = jnp.zeros_like(dv)

        for j in range(heads):
            spot = slice(j * head_size, (j + 1) * head_size)
            query = q_ref[:, spot]
            grad = g_ref[:, spot]
            joint = grad.astype(F32) * o_ref[:, spot].astype(F32)
            delta = jnp.sum(joint.T, axis=0, keepdims=True)
            logs = log_ref[0, j : j + 1, :]
            total = jnp.zeros((head_size, tok), F32)
            for start in range(0, seq_len, block):
                part = slice(start, start + block)
                scores = matmul_nt(k_ref[part, :], query) * scale + mask_ref[part, :]
                probs = jnp.exp2(scores - logs)
                grad_probs = matmul_nt(v_ref[part, :], grad)
                grad_scores = (probs * (grad_probs - delta)).astype(BF16)
                dv[part, :] += matmul(probs.astype(BF16), grad)
                dk[part, :] += matmul(grad_scores, query)
                total += matmul(kt_ref[:, part], grad_scores)
            dq_ref[:, spot] = (total * plain_scale).T.astype(BF16)

        @pl.when(step == slabs - 1)
        def _():
            dkv_ref[:, :head_size] = (dk[...] * plain_scale).astype(BF16)
            dkv_ref[:, head_size:] = dv[...].astype(BF16)

    whole = lambda *shape: pl.BlockSpec(shape, lambda i: (0,) * len(shape))
    part = pl.BlockSpec((tok, slab), lambda i: (0, i))
    return pl.pallas_call(
        kernel,
        grid=(slabs,),
        out_shape=(
            jax.ShapeDtypeStruct((tok, width), BF16),
            jax.ShapeDtypeStruct((seq_len, 2 * head_size), BF16),
        ),
        in_specs=[
            part,
            whole(seq_len, head_size),
            whole(head_size, seq_len),
            whole(seq_len, head_size),
            whole(seq_len, tok),
            pl.BlockSpec((1, heads, tok), lambda i: (i, 0, 0)),
            part,
            part,
        ],
        out_specs=(part, whole(seq_len, 2 * head_size)),
        scratch_shapes=[
            pltpu.VMEM((seq_len, head_size), F32),
            pltpu.VMEM((seq_len, head_size), F32),
        ],
        compiler_params=pltpu.CompilerParams(vmem_limit_bytes=VMEM_LIMIT),
        cost_estimate=pl.CostEstimate(
            flops=20 * tok * seq_len * width,
            bytes_accessed=8 * tok * width,
            transcendentals=tok * seq_len * slabs * heads,
        ),
        name="attention_backward",
    )(queries, key_rows, key_turned, value_rows, mask, log_totals, attended, grad_attended)


def tiled_gradient(wide, narrow, owner, batch_size, pieces):
    tok, width = wide.shape
    columns = narrow.shape[1]
    per_step = width // TILE // batch_size
    piece = columns // pieces

    def kernel(owner_ref, *refs):
        del owner_ref
        wide_refs, n_ref, o_ref = refs[:per_step], refs[per_step], refs[per_step + 1]
        left = jnp.concatenate([ref[...] for ref in wide_refs], axis=1)
        result = matmul_t(left, n_ref[...])
        for i in range(pieces):
            o_ref[0, i] = result[:, i * piece : (i + 1) * piece].astype(BF16)

    def pick(j):
        return pl.BlockSpec((tok, TILE), lambda i, ids: (0, ids[i * per_step + j]))

    return pl.pallas_call(
        kernel,
        grid_spec=pltpu.PrefetchScalarGridSpec(
            num_scalar_prefetch=1,
            grid=(batch_size,),
            in_specs=[pick(j) for j in range(per_step)]
            + [pl.BlockSpec((tok, columns), lambda i, ids: (0, 0))],
            out_specs=pl.BlockSpec(
                (1, pieces, per_step * TILE, piece), lambda i, ids: (i, 0, 0, 0)
            ),
        ),
        out_shape=jax.ShapeDtypeStruct((batch_size, pieces, per_step * TILE, piece), BF16),
        compiler_params=pltpu.CompilerParams(vmem_limit_bytes=VMEM_LIMIT),
        cost_estimate=pl.CostEstimate(
            flops=2 * tok * width * columns,
            bytes_accessed=2 * (tok * width + tok * columns + width * columns),
            transcendentals=0,
        ),
        name="tiled_gradient",
    )(owner, *([wide] * per_step), narrow)


def exchange_batch(chunks, batch_size):
    b = lax.axis_index("batch")
    kept = lax.dynamic_index_in_dim(chunks, b, 0, keepdims=False)
    arrived = [
        lax.ppermute(
            lax.dynamic_index_in_dim(chunks, b ^ k, 0, keepdims=False),
            "batch",
            [(i, i ^ k) for i in range(batch_size)],
        )
        for k in range(1, batch_size)
    ]
    return [kept] + arrived


def flush(chunks, batch_size, head_count):
    chips = head_count // 2
    h = lax.axis_index("head")
    z = h // 2
    c = h % 2
    _, _, rows, cols = chunks.shape
    split = chunks.reshape(batch_size, chips, 2, rows, cols)
    keep = lax.dynamic_index_in_dim(split, c, 2, keepdims=False)
    give = lax.dynamic_index_in_dim(split, 1 - c, 2, keepdims=False)
    got = lax.ppermute(give, "head", [(i, i ^ 1) for i in range(head_count)])
    paired = (keep.astype(F32) + got.astype(F32)).astype(BF16)
    parts = exchange_batch(paired, batch_size)
    summed = sum(part.astype(F32) for part in parts).astype(BF16)
    total = lax.dynamic_index_in_dim(summed, z, 0, keepdims=False).astype(F32)
    for r in range(1, chips):
        there = lax.rem(z + r, chips)
        total += lax.ppermute(
            lax.dynamic_index_in_dim(summed, there, 0, keepdims=False),
            "head",
            [(i, (i + 2 * r) % head_count) for i in range(head_count)],
        ).astype(F32)
    return total


def scatter_rows(partial_rows, head_count):
    rows, cols = partial_rows.shape
    own = rows // head_count
    chips = head_count // 2
    stacked = partial_rows.reshape(chips, 2, own, cols)

    def kernel(x_ref, o_ref, here, pair, land, cs, cr, zs, zr):
        h = lax.axis_index("head")
        z = h // 2
        c = h % 2
        sibling = {"head": h + 1 - 2 * c}

        def at_chip(r):
            return {"head": lax.rem(z + r, chips) * 2 + c}

        greet([sibling] + [at_chip(r) for r in range(1, chips)])
        swaps = []
        for r in range(chips):
            there = lax.rem(z + chips - 1 - r, chips)
            copy = pltpu.make_async_remote_copy(
                src_ref=x_ref.at[there, 1 - c],
                dst_ref=pair.at[r],
                send_sem=cs.at[r],
                recv_sem=cr.at[r],
                device_id=sibling,
                device_id_type=MESH,
            )
            copy.start()
            swaps.append(copy)
        sends = []
        for r in range(chips - 1):
            step = chips - 1 - r
            there = lax.rem(z + step, chips)
            swaps[r].wait_recv()
            here[r] = (x_ref[there, c].astype(F32) + pair[r].astype(F32)).astype(BF16)
            copy = pltpu.make_async_remote_copy(
                src_ref=here.at[r],
                dst_ref=land.at[r],
                send_sem=zs.at[r],
                recv_sem=zr.at[r],
                device_id=at_chip(step),
                device_id_type=MESH,
            )
            copy.start()
            sends.append(copy)
        swaps[chips - 1].wait_recv()
        total = x_ref[z, c].astype(F32) + pair[chips - 1].astype(F32)
        for r in range(chips - 1):
            sends[r].wait_recv()
            total += land[r].astype(F32)
        o_ref[...] = total
        for copy in swaps + sends:
            copy.wait_send()

    dma = pltpu.SemaphoreType.DMA
    return pl.pallas_call(
        kernel,
        out_shape=jax.ShapeDtypeStruct((own, cols), F32),
        in_specs=[WHOLE],
        out_specs=WHOLE,
        scratch_shapes=[
            pltpu.VMEM((chips, own, cols), BF16),
            pltpu.VMEM((chips, own, cols), BF16),
            pltpu.VMEM((chips, own, cols), BF16),
            dma((chips,)),
            dma((chips,)),
            dma((chips,)),
            dma((chips,)),
        ],
        compiler_params=pltpu.CompilerParams(
            collective_id=1, has_side_effects=True, vmem_limit_bytes=VMEM_LIMIT
        ),
        name="scatter_rows",
    )(stacked)


def small_sums(kv_parts, vector_parts, up_parts, batch_size, head_count):
    _, chips, _, rows, cols = kv_parts.shape
    _, vrows, vcols = vector_parts.shape

    def kernel(
        kv_ref, vec_ref, up_ref, kv_out, vec_out, up_out,
        kv_pair, kv_sum, kv_land, kv_half, kv_zland, kv_own, kv_all,
        vec_land, vec_sum, vec_bland, vec_total, up_land,
        s_pair, r_pair, s_kvb, r_kvb, s_kvz, r_kvz, s_kva, r_kva,
        s_vh, r_vh, s_vb, r_vb, s_va, r_va, s_up, r_up,
    ):
        b = lax.axis_index("batch")
        h = lax.axis_index("head")
        z = h // 2
        c = h % 2
        sibling = {"head": h + 1 - 2 * c}

        def at_chip(r):
            return {"head": lax.rem(z + r, chips) * 2 + c}

        def other(d):
            return {"head": lax.rem(h + d, head_count)}

        def peer(k):
            return {"batch": b ^ k}

        def remote(src, dst, send, recv, target):
            copy = pltpu.make_async_remote_copy(
                src_ref=src, dst_ref=dst, send_sem=send, recv_sem=recv,
                device_id=target, device_id_type=MESH,
            )
            copy.start()
            return copy

        greet([other(d) for d in range(1, head_count)] + [peer(k) for k in range(1, batch_size)])
        done = []
        pair_copy = remote(kv_ref.at[1 - c], kv_pair, s_pair, r_pair, sibling)
        up_copies = [
            remote(up_ref, up_land.at[k], s_up.at[k], r_up.at[k], peer(k))
            for k in range(1, batch_size)
        ]
        vec_copies = [
            remote(
                vec_ref.at[lax.rem(h + d, head_count)], vec_land.at[d], s_vh.at[d], r_vh.at[d],
                other(d),
            )
            for d in range(1, head_count)
        ]
        pair_copy.wait_recv()
        kv_sum[...] = (kv_ref[c].astype(F32) + kv_pair[...].astype(F32)).astype(BF16)
        kv_copies = [
            remote(kv_sum.at[b ^ k], kv_land.at[k], s_kvb.at[k], r_kvb.at[k], peer(k))
            for k in range(1, batch_size)
        ]
        total = vec_ref[h]
        for copy in vec_copies:
            copy.wait_recv()
        for d in range(1, head_count):
            total += vec_land[d]
        vec_sum[...] = total
        vec_bcopies = [
            remote(vec_sum, vec_bland.at[k], s_vb.at[k], r_vb.at[k], peer(k))
            for k in range(1, batch_size)
        ]
        for copy in kv_copies:
            copy.wait_recv()
        kv_total = kv_sum[b].astype(F32)
        for k in range(1, batch_size):
            kv_total += kv_land[k].astype(F32)
        kv_half[...] = kv_total.astype(BF16)
        kv_zcopies = [
            remote(
                kv_half.at[lax.rem(z + r, chips)], kv_zland.at[r], s_kvz.at[r], r_kvz.at[r],
                at_chip(r),
            )
            for r in range(1, chips)
        ]
        for copy in vec_bcopies:
            copy.wait_recv()
        total = vec_sum[...]
        for k in range(1, batch_size):
            total += vec_bland[k]
        vec_total[h] = total
        vec_acopies = [
            remote(vec_total.at[h], vec_total.at[h], s_va.at[d], r_va.at[d], other(d))
            for d in range(1, head_count)
        ]
        up_total = up_ref[...]
        for copy in up_copies:
            copy.wait_recv()
        for k in range(1, batch_size):
            up_total += up_land[k]
        up_out[...] = up_total
        for copy in kv_zcopies:
            copy.wait_recv()
        kv_mine = kv_half[z].astype(F32)
        for r in range(1, chips):
            kv_mine += kv_zland[r].astype(F32)
        kv_all[b] = kv_mine
        kv_acopies = [
            remote(kv_all.at[b], kv_all.at[b], s_kva.at[k], r_kva.at[k], peer(k))
            for k in range(1, batch_size)
        ]
        for copy in vec_acopies + kv_acopies:
            copy.wait_recv()
        kv_out[...] = kv_all[...]
        vec_out[...] = vec_total[...]
        del kv_own
        done = [pair_copy] + up_copies + vec_copies + kv_copies + vec_bcopies
        for copy in done + kv_zcopies + vec_acopies + kv_acopies:
            copy.wait_send()

    dma = pltpu.SemaphoreType.DMA
    vm = pltpu.VMEM
    nb, nh = batch_size, head_count
    return pl.pallas_call(
        kernel,
        out_shape=(
            jax.ShapeDtypeStruct((nb, rows, cols), F32),
            jax.ShapeDtypeStruct((nh, vrows, vcols), F32),
            jax.ShapeDtypeStruct(up_parts.shape, F32),
        ),
        in_specs=[WHOLE] * 3,
        out_specs=(WHOLE,) * 3,
        scratch_shapes=[
            vm((nb, chips, rows, cols), BF16),
            vm((nb, chips, rows, cols), BF16),
            vm((nb, chips, rows, cols), BF16),
            vm((chips, rows, cols), BF16),
            vm((chips, rows, cols), BF16),
            vm((8, 128), F32),
            vm((nb, rows, cols), F32),
            vm((nh, vrows, vcols), F32),
            vm((vrows, vcols), F32),
            vm((nb, vrows, vcols), F32),
            vm((nh, vrows, vcols), F32),
            vm((nb,) + up_parts.shape, F32),
            dma, dma, dma((nb,)), dma((nb,)), dma((chips,)), dma((chips,)), dma((nb,)), dma((nb,)),
            dma((nh,)), dma((nh,)), dma((nb,)), dma((nb,)), dma((nh,)), dma((nh,)),
            dma((nb,)), dma((nb,)),
        ],
        compiler_params=pltpu.CompilerParams(
            collective_id=2, has_side_effects=True, vmem_limit_bytes=VMEM_LIMIT
        ),
        name="small_sums",
    )(kv_parts.transpose(2, 0, 1, 3, 4), vector_parts, up_parts)


def split_high(value):
    high = value.astype(BF16)
    return high, (value - high.astype(F32)).astype(BF16)


def matmul_three(first_op, second_op):
    first_high, first_low = split_high(first_op)
    second_high, second_low = split_high(second_op)
    return (
        matmul(first_high, second_high)
        + matmul(first_high, second_low)
        + matmul(first_low, second_high)
    )


def shampoo(first, second, first_weight, second_weight, owned, left, right, root_left, root_right):
    _, owned_count, columns, _, _ = left.shape
    shares = len(first)

    def kernel(ids_ref, *refs):
        del ids_ref
        one, two = refs[:shares], refs[shares : 2 * shares]
        w_one, w_two, l_ref, r_ref, p_ref, q_ref, g_out, l_out, r_out, w_out = refs[2 * shares :]

        def update(turned):
            for t in range(columns):
                spot = slice(t * TILE, (t + 1) * TILE)
                share_refs = two if turned else one
                grad = share_refs[0][:, spot].astype(F32)
                for ref in share_refs[1:]:
                    grad += ref[:, spot].astype(F32)
                if turned:
                    grad = grad.T
                    weight = w_two[spot, :].astype(F32)
                else:
                    weight = w_one[:, spot].astype(F32)
                high = grad.astype(BF16)
                g_out[0, 0, t] = grad
                l_out[0, 0, t] = DECAY_RATE * l_ref[0, 0, t] + (1.0 - DECAY_RATE) * matmul_nt(
                    high, high
                )
                r_out[0, 0, t] = DECAY_RATE * r_ref[0, 0, t] + (1.0 - DECAY_RATE) * matmul_t(
                    high, high
                )
                stepped = matmul_three(p_ref[0, 0, t], grad)
                stepped = matmul_three(stepped, q_ref[0, 0, t])
                w_out[0, 0, t] = weight - MATRIX_RATE * stepped

        @pl.when(pl.program_id(0) == 0)
        def _():
            update(False)

        @pl.when(pl.program_id(0) == 1)
        def _():
            update(True)

    last = owned_count - 1
    share_one = pl.BlockSpec(
        (TILE, columns * TILE), lambda m, p, ids: (jnp.where(m == 0, p, last), 0)
    )
    share_two = pl.BlockSpec((TILE, columns * TILE), lambda m, p, ids: (jnp.where(m == 1, p, 0), 0))
    weight_one = pl.BlockSpec(
        (TILE, columns * TILE), lambda m, p, ids: (ids[jnp.where(m == 0, p, last)], 0)
    )
    weight_two = pl.BlockSpec(
        (columns * TILE, TILE), lambda m, p, ids: (0, ids[jnp.where(m == 1, p, 0)])
    )
    stat = pl.BlockSpec((1, 1, columns, TILE, TILE), lambda m, p, ids: (m, p, 0, 0, 0))
    shape = jax.ShapeDtypeStruct(left.shape, F32)
    return pl.pallas_call(
        kernel,
        grid_spec=pltpu.PrefetchScalarGridSpec(
            num_scalar_prefetch=1,
            grid=(2, owned_count),
            in_specs=[share_one] * shares
            + [share_two] * shares
            + [weight_one, weight_two]
            + [stat] * 4,
            out_specs=[stat] * 4,
        ),
        out_shape=[shape] * 4,
        compiler_params=pltpu.CompilerParams(vmem_limit_bytes=VMEM_LIMIT),
        cost_estimate=pl.CostEstimate(
            flops=left.size * TILE * 16, bytes_accessed=left.size * 40, transcendentals=0
        ),
        name="shampoo",
    )(owned, *first, *second, first_weight, second_weight, left, right, root_left, root_right)


def shampoo_update(grad_tiles, left_old, right_old, root_left, root_right, weight_tiles):
    outer_left = jnp.einsum("...ij,...kj->...ik", grad_tiles, grad_tiles, precision=PRECISE)
    outer_right = jnp.einsum("...ji,...jk->...ik", grad_tiles, grad_tiles, precision=PRECISE)
    left_new = DECAY_RATE * left_old + (1.0 - DECAY_RATE) * outer_left
    right_new = DECAY_RATE * right_old + (1.0 - DECAY_RATE) * outer_right
    stepped = jnp.einsum("...ij,...jk->...ik", root_left, grad_tiles, precision=PRECISE)
    stepped = jnp.einsum("...ij,...jk->...ik", stepped, root_right, precision=PRECISE)
    return (grad_tiles, left_new, right_new, weight_tiles - MATRIX_RATE * stepped)


def diagonal_update(gradient, second, current):
    second_new = DECAY_RATE * second + (1.0 - DECAY_RATE) * gradient * gradient
    return (
        gradient,
        second_new,
        current - VECTOR_RATE * gradient / (jnp.sqrt(second_new) + SAFE_ADD),
    )


def gelu_pair(u):
    root = math.sqrt(2.0 / math.pi)
    square = u * u
    turn = jnp.tanh(root * u * (1.0 + 0.044715 * square))
    half = 0.5 * (1.0 + turn)
    slope = half + 0.5 * u * (1.0 - turn * turn) * root * (1.0 + 3.0 * 0.044715 * square)
    return u * half, slope


def body(
    tokens,
    cotangent,
    doc_starts,
    owner,
    vectors,
    bias_query,
    bias_value,
    bias_up,
    w_query,
    w_key,
    w_value,
    w_out,
    w_up,
    w_down,
    attn_left,
    attn_right,
    attn_root_left,
    attn_root_right,
    mixer_left,
    mixer_right,
    mixer_root_left,
    mixer_root_right,
    kv_left,
    kv_right,
    kv_root_left,
    kv_root_right,
    vector_second,
    query_second,
    value_second,
    up_second,
):
    batch_size = lax.axis_size("batch")
    head_count = lax.axis_size("head")
    batch_index = lax.axis_index("batch")
    head_index = lax.axis_index("head")
    tok_dev, width = tokens.shape
    seq_len = tok_dev * head_count
    row_start = head_index * tok_dev
    head_size = w_key.shape[1]
    slab = w_query.shape[1]
    chips = head_count // 2
    gain_one = vectors[0]
    shift_one = vectors[1]
    gain_two = vectors[2]
    bias_down = vectors[5]

    positions = jnp.arange(seq_len, dtype=jnp.int32)
    documents = jnp.sum((doc_starts[0][None, :] <= positions[:, None]).astype(jnp.int32), axis=1)
    row_ids = row_start + jnp.arange(tok_dev, dtype=jnp.int32)
    row_docs = lax.dynamic_slice_in_dim(documents, row_start, tok_dev, 0)
    allowed = (documents[:, None] == row_docs[None, :]) & (positions[:, None] <= row_ids[None, :])
    mask = jnp.where(allowed, 0.0, MASKED).astype(F32)

    rows_own = tokens.astype(F32)
    normed_one, inverse_one = norm_stats(rows_own)
    normed_in = (normed_one * gain_one + shift_one).astype(BF16)
    w_kv = jnp.concatenate([w_key, w_value], axis=1)
    kv_bias = jnp.concatenate([jnp.zeros_like(bias_value), bias_value])
    kv_own = (matmul(normed_in, w_kv) + kv_bias).astype(BF16)
    kv_all = lax.all_gather(kv_own, "head", axis=0, tiled=True)
    key_rows = kv_all[:, :head_size]
    value_rows = kv_all[:, head_size:]

    w_query_all, w_out_all, bias_all = gather_weights(
        w_query, w_out, bias_query.reshape(1, slab), batch_size, head_count
    )
    cot_all = lax.all_gather(cotangent, "head", axis=0, tiled=True)

    queries = (matmul(normed_in, w_query_all) + bias_all.reshape(1, width)).astype(BF16)
    attended, log_totals = attention_forward(queries, key_rows, value_rows.T, mask, head_count)
    attended, cot_all = lax.optimization_barrier((attended, cot_all))
    resid, mixer_in, normed_two, inverse_wide = project_out(
        attended, w_out_all, tokens, vectors
    )
    inverse_two = inverse_wide[:, :1]

    mix_part, grad_up, grad_down, grad_mixer_in, grad_up_bias = mixer_pass(
        mixer_in, cot_all, w_up, w_down, bias_up, owner, batch_size, head_count, 2
    )
    down_shares = [lax.psum_scatter(grad_down, "batch", scatter_dimension=0, tiled=False)]
    up_shares = [lax.psum_scatter(grad_up, "batch", scatter_dimension=0, tiled=False)]
    mix_one = lax.psum_scatter(mix_part, "head", scatter_dimension=0, tiled=True)

    cot_one = cotangent.astype(F32)
    grad_resid = cot_one + norm_back(grad_mixer_in, normed_two, inverse_two, gain_two)
    grad_branch = grad_resid.astype(BF16)
    grad_attended = matmul_nt(grad_branch, w_out_all).astype(BF16)
    grad_out = tiled_gradient(grad_branch, attended, owner, batch_size, head_count)
    out_total = flush(grad_out, batch_size, head_count).astype(BF16)
    grad_q, grad_kv_part = attention_backward(
        queries,
        key_rows,
        key_rows.T,
        value_rows,
        mask,
        log_totals,
        attended,
        grad_attended,
        head_count,
    )
    grad_query = tiled_gradient(normed_in, grad_q, owner, batch_size, head_count)
    query_total = flush(grad_query, batch_size, head_count).astype(BF16)
    _, down_shares, up_shares = lax.optimization_barrier((grad_query, down_shares, up_shares))
    grad_kv = scatter_rows(grad_kv_part, head_count)
    grad_kv_low = grad_kv.astype(BF16)
    grad_normed_in = matmul_nt(grad_q, w_query_all) + matmul_nt(grad_kv_low, w_kv)
    grad_tokens = grad_resid + norm_back(grad_normed_in, normed_one, inverse_one, gain_one)

    kv_part = matmul_t(normed_in, grad_kv_low).astype(BF16)
    kv_rows = width // head_count // batch_size
    kv_parts = kv_part.reshape(chips, 2, batch_size, kv_rows, 2 * head_size).transpose(
        2, 0, 1, 3, 4
    )
    value_bias_row = jnp.concatenate(
        [
            jnp.sum(grad_kv_low[:, head_size:].astype(F32), axis=0),
            jnp.zeros((width - head_size,), F32),
        ]
    )
    vector_part = jnp.stack(
        [
            jnp.sum(grad_normed_in * normed_one, axis=0),
            jnp.sum(grad_normed_in, axis=0),
            jnp.sum(grad_mixer_in * normed_two, axis=0),
            jnp.sum(grad_mixer_in, axis=0),
            jnp.sum(grad_branch.astype(F32), axis=0),
            jnp.sum(cot_one, axis=0),
            jnp.sum(grad_q.astype(F32), axis=0),
            value_bias_row,
        ]
    )
    kv_total, vector_wide, up_bias_total = small_sums(
        kv_parts,
        vector_part.reshape(8, head_count, width // head_count).transpose(1, 0, 2),
        grad_up_bias.reshape(8, -1),
        batch_size,
        head_count,
    )
    kv_total = kv_total.reshape(batch_size * kv_rows, 2 * head_size)
    up_bias_total = up_bias_total.reshape(-1)
    vector_all = vector_wide.transpose(1, 0, 2).reshape(8, width)
    vector_total = vector_all[:6]
    query_bias_total = lax.dynamic_slice_in_dim(vector_all[6], head_index * slab, slab, 0)
    value_bias_total = vector_all[7, :head_size]

    owned_count = attn_left.shape[1]
    owned = lax.dynamic_slice_in_dim(owner, batch_index * owned_count, owned_count, 0)
    mixer_out = shampoo(
        up_shares,
        down_shares,
        w_up,
        w_down,
        owned,
        mixer_left,
        mixer_right,
        mixer_root_left,
        mixer_root_right,
    )
    attn_out = shampoo(
        [query_total],
        [out_total],
        w_query,
        w_out,
        owned,
        attn_left,
        attn_right,
        attn_root_left,
        attn_root_right,
    )
    kv_count = width // head_count

    def kv_tiles(matrix):
        return matrix.reshape(kv_count // TILE, TILE, head_size // TILE, TILE).transpose(0, 2, 1, 3)

    kv_slab = lax.dynamic_slice_in_dim(w_kv, head_index * kv_count, kv_count, 0).astype(F32)
    kv_out = shampoo_update(
        jnp.stack([kv_tiles(kv_total[:, :head_size]), kv_tiles(kv_total[:, head_size:])]),
        kv_left,
        kv_right,
        kv_root_left,
        kv_root_right,
        jnp.stack([kv_tiles(kv_slab[:, :head_size]), kv_tiles(kv_slab[:, head_size:])]),
    )
    _, mix_one = lax.optimization_barrier((kv_total, mix_one))
    output = resid + mix_one.astype(F32) + bias_down
    vec_out = diagonal_update(vector_total, vector_second, vectors)
    query_out = diagonal_update(query_bias_total, query_second, bias_query)
    value_out = diagonal_update(value_bias_total, value_second, bias_value)
    up_out = diagonal_update(up_bias_total, up_second, bias_up)
    return (
        output,
        grad_tokens,
        vec_out[0],
        vec_out[1][2:],
        vec_out[1][:2],
        vec_out[2],
        query_out[0],
        query_out[1],
        query_out[2],
        value_out[0],
        value_out[1],
        value_out[2],
        up_out[0],
        up_out[1],
        up_out[2],
        attn_out[0],
        attn_out[1],
        attn_out[2],
        attn_out[3],
        mixer_out[0],
        mixer_out[1],
        mixer_out[2],
        mixer_out[3],
        kv_out[0],
        kv_out[1],
        kv_out[2],
        kv_out[3],
    )


def solution(mesh):
    rows = P(("batch", "head"), None)
    whole = P()
    head = P("head")
    tiles = P(None, "batch", "head", None, None)
    kv_tiles = P(None, "head", None, None, None)
    in_specs = (
        rows,
        rows,
        P("batch", None),
        whole,
        whole,
        head,
        whole,
        head,
        P(None, "head"),
        whole,
        whole,
        P("head", None),
        P(None, "head"),
        P("head", None),
        *([tiles] * 8),
        *([kv_tiles] * 4),
        whole,
        head,
        whole,
        head,
    )
    out_specs = (
        rows,
        rows,
        *([whole] * 4),
        *([head] * 3),
        *([whole] * 3),
        *([head] * 3),
        *([tiles] * 8),
        *([kv_tiles] * 4),
    )
    return jax.shard_map(body, mesh=mesh, in_specs=in_specs, out_specs=out_specs, check_vma=False)
```

```python
from functools import partial
import math

import jax
import jax.numpy as jnp
from jax import lax
from jax.experimental import pallas as pl
from jax.experimental.pallas import tpu as pltpu
from jax.sharding import PartitionSpec as P

EPSILON = 1e-05
DECAY_RATE = 0.5
MATRIX_RATE = 0.01
VECTOR_RATE = 0.1
SAFE_ADD = 1e-08
PRECISE = lax.Precision.HIGHEST
LOG2E = math.log2(math.e)
MASKED = -1e30
TILE = 128
MESH = pl.DeviceIdType.MESH
BF16 = jnp.bfloat16
F32 = jnp.float32
VMEM_LIMIT = 60 * 1024 * 1024
ANY = pl.BlockSpec(memory_space=pl.ANY)
WHOLE = pl.BlockSpec(memory_space=pltpu.VMEM)


def matmul(first_op, second_op):
    return jnp.dot(first_op, second_op, preferred_element_type=F32)


def matmul_t(first_op, second_op):
    return lax.dot_general(
        first_op, second_op, (((0,), (0,)), ((), ())), preferred_element_type=F32
    )


def matmul_nt(first_op, second_op):
    return lax.dot_general(
        first_op, second_op, (((1,), (1,)), ((), ())), preferred_element_type=F32
    )


def norm_stats(rows_in):
    mean_row = jnp.mean(rows_in, axis=-1, keepdims=True)
    centered = rows_in - mean_row
    variance = jnp.mean(centered * centered, axis=-1, keepdims=True)
    inverse = lax.rsqrt(variance + EPSILON)
    return (centered * inverse, inverse)


def norm_back(grad_out, normed, inverse, gain):
    scaled = grad_out * gain
    mean_one = jnp.mean(scaled, axis=-1, keepdims=True)
    mean_two = jnp.mean(scaled * normed, axis=-1, keepdims=True)
    return inverse * (scaled - mean_one - normed * mean_two)


def lanes(start, size, unit):
    return pl.ds(pl.multiple_of(start, unit), size)


def greet(targets):
    barrier = pltpu.get_barrier_semaphore()
    for target in targets:
        pl.semaphore_signal(barrier, inc=1, device_id=target, device_id_type=MESH)
    pl.semaphore_wait(barrier, len(targets))


def gather_tools(batch_size, head_count):
    chips = head_count // 2
    b = lax.axis_index("batch")
    h = lax.axis_index("head")
    z = h // 2
    c = h % 2

    def at_chip(r):
        return {"head": lax.rem(z + r, chips) * 2 + c}

    def other(d):
        return {"head": lax.rem(h + d, head_count)}

    def peer(k):
        return {"batch": b ^ k}

    def source(r):
        return lax.rem(z - r + chips, chips) * 2 + c

    def remote(src, dst, send, recv, target):
        copy = pltpu.make_async_remote_copy(
            src_ref=src,
            dst_ref=dst,
            send_sem=send,
            recv_sem=recv,
            device_id=target,
            device_id_type=MESH,
        )
        copy.start()
        return copy

    return b, h, {"head": h + 1 - 2 * c}, at_chip, other, peer, source, remote


def plane_exchange(place, tools, sems, batch_size, chips):
    b, _, sibling, _, _, peer, source, remote = tools
    xs, xr, fs, fr, cs, cr = sems
    ring = batch_size == 4
    direct = (1, 2) if ring else tuple(range(1, batch_size))
    hops = {}

    def start(r):
        spot = place(b, source(r))
        for k in direct:
            hops[k, r] = remote(spot, spot, xs.at[k, r], xr.at[k, r], peer(k))

    def finish():
        halves = {}
        sent = list(hops.values())
        received = []
        for r in range(1, chips):
            for k in direct:
                hops[k, r].wait_recv()
                if ring:
                    spot = place(b ^ k, source(r), k - 1)
                    halves[k, r] = remote(spot, spot, fs.at[k, r], fr.at[k, r], peer(3 - k))
                spot = place(b ^ k, source(r))
                received.append(remote(spot, spot, cs.at[k, r], cr.at[k, r], sibling))
        if ring:
            for r in range(1, chips):
                for k in direct:
                    halves[k, r].wait_recv()
                spot = place(b ^ 3, source(r))
                received.append(remote(spot, spot, cs.at[3, r], cr.at[3, r], sibling))
        return received, sent + received + list(halves.values())

    return start, finish


def place_rows(w_all, rows, batch_size):
    def place(quarter, head, half=None):
        part = rows // batch_size
        if half is not None:
            part = part // 2
            quarter = quarter * 2 + half
        return w_all.at[lanes(head * rows + quarter * part, part, part), :]

    return place


def gather_weights(w_query, w_out, bias_local, batch_size, head_count):
    rows, cols = w_query.shape
    chips = head_count // 2

    def kernel(
        q_ref, w_ref, bias_ref, q_all, w_all, bias_all, loc, zs, zr, ys, yr, xs, xr, fs, fr, cs, cr,
        bs, br,
    ):
        tools = gather_tools(batch_size, head_count)
        b, h, sibling, at_chip, other, peer, source, remote = tools

        def place_query(quarter, head, half=None):
            part = rows // batch_size
            if half is not None:
                part = part // 2
                quarter = quarter * 2 + half
            return q_all.at[lanes(quarter * part, part, part), lanes(head * cols, cols, cols)]

        place_out = place_rows(w_all, cols, batch_size)
        greet([other(d) for d in range(1, head_count)] + [peer(k) for k in range(1, batch_size)])
        own = (q_all.at[:, lanes(h * cols, cols, cols)], w_all.at[lanes(h * cols, cols, cols), :])
        q_part, w_part = rows // batch_size, cols // batch_size
        mine = (
            q_ref.at[lanes(b * q_part, q_part, q_part), :],
            w_ref.at[lanes(b * w_part, w_part, w_part), :],
        )
        sent = []
        received = []

        def z_start(m, place):
            copies = [
                remote(mine[m], place(b, h), zs.at[m, r], zr.at[m, r], at_chip(r))
                for r in range(1, chips)
            ]
            sent.extend(copies)
            return copies

        z_query = z_start(0, place_query)
        locals_ = []
        for m, src in enumerate((q_ref, w_ref)):
            local = pltpu.make_async_copy(src, own[m], loc.at[m])
            local.start()
            locals_.append(local)
            last = remote(src, own[m], ys.at[m, 0], yr.at[m, 0], sibling)
            sent.append(last)
            received.append(last)
        for d in range(1, head_count):
            copy = remote(bias_ref, bias_all.at[h], bs.at[d], br.at[d], other(d))
            sent.append(copy)
            received.append(copy)
        bias_own = pltpu.make_async_copy(bias_ref, bias_all.at[h], bs.at[0])
        bias_own.start()

        start, finish = plane_exchange(
            place_query, tools, (xs, xr, fs, fr, cs, cr), batch_size, chips
        )

        def across(m, place, r):
            spot = place(b, source(r))
            copy = remote(spot, spot, ys.at[m, r], yr.at[m, r], sibling)
            sent.append(copy)
            received.append(copy)

        for r in range(1, chips):
            z_query[r - 1].wait_recv()
            start(r)
            across(0, place_query, r)
        z_out = z_start(1, place_out)
        more_received, more_sent = finish()
        received.extend(more_received)
        sent.extend(more_sent)
        for r in range(1, chips):
            z_out[r - 1].wait_recv()
            across(1, place_out, r)
        for copy in received:
            copy.wait_recv()
        for copy in sent:
            copy.wait_send()
        for local in locals_:
            local.wait()
        bias_own.wait()

    dma = pltpu.SemaphoreType.DMA
    hop = dma((batch_size, chips))
    two = dma((2, chips))
    return pl.pallas_call(
        kernel,
        out_shape=(
            jax.ShapeDtypeStruct((rows, cols * head_count), w_query.dtype),
            jax.ShapeDtypeStruct((cols * head_count, w_out.shape[1]), w_out.dtype),
            jax.ShapeDtypeStruct((head_count, 1, cols), F32),
        ),
        in_specs=[WHOLE] * 3,
        out_specs=(ANY,) * 3,
        scratch_shapes=[
            dma((2,)), two, two, two, two, hop, hop, hop, hop, hop, hop,
            dma((head_count,)), dma((head_count,)),
        ],
        compiler_params=pltpu.CompilerParams(collective_id=0, has_side_effects=True),
        cost_estimate=pl.CostEstimate(
            flops=0, bytes_accessed=120 * 1024 * 1024, transcendentals=0
        ),
        name="gather_weights",
    )(w_query, w_out, bias_local)


def gather_rest(w_all, batch_size, head_count):
    chips = head_count // 2
    rows = w_all.shape[0] // head_count

    def kernel(in_ref, w_ref, xs, xr, fs, fr, cs, cr):
        del in_ref
        tools = gather_tools(batch_size, head_count)
        _, _, sibling, _, _, peer, _, _ = tools
        greet([sibling] + [peer(k) for k in range(1, batch_size)])
        start, finish = plane_exchange(
            place_rows(w_ref, rows, batch_size), tools, (xs, xr, fs, fr, cs, cr), batch_size, chips
        )
        for r in range(1, chips):
            start(r)
        received, sent = finish()
        for copy in received:
            copy.wait_recv()
        for copy in sent:
            copy.wait_send()

    hop = pltpu.SemaphoreType.DMA((batch_size, chips))
    return pl.pallas_call(
        kernel,
        out_shape=jax.ShapeDtypeStruct(w_all.shape, w_all.dtype),
        in_specs=[ANY],
        out_specs=ANY,
        scratch_shapes=[hop] * 6,
        input_output_aliases={0: 0},
        compiler_params=pltpu.CompilerParams(collective_id=5, has_side_effects=True),
        cost_estimate=pl.CostEstimate(
            flops=0, bytes_accessed=100 * 1024 * 1024, transcendentals=0
        ),
        name="gather_rest",
    )(w_all)


def project_out(attended, weight, tokens, vectors):
    tok, width = attended.shape

    def kernel(att_ref, tok_ref, vec_ref, w_ref, resid_ref, mixer_ref, normed_ref, inverse_ref):
        resid = matmul(att_ref[...], w_ref[...]) + vec_ref[4:5, :] + tok_ref[...].astype(F32)
        normed, inverse = norm_stats(resid)
        resid_ref[...] = resid
        normed_ref[...] = normed
        inverse_ref[...] = jnp.broadcast_to(inverse, inverse_ref.shape)
        mixer_ref[...] = (normed * vec_ref[2:3, :] + vec_ref[3:4, :]).astype(BF16)

    return pl.pallas_call(
        kernel,
        out_shape=(
            jax.ShapeDtypeStruct((tok, width), F32),
            jax.ShapeDtypeStruct((tok, width), BF16),
            jax.ShapeDtypeStruct((tok, width), F32),
            jax.ShapeDtypeStruct((tok, TILE), F32),
        ),
        in_specs=[WHOLE] * 4,
        out_specs=(WHOLE,) * 4,
        compiler_params=pltpu.CompilerParams(vmem_limit_bytes=VMEM_LIMIT),
        cost_estimate=pl.CostEstimate(
            flops=2 * tok * width * width, bytes_accessed=14 * width * width, transcendentals=0
        ),
        name="project_out",
    )(attended, tokens, vectors, weight)


def mixer_pass(mixer_in, cot_all, w_up, w_down, bias_up, owner, batch_size, head_count, cuts):
    tok, width = mixer_in.shape
    hid = w_up.shape[1]
    n = head_count // 2
    sub = tok // cuts
    block = (n, 2, cuts, sub)
    tiles = width // TILE
    owned = tiles // batch_size
    total_events = n * cuts

    def kernel(
        owner_ref, x_ref, cot_ref, up_ref, down_ref, bias_ref,
        all_ref, hid_ref, pre_ref, mix_ref, grad_up_ref, down_ref_all, out_ref, sum_ref,
        x_buf, cot_buf, hid_buf, pre_buf, mine, give, pair_in, chain_in, right_in,
        up_acc, down_acc, stage, grad_down_ref,
        own_sem, x_sem, cot_sem, hid_sem, pre_sem, mix_sem,
        right_send, left_send, side_send, side_recv, line_recv,
        pair_send, pair_recv, chain_send, chain_recv, last_recv, down_send, down_recv, down_sem,
    ):
        h = lax.axis_index("head")
        z = h // 2
        c = h % 2
        has_left = z > 0
        has_right = z < n - 1

        def at(chip):
            return {"head": chip * 2 + c}

        sibling = {"head": h + 1 - 2 * c}

        def remote(src, dst, send, recv, target):
            return pltpu.make_async_remote_copy(
                src_ref=src, dst_ref=dst, send_sem=send, recv_sem=recv,
                device_id=target, device_id_type=MESH,
            )

        def row_copy(chip, g, way):
            spot = all_ref.at[chip, c, g]
            if way == 0:
                return remote(spot, spot, right_send.at[chip, g], line_recv.at[chip, g], at(z + 1))
            if way == 1:
                return remote(spot, spot, left_send.at[chip, g], line_recv.at[chip, g], at(z - 1))
            return remote(spot, spot, side_send.at[chip, g], side_recv.at[chip, g], sibling)

        def pair_copy(chip, g):
            return remote(
                give.at[chip, g], pair_in.at[chip, g], pair_send.at[chip, g],
                pair_recv.at[chip, g], sibling,
            )

        def chain_copy(chip, g, target):
            return remote(
                mine.at[chip, g], chain_in.at[chip, g], chain_send.at[chip, g],
                chain_recv.at[chip, g], at(target),
            )

        def last_copy(chip, g):
            return remote(
                mine.at[chip, g], right_in.at[g], chain_send.at[chip, g], last_recv.at[g],
                at(z - 1),
            )

        b = lax.axis_index("batch")

        def peer(k):
            return {"batch": b ^ k}

        def down_copy(k):
            return remote(
                grad_down_ref.at[pl.ds((b ^ k) * owned, owned)], down_ref_all.at[k],
                down_send.at[k], down_recv.at[k], peer(k),
            )

        def down_own():
            return pltpu.make_async_copy(
                grad_down_ref.at[pl.ds(b * owned, owned)], down_ref_all.at[0], down_sem
            )

        barrier = pltpu.get_barrier_semaphore()
        pl.semaphore_signal(barrier, inc=1, device_id=sibling, device_id_type=MESH)
        for k in range(1, batch_size):
            pl.semaphore_signal(barrier, inc=1, device_id=peer(k), device_id_type=MESH)

        @pl.when(has_left)
        def _():
            pl.semaphore_signal(barrier, inc=1, device_id=at(z - 1), device_id_type=MESH)

        @pl.when(has_right)
        def _():
            pl.semaphore_signal(barrier, inc=1, device_id=at(z + 1), device_id_type=MESH)

        own = pltpu.make_async_copy(x_ref, all_ref.at[z, c], own_sem)
        own.start()
        sum_ref[...] = jnp.zeros_like(sum_ref)
        up_acc[...] = jnp.zeros_like(up_acc)
        down_acc[...] = jnp.zeros_like(down_acc)
        pl.semaphore_wait(
            barrier, batch_size + has_left.astype(jnp.int32) + has_right.astype(jnp.int32)
        )
        own.wait()

        def pass_on(chip, g):
            @pl.when((chip <= z) & has_right)
            def _():
                row_copy(chip, g, 0).start()

            @pl.when((chip >= z) & has_left)
            def _():
                row_copy(chip, g, 1).start()

            row_copy(chip, g, 2).start()

        for g in range(cuts):
            pass_on(z, g)

        def compute(chip, g):
            cot_load = pltpu.make_async_copy(cot_ref.at[chip, :, g], cot_buf, cot_sem)
            cot_load.start()
            row_copy(chip, g, 2).wait_recv()
            x_load = pltpu.make_async_copy(all_ref.at[chip, :, g], x_buf, x_sem)
            x_load.start()
            cot_load.wait()
            grad_hidden = matmul_nt(cot_buf[...].reshape(2 * sub, width), down_ref[...])
            x_load.wait()
            pre_act = matmul(x_buf[...].reshape(2 * sub, width), up_ref[...]) + bias_ref[...]
            hidden, slope = gelu_pair(pre_act)
            hid_buf[...] = hidden.astype(BF16).reshape(2, sub, hid)
            hid_store = pltpu.make_async_copy(hid_buf, hid_ref.at[chip, :, g], hid_sem)
            hid_store.start()
            grad_pre = (grad_hidden * slope).astype(BF16)
            pre_buf[...] = grad_pre.reshape(2, sub, hid)
            pre_store = pltpu.make_async_copy(pre_buf, pre_ref.at[chip, :, g], pre_sem)
            pre_store.start()
            sum_ref[...] += jnp.sum(
                grad_pre.astype(F32).reshape(2 * sub // 8, 8, hid), axis=0
            )
            share = matmul_nt(grad_pre, up_ref[...]).astype(BF16).reshape(2, sub, width)

            @pl.when(c == 0)
            def _():
                mine[chip, g] = share[0]
                give[chip, g] = share[1]

            @pl.when(c == 1)
            def _():
                mine[chip, g] = share[1]
                give[chip, g] = share[0]

            pair_copy(chip, g).start()
            down_acc[...] += matmul_t(
                cot_buf[...].reshape(2 * sub, width), hid_buf[...].reshape(2 * sub, hid)
            ).reshape(tiles, TILE, hid)
            hid_store.wait()
            pre_store.wait()

        def nearest(i):
            edge = jnp.minimum(z, n - 1 - z)
            near = (i + 1) // 2
            inner = jnp.where(i % 2 == 1, z - near, z + near)
            far = i - edge
            outer = jnp.where(z < n - 1 - z, z + far, z - far)
            return jnp.where(i <= 2 * edge, inner, outer)

        def compute_rest(index):
            chip = nearest(index // cuts)
            g = index % cuts
            loads = [
                pltpu.make_async_copy(hid_ref.at[chip, :, g], hid_buf, hid_sem),
                pltpu.make_async_copy(all_ref.at[chip, :, g], x_buf, x_sem),
                pltpu.make_async_copy(pre_ref.at[chip, :, g], pre_buf, pre_sem),
            ]
            for load in loads:
                load.start()
            loads[0].wait()
            hidden = hid_buf[...].reshape(2 * sub, hid)
            stage[...] = matmul(hidden, down_ref[...]).astype(BF16).reshape(2, sub, width)
            mix_store = pltpu.make_async_copy(stage, mix_ref.at[chip, :, g], mix_sem)
            mix_store.start()
            loads[1].wait()
            loads[2].wait()
            up_acc[...] += matmul_t(
                x_buf[...].reshape(2 * sub, width), pre_buf[...].reshape(2 * sub, hid)
            ).reshape(tiles, TILE, hid)
            mix_store.wait()

        def add_up(chip, g, more):
            pair_copy(chip, g).wait_recv()
            total = mine[chip, g].astype(F32) + pair_in[chip, g].astype(F32)

            @pl.when(more)
            def _():
                chain_copy(chip, g, z).wait_recv()
                mine[chip, g] = (total + chain_in[chip, g].astype(F32)).astype(BF16)

            @pl.when(jnp.logical_not(more))
            def _():
                mine[chip, g] = total.astype(BF16)

        def step(t, carry):
            d = t // cuts
            g = t % cuts

            @pl.when((d > 0) & (z >= d))
            def _():
                row_copy(z - d, g, 0).wait_recv()
                pass_on(z - d, g)

            @pl.when((d > 0) & (z + d < n))
            def _():
                row_copy(z + d, g, 1).wait_recv()
                pass_on(z + d, g)

            def one_side(side, inner):
                chip = z + d * (2 * side - 1)

                @pl.when((chip >= 0) & (chip < n) & (d < n) & ((d > 0) | (side == 0)))
                def _():
                    compute(chip, g)

                return inner

            lax.fori_loop(0, 2, one_side, 0)

            @pl.when(t == (jnp.maximum(z, n - 1 - z) + 1) * cuts - 1)
            def _():
                def put_down(p, inner):
                    grad_down_ref[p] = down_acc[owner_ref[p]].astype(BF16)
                    return inner

                lax.fori_loop(0, tiles, put_down, 0)
                for k in range(1, batch_size):
                    down_copy(k).start()
                down_own().start()

            from_left = jnp.maximum(t - z, 0)
            chip_right = from_left // cuts
            g_right = from_left % cuts

            @pl.when((t >= z) & (chip_right > z) & (chip_right < n))
            def _():
                add_up(chip_right, g_right, has_left)
                chain_copy(chip_right, g_right, z + 1).start()

            from_right = jnp.maximum(t - (n - 1 - z), 0)
            chip_left = n - 1 - from_right // cuts
            g_left = from_right % cuts

            @pl.when((t >= n - 1 - z) & (chip_left < z) & (chip_left >= 0))
            def _():
                add_up(chip_left, g_left, has_right)

                @pl.when(chip_left == z - 1)
                def _():
                    last_copy(chip_left, g_left).start()

                @pl.when(chip_left < z - 1)
                def _():
                    chain_copy(chip_left, g_left, z - 1).start()

            events = (z >= d).astype(jnp.int32) + (z + d < n).astype(jnp.int32)
            events = jnp.where((d == 0) | (d >= n), 1, events)
            ready = (events < 2) & (carry < total_events)

            @pl.when(ready)
            def _():
                compute_rest(carry)

            return carry + ready.astype(jnp.int32)

        done = lax.fori_loop(0, n * cuts + n - 1, step, 0)

        def left_over(index, carry):
            @pl.when(index >= done)
            def _():
                compute_rest(index)

            return carry

        lax.fori_loop(0, total_events, left_over, 0)

        def put_tile(p, carry):
            grad_up_ref[p] = up_acc[owner_ref[p]].astype(BF16)
            return carry

        lax.fori_loop(0, tiles, put_tile, 0)

        for g in range(cuts):
            pair_copy(z, g).wait_recv()
            out_ref[g] = mine[z, g].astype(F32) + pair_in[z, g].astype(F32)

            @pl.when(has_left)
            def _():
                chain_copy(z, g, z).wait_recv()
                out_ref[g] += chain_in[z, g].astype(F32)

            @pl.when(has_right)
            def _():
                last_copy(z, g).wait_recv()
                out_ref[g] += right_in[g].astype(F32)

        def finish(chip, carry):
            for g in range(cuts):

                @pl.when((chip <= z) & has_right)
                def _():
                    row_copy(chip, g, 0).wait_send()

                @pl.when((chip >= z) & has_left)
                def _():
                    row_copy(chip, g, 1).wait_send()

                row_copy(chip, g, 2).wait_send()
                pair_copy(chip, g).wait_send()

                @pl.when(chip != z)
                def _():
                    chain_copy(chip, g, z).wait_send()

            return carry

        lax.fori_loop(0, n, finish, 0)
        for k in range(1, batch_size):
            down_copy(k).wait()
        down_own().wait()

    dma = pltpu.SemaphoreType.DMA
    vm = pltpu.VMEM
    each = dma((n, cuts))
    shares = vm((n, cuts, sub, width), BF16)
    outs = pl.pallas_call(
        kernel,
        out_shape=(
            jax.ShapeDtypeStruct(block + (width,), BF16),
            jax.ShapeDtypeStruct(block + (hid,), BF16),
            jax.ShapeDtypeStruct(block + (hid,), BF16),
            jax.ShapeDtypeStruct(block + (width,), BF16),
            jax.ShapeDtypeStruct((tiles, TILE, hid), BF16),
            jax.ShapeDtypeStruct((batch_size, owned, TILE, hid), BF16),
            jax.ShapeDtypeStruct((cuts, sub, width), F32),
            jax.ShapeDtypeStruct((8, hid), F32),
        ),
        in_specs=[pl.BlockSpec(memory_space=pltpu.SMEM), WHOLE, ANY, WHOLE, WHOLE, WHOLE],
        out_specs=(ANY, ANY, ANY, ANY, WHOLE, ANY, WHOLE, WHOLE),
        scratch_shapes=[
            vm((2, sub, width), BF16),
            vm((2, sub, width), BF16),
            vm((2, sub, hid), BF16),
            vm((2, sub, hid), BF16),
            shares, shares, shares, shares,
            vm((cuts, sub, width), BF16),
            vm((tiles, TILE, hid), F32),
            vm((tiles, TILE, hid), F32),
            vm((2, sub, width), BF16),
            vm((tiles, TILE, hid), BF16),
            dma, dma, dma, dma, dma, dma,
            each, each, each, each, each,
            each, each, each, each,
            dma((cuts,)),
            dma((batch_size,)), dma((batch_size,)), dma,
        ],
        compiler_params=pltpu.CompilerParams(
            collective_id=3, has_side_effects=True, vmem_limit_bytes=VMEM_LIMIT
        ),
        cost_estimate=pl.CostEstimate(
            flops=12 * n * 2 * tok * width * hid, bytes_accessed=300 * 1024 * 1024, transcendentals=0
        ),
        name="mixer_pass",
    )(
        owner,
        mixer_in.reshape(cuts, sub, width),
        cot_all.reshape(block + (width,)),
        w_up,
        w_down,
        bias_up.reshape(1, hid),
    )
    _, _, _, mix_part, grad_up, grad_down, grad_in, bias_sum = outs
    return (
        mix_part.reshape(2 * n * tok, width),
        grad_up.reshape(batch_size, owned * TILE, hid),
        grad_down.reshape(batch_size, owned * TILE, hid),
        grad_in.reshape(tok, width),
        jnp.sum(bias_sum, axis=0),
    )


def attention_forward(queries, key_rows, value_turned, mask, slabs):
    tok, width = queries.shape
    seq_len, head_size = key_rows.shape
    slab = width // slabs
    heads = slab // head_size
    scale = LOG2E / math.sqrt(head_size)

    def kernel(q_ref, k_ref, v_ref, mask_ref, o_ref, log_ref):
        for j in range(heads):
            spot = slice(j * head_size, (j + 1) * head_size)
            scores = matmul_nt(k_ref[...], q_ref[:, spot]) * scale + mask_ref[...]
            highest = jnp.max(scores, axis=0, keepdims=True)
            raised = jnp.exp2(scores - highest)
            total = jnp.sum(raised, axis=0, keepdims=True)
            out = matmul(v_ref[...], raised.astype(BF16)) / total
            o_ref[:, spot] = out.T.astype(BF16)
            log_ref[0, j : j + 1, :] = highest + jnp.log2(total)

    return pl.pallas_call(
        kernel,
        grid=(slabs,),
        out_shape=(
            jax.ShapeDtypeStruct((tok, width), BF16),
            jax.ShapeDtypeStruct((slabs, heads, tok), F32),
        ),
        in_specs=[
            pl.BlockSpec((tok, slab), lambda i: (0, i)),
            pl.BlockSpec((seq_len, head_size), lambda i: (0, 0)),
            pl.BlockSpec((head_size, seq_len), lambda i: (0, 0)),
            pl.BlockSpec((seq_len, tok), lambda i: (0, 0)),
        ],
        out_specs=(
            pl.BlockSpec((tok, slab), lambda i: (0, i)),
            pl.BlockSpec((1, heads, tok), lambda i: (i, 0, 0)),
        ),
        compiler_params=pltpu.CompilerParams(vmem_limit_bytes=VMEM_LIMIT),
        cost_estimate=pl.CostEstimate(
            flops=8 * tok * seq_len * width,
            bytes_accessed=4 * tok * width,
            transcendentals=tok * seq_len * slabs * heads,
        ),
        name="attention_forward",
    )(queries, key_rows, value_turned, mask)


def backward_pass(
    owner, grad_mixer, cotangent, tokens, normed_two, inverse_two, vectors, queries, attended,
    log_totals, key_rows, key_turned, value_rows, mask, w_query_all, w_out_all, w_kv, up_parts,
    grad_up, batch_size, head_count,
):
    tok, width = tokens.shape
    seq_len, head_size = key_rows.shape
    slab = width // head_count
    heads = slab // head_size
    n = head_count // 2
    tiles = width // TILE
    cols_out = width // batch_size
    owned = tiles // batch_size
    half_rows = slab // 2
    kv_cols = 2 * head_size
    kv_rows = width // head_count // batch_size
    ring = batch_size == 4
    scale = LOG2E / math.sqrt(head_size)
    plain_scale = 1.0 / math.sqrt(head_size)
    block = 512 if seq_len % 512 == 0 else seq_len

    def kernel(
        owner_ref, gm_ref, cot_ref, tok_ref, n2_ref, i2_ref, vec_ref, q_ref, att_ref, log_ref,
        k_ref, kt_ref, v_ref, mask_ref, wq_ref, wo_ref, wkv_ref, up_ref, gu_ref,
        tokens_out, query_out, out_out, kv_out, vec_out, up_out, gu_out,
        branch, wide_tiles, normed_owned, branch_owned, grad_in, wq_buf, wo_buf, dk, dv,
        give, mine, pair_in, land, hop, z_land,
        dkv, dkv_pair, dkv_here, dkv_land,
        kv_part, kv_pair, kv_sum, kv_land, kv_half, kv_zland,
        vec_part, vec_land, vec_sum, vec_bland, up_land,
        gm_sem, n2_sem, cot_sem, free_sem, wq_sem, wo_sem, pair_send, pair_recv, hop_send, hop_recv, land_send, land_recv,
        z_send, z_recv, dkv_s, dkv_r, dkz_s, dkz_r,
        s_pair, r_pair, s_kvb, r_kvb, s_kvz, r_kvz, s_kva, r_kva,
        s_vh, r_vh, s_vb, r_vb, s_va, r_va, s_up, r_up, gu_send, gu_recv, gu_sem,
    ):
        b = lax.axis_index("batch")
        h = lax.axis_index("head")
        z = h // 2
        c = h % 2
        sibling = {"head": h + 1 - 2 * c}

        def at_chip(r):
            return {"head": lax.rem(z + r, n) * 2 + c}

        def other(d):
            return {"head": lax.rem(h + d, head_count)}

        def peer(k):
            return {"batch": b ^ k}

        def remote(src, dst, send, recv, target):
            return pltpu.make_async_remote_copy(
                src_ref=src, dst_ref=dst, send_sem=send, recv_sem=recv,
                device_id=target, device_id_type=MESH,
            )

        greet([other(d) for d in range(1, head_count)] + [peer(k) for k in range(1, batch_size)])

        up_copies = [
            remote(up_ref, up_land.at[k], s_up.at[k], r_up.at[k], peer(k))
            for k in range(1, batch_size)
        ]
        for copy in up_copies:
            copy.start()

        gu_own = pltpu.make_async_copy(gu_ref.at[b], gu_out.at[0], gu_sem)
        gu_own.start()

        def gu_copies(p):
            part = pl.ds(p * TILE, TILE)
            return [
                remote(
                    gu_ref.at[b ^ k, part], gu_out.at[k, part], gu_send.at[k, p], gu_recv.at[k, p],
                    peer(k),
                )
                for k in range(1, batch_size)
            ]

        for copy in gu_copies(0):
            copy.start()

        def slab_at(s):
            chip = lax.rem(z + 1 + s // 2, n)
            return chip * 2 + jnp.where(s % 2 == 0, 1 - c, c)

        def weight_loads(s):
            i = slab_at(s)
            return (
                pltpu.make_async_copy(
                    wq_ref.at[:, lanes(i * slab, slab, slab)], wq_buf, wq_sem
                ),
                pltpu.make_async_copy(
                    wo_ref.at[lanes(i * slab, slab, slab), :], wo_buf, wo_sem
                ),
            )

        norm_loads = (
            pltpu.make_async_copy(gm_ref, tokens_out, gm_sem),
            pltpu.make_async_copy(n2_ref, grad_in, n2_sem),
            pltpu.make_async_copy(cot_ref, branch, cot_sem),
        )
        for load in norm_loads + weight_loads(0):
            load.start()

        def put_vector(row, value):
            for i in range(head_count):
                vec_part[i, row : row + 1, :] = value[:, i * slab : (i + 1) * slab]

        def column_sum(value):
            return jnp.sum(value, axis=0, keepdims=True)

        for load in norm_loads:
            load.wait()
        grad_mix = tokens_out[...]
        normed_two_rows = grad_in[...]
        grad_out_rows = branch[...].astype(F32)
        put_vector(5, column_sum(grad_out_rows))
        grad_resid = grad_out_rows + norm_back(
            grad_mix, normed_two_rows, i2_ref[:, :1], vec_ref[2:3, :]
        )
        put_vector(2, column_sum(grad_mix * normed_two_rows))
        put_vector(3, column_sum(grad_mix))
        tokens_out[...] = grad_resid
        grad_branch = grad_resid.astype(BF16)
        branch[...] = grad_branch

        put_vector(4, column_sum(grad_branch.astype(F32)))

        for p in range(tiles):
            wide_tiles[p] = branch[:, p * TILE : (p + 1) * TILE]

        for p in range(tiles):
            branch_owned[:, p * TILE : (p + 1) * TILE] = wide_tiles[owner_ref[p]]
        normed_one, inverse_one = norm_stats(tok_ref[...].astype(F32))
        normed_in = (normed_one * vec_ref[0:1, :] + vec_ref[1:2, :]).astype(BF16)
        for p in range(tiles):
            wide_tiles[p] = normed_in[:, p * TILE : (p + 1) * TILE]

        for p in range(tiles):
            normed_owned[:, p * TILE : (p + 1) * TILE] = wide_tiles[owner_ref[p]]
        dk[...] = jnp.zeros_like(dk)
        dv[...] = jnp.zeros_like(dv)
        grad_in[...] = jnp.zeros_like(grad_in)

        def pair_copy(q):
            return remote(
                give.at[q % 2], pair_in.at[q % 2], pair_send.at[q], pair_recv.at[q], sibling
            )

        halves = (pl.ds(0, half_rows), pl.ds(half_rows, half_rows))

        def hop_copy(q, k):
            part = halves[1 if k == 1 else 0]
            return remote(
                mine.at[q, b ^ 3, part], hop.at[q, k - 1], hop_send.at[q, k], hop_recv.at[q, k],
                peer(k),
            )

        def land_copy(q, k, which):
            if which is None:
                return remote(
                    mine.at[q, b ^ k], land.at[q, k - 1], land_send.at[q, k, 0],
                    land_recv.at[q, k, 0], peer(k),
                )
            part = halves[which]
            return remote(
                mine.at[q, b ^ k, part], land.at[q, k - 1, part], land_send.at[q, k, which],
                land_recv.at[q, k, which], peer(k),
            )

        def z_copy(q):
            return remote(
                mine.at[q, b], z_land.at[q], z_send.at[q], z_recv.at[q], at_chip(q % n + 1)
            )

        def pair_start(q, value):
            @pl.when(q >= 2)
            def _():
                pair_copy(q - 2).wait_send()
                pl.semaphore_wait(free_sem, 1)

            for k in range(batch_size):
                give[q % 2, k] = value[:, k * cols_out : (k + 1) * cols_out]
            pair_copy(q).start()

        def plane_start(q):
            pair_copy(q).wait_recv()
            mine[q] = (mine[q].astype(F32) + pair_in[q % 2].astype(F32)).astype(BF16)

            @pl.when(q < 2 * n - 2)
            def _():
                pl.semaphore_signal(free_sem, inc=1, device_id=sibling, device_id_type=MESH)

            if ring:
                hop_copy(q, 1).start()
                hop_copy(q, 2).start()
                land_copy(q, 1, 1).start()
                land_copy(q, 2, 0).start()
            else:
                for k in range(1, batch_size):
                    land_copy(q, k, None).start()

        def plane_hop(q):
            if not ring:
                return
            for k in (1, 2):
                hop_copy(q, 3 - k).wait_recv()
                which = 0 if k == 1 else 1
                part = halves[which]
                mine[q, b ^ k, part, :] = (
                    mine[q, b ^ k, part, :].astype(F32) + hop[q, 2 - k].astype(F32)
                ).astype(BF16)
                land_copy(q, k, which).start()

        def plane_end(q):
            total = mine[q, b].astype(F32)
            for k in range(1, 3 if ring else batch_size):
                for which in (0, 1) if ring else (None,):
                    land_copy(q, k, which).wait_recv()
                total += land[q, k - 1].astype(F32)
            mine[q, b] = total.astype(BF16)

            @pl.when(q % n < n - 1)
            def _():
                z_copy(q).start()

        def out_gradient(i):
            att = att_ref[:, lanes(i * slab, slab, slab)]
            return matmul(att.astype(F32).T.astype(BF16), branch_owned[...]).astype(BF16)

        def put_mine(q, value):
            for k in range(batch_size):
                mine[q, k] = value[:, k * cols_out : (k + 1) * cols_out]

        def out_pairs(j, carry):
            pair_start(j, out_gradient(slab_at(2 * j)))
            put_mine(j, out_gradient(slab_at(2 * j + 1)))

            @pl.when(j >= 1)
            def _():
                plane_start(j - 1)

            return carry

        lax.fori_loop(0, n, out_pairs, 0)
        plane_start(n - 1)

        def work(s, carry):
            j = s // 2
            i = slab_at(s)
            cols = lanes(i * slab, slab, slab)

            loads = weight_loads(s)
            loads[1].wait()
            grad_att = matmul_nt(branch[...], wo_buf[...]).astype(BF16)

            @pl.when(s + 1 < head_count)
            def _():
                weight_loads(s + 1)[1].start()

            queries_here = q_ref[:, cols]
            att_here = att_ref[:, cols]
            logs_here = log_ref[i]
            parts = []
            for e in range(heads):
                spot = slice(e * head_size, (e + 1) * head_size)
                query = queries_here[:, spot]
                grad = grad_att[:, spot]
                joint = grad.astype(F32) * att_here[:, spot].astype(F32)
                delta = jnp.sum(joint.T, axis=0, keepdims=True)
                logs = logs_here[e : e + 1, :]
                total = jnp.zeros((head_size, tok), F32)
                for start in range(0, seq_len, block):
                    part = slice(start, start + block)
                    scores = matmul_nt(k_ref[part, :], query) * scale
                    probs = jnp.exp2(scores + (mask_ref[part, :].astype(F32) - logs))
                    grad_probs = matmul_nt(v_ref[part, :], grad)
                    grad_scores = (probs * (grad_probs - delta)).astype(BF16)
                    dv[part, :] += matmul(probs.astype(BF16), grad)
                    dk[part, :] += matmul(grad_scores, query)
                    total += matmul(kt_ref[:, part], grad_scores)
                parts.append(total * plain_scale)
            turned = jnp.concatenate(parts, axis=0) if heads > 1 else parts[0]
            grad_q = turned.T.astype(BF16)
            vec_part[i, 6:7, :] = column_sum(grad_q.astype(F32))
            grad_query = matmul(turned.astype(BF16), normed_owned[...]).astype(BF16)

            @pl.when(s % 2 == 0)
            def _():
                pair_start(n + j, grad_query)

            @pl.when(s % 2 == 1)
            def _():
                put_mine(n + j, grad_query)

            loads[0].wait()
            grad_in[...] += matmul_nt(grad_q, wq_buf[...])

            @pl.when(s + 1 < head_count)
            def _():
                weight_loads(s + 1)[0].start()

            @pl.when(s < n)
            def _():
                plane_hop(s)

            @pl.when((s >= 2) & (s < n + 2))
            def _():
                plane_end(s - 2)

            @pl.when(s % 2 == 1)
            def _():
                plane_start(n + j)

                @pl.when(j >= 1)
                def _():
                    plane_hop(n + j - 1)

                @pl.when(j >= 2)
                def _():
                    plane_end(n + j - 2)

            return carry

        lax.fori_loop(0, head_count, work, 0)

        dkv[:, :, :, :head_size] = (dk[...] * plain_scale).astype(BF16).reshape(n, 2, tok, head_size)
        dkv[:, :, :, head_size:] = dv[...].astype(BF16).reshape(n, 2, tok, head_size)
        dkv_swap = remote(dkv.at[:, 1 - c], dkv_pair, dkv_s, dkv_r, sibling)
        dkv_swap.start()
        dkv_swap.wait_recv()
        for r in range(n):
            dkv_here[r] = (dkv[r, c].astype(F32) + dkv_pair[r].astype(F32)).astype(BF16)
        dkv_copies = [
            remote(
                dkv_here.at[lax.rem(z + r, n)], dkv_land.at[r], dkz_s.at[r], dkz_r.at[r],
                at_chip(r),
            )
            for r in range(1, n)
        ]
        for copy in dkv_copies:
            copy.start()
        normed_one, inverse_one = norm_stats(tok_ref[...].astype(F32))
        normed_in = (normed_one * vec_ref[0:1, :] + vec_ref[1:2, :]).astype(BF16)
        plane_hop(2 * n - 1)
        for p in range(1, owned):
            for copy in gu_copies(p):
                copy.start()
        grad_kv = dkv_here[z].astype(F32)
        for copy in dkv_copies:
            copy.wait_recv()
        for r in range(1, n):
            grad_kv += dkv_land[r].astype(F32)
        grad_kv = grad_kv.astype(BF16)

        kv_part[...] = (
            matmul_t(normed_in, grad_kv)
            .astype(BF16)
            .reshape(n, 2, batch_size, kv_rows, kv_cols)
        )
        pair_kv = remote(kv_part.at[:, 1 - c], kv_pair, s_pair, r_pair, sibling)
        pair_kv.start()

        grad_normed = grad_in[...] + matmul_nt(grad_kv, wkv_ref[...])
        pair_kv.wait_recv()
        for r in range(n):
            kv_sum[r] = (kv_part[r, c].astype(F32) + kv_pair[r].astype(F32)).astype(BF16)
        kv_copies = [
            remote(kv_sum.at[:, b ^ k], kv_land.at[k], s_kvb.at[k], r_kvb.at[k], peer(k))
            for k in range(1, batch_size)
        ]
        for copy in kv_copies:
            copy.start()
        put_vector(0, column_sum(grad_normed * normed_one))
        put_vector(1, column_sum(grad_normed))
        for i in range(head_count):
            vec_part[i, 7:8, :] = jnp.zeros((1, slab), F32)
        vec_part[0, 7:8, :head_size] = column_sum(grad_kv[:, head_size:].astype(F32))
        vec_copies = [
            remote(
                vec_part.at[lax.rem(h + d, head_count)], vec_land.at[d], s_vh.at[d], r_vh.at[d],
                other(d),
            )
            for d in range(1, head_count)
        ]
        for copy in vec_copies:
            copy.start()
        tokens_out[...] += norm_back(grad_normed, normed_one, inverse_one, vec_ref[0:1, :])
        total = vec_part[h]
        for copy in vec_copies:
            copy.wait_recv()
        for d in range(1, head_count):
            total += vec_land[d]
        vec_sum[...] = total
        vec_bcopies = [
            remote(vec_sum, vec_bland.at[k], s_vb.at[k], r_vb.at[k], peer(k))
            for k in range(1, batch_size)
        ]
        for copy in vec_bcopies:
            copy.start()
        up_total = up_ref[...]
        for copy in up_copies:
            copy.wait_recv()
        for k in range(1, batch_size):
            up_total += up_land[k]
        up_out[...] = up_total
        for copy in kv_copies:
            copy.wait_recv()
        kv_total = kv_sum[:, b].astype(F32)
        for k in range(1, batch_size):
            kv_total += kv_land[k].astype(F32)
        kv_half[...] = kv_total.astype(BF16)
        kv_zcopies = [
            remote(
                kv_half.at[lax.rem(z + r, n)], kv_zland.at[r], s_kvz.at[r], r_kvz.at[r], at_chip(r)
            )
            for r in range(1, n)
        ]
        for copy in kv_zcopies:
            copy.start()
        for copy in vec_bcopies:
            copy.wait_recv()
        total = vec_sum[...]
        for k in range(1, batch_size):
            total += vec_bland[k]
        vec_out[h] = total
        vec_acopies = [
            remote(vec_out.at[h], vec_out.at[h], s_va.at[d], r_va.at[d], other(d))
            for d in range(1, head_count)
        ]
        for copy in vec_acopies:
            copy.start()
        for copy in kv_zcopies:
            copy.wait_recv()
        kv_mine = kv_half[z].astype(F32)
        for r in range(1, n):
            kv_mine += kv_zland[r].astype(F32)
        kv_out[b] = kv_mine
        kv_acopies = [
            remote(kv_out.at[b], kv_out.at[b], s_kva.at[k], r_kva.at[k], peer(k))
            for k in range(1, batch_size)
        ]
        for copy in kv_acopies:
            copy.start()

        plane_end(2 * n - 2)
        plane_end(2 * n - 1)
        for first, target in ((0, out_out), (n, query_out)):
            total = mine[first + n - 1, b].astype(F32)
            for r in range(n - 1):
                z_copy(first + r).wait_recv()
                total += z_land[first + r].astype(F32)
            target[0] = total.astype(BF16)
        for copy in vec_acopies + kv_acopies:
            copy.wait_recv()

        for copy in up_copies + [dkv_swap, pair_kv] + dkv_copies + vec_copies + kv_copies:
            copy.wait_send()
        for copy in vec_bcopies + kv_zcopies + vec_acopies + kv_acopies:
            copy.wait_send()
        pair_copy(2 * n - 2).wait_send()
        pair_copy(2 * n - 1).wait_send()
        for p in range(owned):
            for copy in gu_copies(p):
                copy.wait()
        gu_own.wait()

        def finish(q, carry):
            @pl.when(q % n < n - 1)
            def _():
                z_copy(q).wait_send()

            if ring:
                for k in (1, 2):
                    hop_copy(q, k).wait_send()
                    for which in (0, 1):
                        land_copy(q, k, which).wait_send()
            else:
                for k in range(1, batch_size):
                    land_copy(q, k, None).wait_send()
            return carry

        lax.fori_loop(0, 2 * n, finish, 0)

    dma = pltpu.SemaphoreType.DMA
    vm = pltpu.VMEM
    nb, nh = batch_size, head_count
    lands = 2 if ring else nb - 1
    shared = (nb, slab, cols_out)
    return pl.pallas_call(
        kernel,
        out_shape=(
            jax.ShapeDtypeStruct((tok, width), F32),
            jax.ShapeDtypeStruct((1, slab, cols_out), BF16),
            jax.ShapeDtypeStruct((1, slab, cols_out), BF16),
            jax.ShapeDtypeStruct((nb, kv_rows, kv_cols), F32),
            jax.ShapeDtypeStruct((nh, 8, slab), F32),
            jax.ShapeDtypeStruct(up_parts.shape, F32),
            jax.ShapeDtypeStruct(grad_up.shape, grad_up.dtype),
        ),
        in_specs=[pl.BlockSpec(memory_space=pltpu.SMEM), ANY, ANY, WHOLE, ANY]
        + [WHOLE] * 9
        + [ANY, ANY, WHOLE, WHOLE, ANY],
        out_specs=(WHOLE,) * 6 + (ANY,),
        scratch_shapes=[
            vm((tok, width), BF16),
            vm((tiles, tok, TILE), BF16),
            vm((tok, width), BF16),
            vm((tok, width), BF16),
            vm((tok, width), F32),
            vm((width, slab), BF16),
            vm((slab, width), BF16),
            vm((seq_len, head_size), F32),
            vm((seq_len, head_size), F32),
            vm((2,) + shared, BF16),
            vm((2 * n,) + shared, BF16),
            vm((2,) + shared, BF16),
            vm((2 * n, lands, slab, cols_out), BF16),
            vm((2 * n, 2, half_rows, cols_out) if ring else (1, 1, 16, TILE), BF16),
            vm((2 * n, slab, cols_out), BF16),
            vm((n, 2, tok, kv_cols), BF16),
            vm((n, tok, kv_cols), BF16),
            vm((n, tok, kv_cols), BF16),
            vm((n, tok, kv_cols), BF16),
            vm((n, 2, nb, kv_rows, kv_cols), BF16),
            vm((n, nb, kv_rows, kv_cols), BF16),
            vm((n, nb, kv_rows, kv_cols), BF16),
            vm((nb, n, kv_rows, kv_cols), BF16),
            vm((n, kv_rows, kv_cols), BF16),
            vm((n, kv_rows, kv_cols), BF16),
            vm((nh, 8, slab), F32),
            vm((nh, 8, slab), F32),
            vm((8, slab), F32),
            vm((nb, 8, slab), F32),
            vm((nb,) + up_parts.shape, F32),
            dma, dma, dma, pltpu.SemaphoreType.REGULAR, dma, dma,
            dma((2 * n,)), dma((2 * n,)), dma((2 * n, 3)), dma((2 * n, 3)),
            dma((2 * n, nb, 2)), dma((2 * n, nb, 2)), dma((2 * n,)), dma((2 * n,)), dma, dma, dma((n,)), dma((n,)),
            dma, dma, dma((nb,)), dma((nb,)), dma((n,)), dma((n,)), dma((nb,)), dma((nb,)),
            dma((nh,)), dma((nh,)), dma((nb,)), dma((nb,)), dma((nh,)), dma((nh,)),
            dma((nb,)), dma((nb,)), dma((nb, owned)), dma((nb, owned)), dma,
        ],
        compiler_params=pltpu.CompilerParams(
            collective_id=4, has_side_effects=True, vmem_limit_bytes=VMEM_LIMIT + 2 * 1024 * 1024
        ),
        cost_estimate=pl.CostEstimate(
            flops=20 * tok * seq_len * width + 8 * tok * width * width,
            bytes_accessed=200 * 1024 * 1024,
            transcendentals=tok * seq_len * width // head_size,
        ),
        name="backward_pass",
    )(
        owner, grad_mixer, cotangent, tokens, normed_two, inverse_two, vectors, queries, attended,
        log_totals, key_rows, key_turned, value_rows, mask, w_query_all, w_out_all, w_kv, up_parts,
        grad_up,
    )


def split_high(value):
    high = value.astype(BF16)
    return high, (value - high.astype(F32)).astype(BF16)


def matmul_three(first_op, second_op):
    first_high, first_low = split_high(first_op)
    second_high, second_low = split_high(second_op)
    return (
        matmul(first_high, second_high)
        + matmul(first_high, second_low)
        + matmul(first_low, second_high)
    )


def shampoo(
    first, second, first_weight, second_weight, owned, left, right, root_left, root_right, wide_rows
):
    _, owned_count, columns, _, _ = left.shape

    def kernel(ids_ref, *refs):
        del ids_ref
        one, two, w_one, w_two, l_ref, r_ref, p_ref, q_ref, g_out, l_out, r_out, w_out = refs

        def update(turned):
            for t in range(columns):
                spot = slice(t * TILE, (t + 1) * TILE)
                shares = two if turned else one
                part = (slice(None), spot) if wide_rows else (spot, slice(None))
                grad = shares[(0,) + part].astype(F32)
                for i in range(1, shares.shape[0]):
                    grad += shares[(i,) + part].astype(F32)
                if turned == wide_rows:
                    grad = grad.T
                if turned:
                    weight = w_two[spot, :].astype(F32)
                else:
                    weight = w_one[:, spot].astype(F32)
                high = grad.astype(BF16)
                g_out[0, 0, t] = grad
                l_out[0, 0, t] = DECAY_RATE * l_ref[0, 0, t] + (1.0 - DECAY_RATE) * matmul_nt(
                    high, high
                )
                r_out[0, 0, t] = DECAY_RATE * r_ref[0, 0, t] + (1.0 - DECAY_RATE) * matmul_t(
                    high, high
                )
                stepped = matmul_three(p_ref[0, 0, t], grad)
                stepped = matmul_three(stepped, q_ref[0, 0, t])
                w_out[0, 0, t] = weight - MATRIX_RATE * stepped

        @pl.when(pl.program_id(0) == 0)
        def _():
            update(False)

        @pl.when(pl.program_id(0) == 1)
        def _():
            update(True)

    last = owned_count - 1
    def share(array, place):
        if wide_rows:
            return pl.BlockSpec(
                (array.shape[0], TILE, columns * TILE), lambda m, p, ids: (0, place(m, p), 0)
            )
        return pl.BlockSpec(
            (array.shape[0], columns * TILE, TILE), lambda m, p, ids: (0, 0, place(m, p))
        )

    share_one = share(first, lambda m, p: jnp.where(m == 0, p, last))
    share_two = share(second, lambda m, p: jnp.where(m == 1, p, 0))
    weight_one = pl.BlockSpec(
        (TILE, columns * TILE), lambda m, p, ids: (ids[jnp.where(m == 0, p, last)], 0)
    )
    weight_two = pl.BlockSpec(
        (columns * TILE, TILE), lambda m, p, ids: (0, ids[jnp.where(m == 1, p, 0)])
    )
    stat = pl.BlockSpec((1, 1, columns, TILE, TILE), lambda m, p, ids: (m, p, 0, 0, 0))
    shape = jax.ShapeDtypeStruct(left.shape, F32)
    return pl.pallas_call(
        kernel,
        grid_spec=pltpu.PrefetchScalarGridSpec(
            num_scalar_prefetch=1,
            grid=(2, owned_count),
            in_specs=[share_one, share_two, weight_one, weight_two] + [stat] * 4,
            out_specs=[stat] * 4,
        ),
        out_shape=[shape] * 4,
        compiler_params=pltpu.CompilerParams(vmem_limit_bytes=VMEM_LIMIT),
        cost_estimate=pl.CostEstimate(
            flops=left.size * TILE * 16, bytes_accessed=left.size * 40, transcendentals=0
        ),
        name="shampoo",
    )(owned, first, second, first_weight, second_weight, left, right, root_left, root_right)


def shampoo_update(grad_tiles, left_old, right_old, root_left, root_right, weight_tiles):
    outer_left = jnp.einsum("...ij,...kj->...ik", grad_tiles, grad_tiles, precision=PRECISE)
    outer_right = jnp.einsum("...ji,...jk->...ik", grad_tiles, grad_tiles, precision=PRECISE)
    left_new = DECAY_RATE * left_old + (1.0 - DECAY_RATE) * outer_left
    right_new = DECAY_RATE * right_old + (1.0 - DECAY_RATE) * outer_right
    stepped = jnp.einsum("...ij,...jk->...ik", root_left, grad_tiles, precision=PRECISE)
    stepped = jnp.einsum("...ij,...jk->...ik", stepped, root_right, precision=PRECISE)
    return (grad_tiles, left_new, right_new, weight_tiles - MATRIX_RATE * stepped)


def diagonal_update(gradient, second, current):
    second_new = DECAY_RATE * second + (1.0 - DECAY_RATE) * gradient * gradient
    return (
        gradient,
        second_new,
        current - VECTOR_RATE * gradient / (jnp.sqrt(second_new) + SAFE_ADD),
    )


def gelu_pair(u):
    root = math.sqrt(2.0 / math.pi)
    square = u * u
    turn = jnp.tanh(root * u * (1.0 + 0.044715 * square))
    half = 0.5 * (1.0 + turn)
    slope = half + 0.5 * u * (1.0 - turn * turn) * root * (1.0 + 3.0 * 0.044715 * square)
    return u * half, slope


def body(
    tokens,
    cotangent,
    doc_starts,
    owner,
    vectors,
    bias_query,
    bias_value,
    bias_up,
    w_query,
    w_key,
    w_value,
    w_out,
    w_up,
    w_down,
    attn_left,
    attn_right,
    attn_root_left,
    attn_root_right,
    mixer_left,
    mixer_right,
    mixer_root_left,
    mixer_root_right,
    kv_left,
    kv_right,
    kv_root_left,
    kv_root_right,
    vector_second,
    query_second,
    value_second,
    up_second,
):
    batch_size = lax.axis_size("batch")
    head_count = lax.axis_size("head")
    batch_index = lax.axis_index("batch")
    head_index = lax.axis_index("head")
    tok_dev, width = tokens.shape
    seq_len = tok_dev * head_count
    row_start = head_index * tok_dev
    head_size = w_key.shape[1]
    slab = w_query.shape[1]
    gain_one = vectors[0]
    shift_one = vectors[1]
    bias_down = vectors[5]

    positions = jnp.arange(seq_len, dtype=jnp.int32)
    documents = jnp.sum((doc_starts[0][None, :] <= positions[:, None]).astype(jnp.int32), axis=1)
    row_ids = row_start + jnp.arange(tok_dev, dtype=jnp.int32)
    row_docs = lax.dynamic_slice_in_dim(documents, row_start, tok_dev, 0)
    allowed = (documents[:, None] == row_docs[None, :]) & (positions[:, None] <= row_ids[None, :])
    mask = jnp.where(allowed, 0.0, MASKED).astype(F32)

    rows_own = tokens.astype(F32)
    normed_one, inverse_one = norm_stats(rows_own)
    normed_in = (normed_one * gain_one + shift_one).astype(BF16)
    w_kv = jnp.concatenate([w_key, w_value], axis=1)
    kv_bias = jnp.concatenate([jnp.zeros_like(bias_value), bias_value])
    kv_own = (matmul(normed_in, w_kv) + kv_bias).astype(BF16)
    kv_all = lax.all_gather(kv_own, "head", axis=0, tiled=True)
    key_rows = kv_all[:, :head_size]
    value_rows = kv_all[:, head_size:]

    w_query_all, w_out_part, bias_all = gather_weights(
        w_query, w_out, bias_query.reshape(1, slab), batch_size, head_count
    )
    w_out_part, cotangent_later = lax.optimization_barrier((w_out_part, cotangent))
    w_out_all = gather_rest(w_out_part, batch_size, head_count)
    cot_all = lax.all_gather(cotangent_later, "head", axis=0, tiled=True)

    queries = (matmul(normed_in, w_query_all) + bias_all.reshape(1, width)).astype(BF16)
    attended, log_totals = attention_forward(queries, key_rows, value_rows.T, mask, head_count)
    resid, mixer_in, normed_two, inverse_wide = project_out(
        attended, w_out_all, tokens, vectors
    )

    mix_part, grad_up, down_shares, grad_mixer_in, grad_up_bias = mixer_pass(
        mixer_in, cot_all, w_up, w_down, bias_up, owner, batch_size, head_count, 2
    )
    mix_one = lax.psum_scatter(mix_part, "head", scatter_dimension=0, tiled=True)

    kv_rows = width // head_count // batch_size
    grad_tokens, query_share, out_share, kv_total, vector_wide, up_bias_total, up_shares = backward_pass(
        owner,
        grad_mixer_in,
        cotangent,
        tokens,
        normed_two,
        inverse_wide,
        vectors,
        queries,
        attended,
        log_totals,
        key_rows,
        key_rows.T,
        value_rows,
        mask.astype(BF16),
        w_query_all,
        w_out_all,
        w_kv,
        grad_up_bias.reshape(8, -1),
        grad_up,
        batch_size,
        head_count,
    )
    kv_total = kv_total.reshape(batch_size * kv_rows, 2 * head_size)
    up_bias_total = up_bias_total.reshape(-1)
    vector_all = vector_wide.transpose(1, 0, 2).reshape(8, width)
    vector_total = vector_all[:6]
    query_bias_total = lax.dynamic_slice_in_dim(vector_all[6], head_index * slab, slab, 0)
    value_bias_total = vector_all[7, :head_size]

    owned_count = attn_left.shape[1]
    owned = lax.dynamic_slice_in_dim(owner, batch_index * owned_count, owned_count, 0)
    mixer_out = shampoo(
        up_shares,
        down_shares,
        w_up,
        w_down,
        owned,
        mixer_left,
        mixer_right,
        mixer_root_left,
        mixer_root_right,
        True,
    )
    attn_out = shampoo(
        query_share,
        out_share,
        w_query,
        w_out,
        owned,
        attn_left,
        attn_right,
        attn_root_left,
        attn_root_right,
        False,
    )
    kv_count = width // head_count

    def kv_tiles(matrix):
        return matrix.reshape(kv_count // TILE, TILE, head_size // TILE, TILE).transpose(0, 2, 1, 3)

    kv_slab = lax.dynamic_slice_in_dim(w_kv, head_index * kv_count, kv_count, 0).astype(F32)
    kv_out = shampoo_update(
        jnp.stack([kv_tiles(kv_total[:, :head_size]), kv_tiles(kv_total[:, head_size:])]),
        kv_left,
        kv_right,
        kv_root_left,
        kv_root_right,
        jnp.stack([kv_tiles(kv_slab[:, :head_size]), kv_tiles(kv_slab[:, head_size:])]),
    )
    _, mix_one = lax.optimization_barrier((kv_total, mix_one))
    output = resid + mix_one.astype(F32) + bias_down
    vec_out = diagonal_update(vector_total, vector_second, vectors)
    query_out = diagonal_update(query_bias_total, query_second, bias_query)
    value_out = diagonal_update(value_bias_total, value_second, bias_value)
    up_out = diagonal_update(up_bias_total, up_second, bias_up)
    return (
        output,
        grad_tokens,
        vec_out[0],
        vec_out[1][2:],
        vec_out[1][:2],
        vec_out[2],
        query_out[0],
        query_out[1],
        query_out[2],
        value_out[0],
        value_out[1],
        value_out[2],
        up_out[0],
        up_out[1],
        up_out[2],
        attn_out[0],
        attn_out[1],
        attn_out[2],
        attn_out[3],
        mixer_out[0],
        mixer_out[1],
        mixer_out[2],
        mixer_out[3],
        kv_out[0],
        kv_out[1],
        kv_out[2],
        kv_out[3],
    )


def solution(mesh):
    rows = P(("batch", "head"), None)
    whole = P()
    head = P("head")
    tiles = P(None, "batch", "head", None, None)
    kv_tiles = P(None, "head", None, None, None)
    in_specs = (
        rows,
        rows,
        P("batch", None),
        whole,
        whole,
        head,
        whole,
        head,
        P(None, "head"),
        whole,
        whole,
        P("head", None),
        P(None, "head"),
        P("head", None),
        *([tiles] * 8),
        *([kv_tiles] * 4),
        whole,
        head,
        whole,
        head,
    )
    out_specs = (
        rows,
        rows,
        *([whole] * 4),
        *([head] * 3),
        *([whole] * 3),
        *([head] * 3),
        *([tiles] * 8),
        *([kv_tiles] * 4),
    )
    return jax.shard_map(body, mesh=mesh, in_specs=in_specs, out_specs=out_specs, check_vma=False)
```

```python
from functools import partial
import math

import jax
import jax.numpy as jnp
from jax import lax
from jax.experimental import pallas as pl
from jax.experimental.pallas import tpu as pltpu
from jax.sharding import PartitionSpec as P

EPSILON = 1e-05
DECAY_RATE = 0.5
MATRIX_RATE = 0.01
VECTOR_RATE = 0.1
SAFE_ADD = 1e-08
PRECISE = lax.Precision.HIGHEST
LOG2E = math.log2(math.e)
MASKED = -1e30
TILE = 128
MESH = pl.DeviceIdType.MESH
BF16 = jnp.bfloat16
F32 = jnp.float32
VMEM_LIMIT = 60 * 1024 * 1024
ANY = pl.BlockSpec(memory_space=pl.ANY)
WHOLE = pl.BlockSpec(memory_space=pltpu.VMEM)


def matmul(first_op, second_op):
    return jnp.dot(first_op, second_op, preferred_element_type=F32)


def matmul_t(first_op, second_op):
    return lax.dot_general(
        first_op, second_op, (((0,), (0,)), ((), ())), preferred_element_type=F32
    )


def matmul_nt(first_op, second_op):
    return lax.dot_general(
        first_op, second_op, (((1,), (1,)), ((), ())), preferred_element_type=F32
    )


def norm_stats(rows_in):
    mean_row = jnp.mean(rows_in, axis=-1, keepdims=True)
    centered = rows_in - mean_row
    variance = jnp.mean(centered * centered, axis=-1, keepdims=True)
    inverse = lax.rsqrt(variance + EPSILON)
    return (centered * inverse, inverse)


def norm_back(grad_out, normed, inverse, gain):
    scaled = grad_out * gain
    mean_one = jnp.mean(scaled, axis=-1, keepdims=True)
    mean_two = jnp.mean(scaled * normed, axis=-1, keepdims=True)
    return inverse * (scaled - mean_one - normed * mean_two)


def lanes(start, size, unit):
    return pl.ds(pl.multiple_of(start, unit), size)


def greet(targets):
    barrier = pltpu.get_barrier_semaphore()
    for target in targets:
        pl.semaphore_signal(barrier, inc=1, device_id=target, device_id_type=MESH)
    pl.semaphore_wait(barrier, len(targets))


def gather_tools(batch_size, head_count):
    chips = head_count // 2
    b = lax.axis_index("batch")
    h = lax.axis_index("head")
    z = h // 2
    c = h % 2

    def at(chip):
        return {"head": chip * 2 + c}

    def peer(k):
        return {"batch": b ^ k}

    def remote(src, dst, send, recv, target):
        return pltpu.make_async_remote_copy(
            src_ref=src,
            dst_ref=dst,
            send_sem=send,
            recv_sem=recv,
            device_id=target,
            device_id_type=MESH,
        )

    others = [lax.rem(z + i, chips) for i in range(1, chips)]
    return b, h, z, c, {"head": h + 1 - 2 * c}, at, peer, remote, others


def plane_exchange(place, tools, sems, batch_size):
    b, _, _, _, sibling, _, peer, remote, others = tools
    xs, xr, fs, fr, cs, cr = sems
    ring = batch_size == 4
    direct = (1, 2) if ring else tuple(range(1, batch_size))

    def hop(k, chip):
        spot = place(b, chip)
        return remote(spot, spot, xs.at[k, chip], xr.at[k, chip], peer(k))

    def half(k, chip):
        spot = place(b ^ k, chip, k - 1)
        return remote(spot, spot, fs.at[k, chip], fr.at[k, chip], peer(3 - k))

    def side(k, chip):
        spot = place(b ^ k, chip)
        return remote(spot, spot, cs.at[k, chip], cr.at[k, chip], sibling)

    def start(chip):
        for k in direct:
            hop(k, chip).start()
        side(0, chip).start()

    def turn():
        for chip in others:
            for k in direct:
                hop(k, chip).wait_recv()
                if ring:
                    half(k, chip).start()
                side(k, chip).start()

    def close():
        if ring:
            for chip in others:
                for k in direct:
                    half(k, chip).wait_recv()
                side(3, chip).start()

    def finish():
        for chip in others:
            for k in range(batch_size):
                side(k, chip).wait()
            for k in direct:
                hop(k, chip).wait_send()
                if ring:
                    half(k, chip).wait_send()

    return start, turn, close, finish


def place_rows(w_all, rows, core, batch_size):
    def place(quarter, chip, half=None):
        part = rows // batch_size
        if half is not None:
            part = part // 2
            quarter = quarter * 2 + half
        return w_all.at[lanes((chip * 2 + core) * rows + quarter * part, part, part), :]

    return place


def gather_weights(w_query, w_out, bias_local, batch_size, head_count):
    rows, cols = w_query.shape
    chips = head_count // 2

    def kernel(
        q_ref, w_ref, bias_ref, q_all, w_all, bias_all, loc, right, left, line, ys, yr, sides_s,
        sides_r, xs, xr, fs, fr, cs, cr, bs, br,
    ):
        tools = gather_tools(batch_size, head_count)
        b, h, z, c, sibling, at, peer, remote, others = tools
        has_left = z > 0
        has_right = z < chips - 1

        def other(d):
            return {"head": lax.rem(h + d, head_count)}

        def place_query(quarter, chip, half=None):
            part = rows // batch_size
            if half is not None:
                part = part // 2
                quarter = quarter * 2 + half
            head = chip * 2 + c
            return q_all.at[lanes(quarter * part, part, part), lanes(head * cols, cols, cols)]

        places = (place_query, place_rows(w_all, cols, c, batch_size))
        greet([other(d) for d in range(1, head_count)] + [peer(k) for k in range(1, batch_size)])
        own = (q_all.at[:, lanes(h * cols, cols, cols)], w_all.at[lanes(h * cols, cols, cols), :])
        q_part, w_part = rows // batch_size, cols // batch_size
        mine = (
            q_ref.at[lanes(b * q_part, q_part, q_part), :],
            w_ref.at[lanes(b * w_part, w_part, w_part), :],
        )

        def z_copy(m, chip, to_right, src=None):
            spot = places[m](b, chip)
            src = spot if src is None else src
            if to_right:
                return remote(src, spot, right.at[m, chip], line.at[m, chip], at(z + 1))
            return remote(src, spot, left.at[m, chip], line.at[m, chip], at(z - 1))

        def z_first(m):
            @pl.when(has_right)
            def _():
                z_copy(m, z, True, mine[m]).start()

            @pl.when(has_left)
            def _():
                z_copy(m, z, False, mine[m]).start()

        def z_steps(m, d, then):
            @pl.when(z >= d)
            def _():
                z_copy(m, z - d, True).wait_recv()

                @pl.when(has_right)
                def _():
                    z_copy(m, z - d, True).start()

                then(z - d)

            @pl.when(z + d < chips)
            def _():
                z_copy(m, z + d, False).wait_recv()

                @pl.when(has_left)
                def _():
                    z_copy(m, z + d, False).start()

                then(z + d)

        z_first(0)
        locals_ = [
            pltpu.make_async_copy(src, own[m], loc.at[m]) for m, src in enumerate((q_ref, w_ref))
        ]
        slices = [
            remote(src, own[m], ys.at[m], yr.at[m], sibling) for m, src in enumerate((q_ref, w_ref))
        ]
        biases = [
            remote(bias_ref, bias_all.at[h], bs.at[d], br.at[d], other(d))
            for d in range(1, head_count)
        ]
        bias_own = pltpu.make_async_copy(bias_ref, bias_all.at[h], bs.at[0])
        for copy in locals_ + slices + biases + [bias_own]:
            copy.start()

        start, turn, close, finish = plane_exchange(
            place_query, tools, (xs, xr, fs, fr, cs, cr), batch_size
        )

        def side(chip):
            spot = places[1](b, chip)
            return remote(spot, spot, sides_s.at[chip], sides_r.at[chip], sibling)

        for d in range(1, chips):
            z_steps(0, d, start)
            if d == 1:
                z_first(1)
        turn()
        for d in range(1, chips):
            z_steps(1, d, lambda chip: side(chip).start())
        close()
        finish()
        for chip in others:
            side(chip).wait()
        for m in range(2):

            @pl.when(has_right)
            def _():
                z_copy(m, z, True, mine[m]).wait_send()

            @pl.when(has_left)
            def _():
                z_copy(m, z, False, mine[m]).wait_send()

            for d in range(1, chips):

                @pl.when((z >= d) & has_right)
                def _():
                    z_copy(m, z - d, True).wait_send()

                @pl.when((z + d < chips) & has_left)
                def _():
                    z_copy(m, z + d, False).wait_send()

        for copy in locals_ + slices + biases + [bias_own]:
            copy.wait()

    dma = pltpu.SemaphoreType.DMA
    hop = dma((batch_size, chips))
    two = dma((2, chips))
    return pl.pallas_call(
        kernel,
        out_shape=(
            jax.ShapeDtypeStruct((rows, cols * head_count), w_query.dtype),
            jax.ShapeDtypeStruct((cols * head_count, w_out.shape[1]), w_out.dtype),
            jax.ShapeDtypeStruct((head_count, 1, cols), F32),
        ),
        in_specs=[WHOLE] * 3,
        out_specs=(ANY,) * 3,
        scratch_shapes=[
            dma((2,)), two, two, two, dma((2,)), dma((2,)), dma((chips,)), dma((chips,)),
            hop, hop, hop, hop, hop, hop, dma((head_count,)), dma((head_count,)),
        ],
        compiler_params=pltpu.CompilerParams(collective_id=0, has_side_effects=True),
        cost_estimate=pl.CostEstimate(
            flops=0, bytes_accessed=120 * 1024 * 1024, transcendentals=0
        ),
        name="gather_weights",
    )(w_query, w_out, bias_local)


def gather_rest(w_all, kv_own, batch_size, head_count):
    chips = head_count // 2
    rows = w_all.shape[0] // head_count
    tok, kv_cols = kv_own.shape

    def kernel(
        in_ref, kv_ref, w_ref, kv_all, xs, xr, fs, fr, cs, cr, own_sem, zs, zr, ss, sr
    ):
        del in_ref
        tools = gather_tools(batch_size, head_count)
        _, h, z, c, sibling, at, peer, remote, others = tools
        greet([sibling] + [at(chip) for chip in others] + [peer(k) for k in range(1, batch_size)])

        def place(chip):
            return kv_all.at[lanes((chip * 2 + c) * tok, tok, tok), :]

        own = pltpu.make_async_copy(kv_ref, place(z), own_sem)
        own.start()

        def away(i):
            return remote(kv_ref, place(z), zs.at[i], zr.at[i], at(others[i]))

        def side(chip):
            src = kv_ref if chip is z else place(chip)
            return remote(src, place(chip), ss.at[chip], sr.at[chip], sibling)

        for i in range(chips - 1):
            away(i).start()
        side(z).start()
        start, turn, close, finish = plane_exchange(
            place_rows(w_ref, rows, c, batch_size), tools, (xs, xr, fs, fr, cs, cr), batch_size
        )
        for chip in others:
            start(chip)
        turn()
        for i in range(chips - 1):
            away(i).wait_recv()
            side(others[chips - 2 - i]).start()
        close()
        finish()
        side(z).wait()
        for i in range(chips - 1):
            side(others[i]).wait()
            away(i).wait_send()
        own.wait()

    dma = pltpu.SemaphoreType.DMA
    hop = dma((batch_size, chips))
    line = dma((chips,))
    return pl.pallas_call(
        kernel,
        out_shape=(
            jax.ShapeDtypeStruct(w_all.shape, w_all.dtype),
            jax.ShapeDtypeStruct((head_count * tok, kv_cols), kv_own.dtype),
        ),
        in_specs=[ANY, WHOLE],
        out_specs=(ANY, ANY),
        scratch_shapes=[hop] * 6 + [dma, line, line, line, line],
        input_output_aliases={0: 0},
        compiler_params=pltpu.CompilerParams(collective_id=5, has_side_effects=True),
        cost_estimate=pl.CostEstimate(
            flops=0, bytes_accessed=100 * 1024 * 1024, transcendentals=0
        ),
        name="gather_rest",
    )(w_all, kv_own)


def project_out(attended, weight, tokens, vectors):
    tok, width = attended.shape

    def kernel(att_ref, tok_ref, vec_ref, w_ref, resid_ref, mixer_ref, normed_ref, inverse_ref):
        resid = matmul(att_ref[...], w_ref[...]) + vec_ref[4:5, :] + tok_ref[...].astype(F32)
        normed, inverse = norm_stats(resid)
        resid_ref[...] = resid
        normed_ref[...] = normed
        inverse_ref[...] = jnp.broadcast_to(inverse, inverse_ref.shape)
        mixer_ref[...] = (normed * vec_ref[2:3, :] + vec_ref[3:4, :]).astype(BF16)

    return pl.pallas_call(
        kernel,
        out_shape=(
            jax.ShapeDtypeStruct((tok, width), F32),
            jax.ShapeDtypeStruct((tok, width), BF16),
            jax.ShapeDtypeStruct((tok, width), F32),
            jax.ShapeDtypeStruct((tok, TILE), F32),
        ),
        in_specs=[WHOLE] * 4,
        out_specs=(WHOLE,) * 4,
        compiler_params=pltpu.CompilerParams(vmem_limit_bytes=VMEM_LIMIT),
        cost_estimate=pl.CostEstimate(
            flops=2 * tok * width * width, bytes_accessed=14 * width * width, transcendentals=0
        ),
        name="project_out",
    )(attended, tokens, vectors, weight)


def mixer_pass(mixer_in, cot_all, w_up, w_down, bias_up, owner, batch_size, head_count, cuts):
    tok, width = mixer_in.shape
    hid = w_up.shape[1]
    n = head_count // 2
    sub = tok // cuts
    block = (n, 2, cuts, sub)
    tiles = width // TILE
    owned = tiles // batch_size
    total_events = n * cuts
    pieces = 2
    piece = sub // pieces

    def kernel(
        owner_ref, x_ref, cot_ref, up_ref, down_ref, bias_ref,
        all_ref, hid_ref, pre_ref, mix_a_ref, mix_b_ref, grad_up_ref, down_ref_all, out_ref,
        sum_ref,
        x_buf, cot_buf, hid_buf, pre_buf, mine, give, pair_in, chain_in, right_in,
        up_acc, down_acc, stage, grad_down_ref,
        own_sem, x_sem, cot_sem, hid_sem, pre_sem, mix_sem,
        right_send, left_send, side_send, side_recv, line_recv,
        pair_send, pair_recv, chain_send, chain_recv, last_recv, down_send, down_recv, down_sem,
    ):
        mix_refs = (mix_a_ref, mix_b_ref)
        h = lax.axis_index("head")
        z = h // 2
        c = h % 2
        has_left = z > 0
        has_right = z < n - 1

        def at(chip):
            return {"head": chip * 2 + c}

        sibling = {"head": h + 1 - 2 * c}

        def remote(src, dst, send, recv, target):
            return pltpu.make_async_remote_copy(
                src_ref=src, dst_ref=dst, send_sem=send, recv_sem=recv,
                device_id=target, device_id_type=MESH,
            )

        def row_copy(chip, g, way):
            spot = all_ref.at[chip, c, g]
            if way == 0:
                return remote(spot, spot, right_send.at[chip, g], line_recv.at[chip, g], at(z + 1))
            if way == 1:
                return remote(spot, spot, left_send.at[chip, g], line_recv.at[chip, g], at(z - 1))
            return remote(spot, spot, side_send.at[chip, g], side_recv.at[chip, g], sibling)

        def pair_copy(chip, g):
            return remote(
                give.at[chip, g], pair_in.at[chip, g], pair_send.at[chip, g],
                pair_recv.at[chip, g], sibling,
            )

        def chain_copy(chip, g, e, target):
            part = pl.ds(e * piece, piece)
            return remote(
                mine.at[chip, g, part], chain_in.at[chip, g, part], chain_send.at[chip, g, e],
                chain_recv.at[chip, g, e], at(target),
            )

        def last_copy(chip, g, e):
            part = pl.ds(e * piece, piece)
            return remote(
                mine.at[chip, g, part], right_in.at[g, part], chain_send.at[chip, g, e],
                last_recv.at[g, e], at(z - 1),
            )

        b = lax.axis_index("batch")

        def peer(k):
            return {"batch": b ^ k}

        def down_copy(k):
            return remote(
                grad_down_ref.at[pl.ds((b ^ k) * owned, owned)], down_ref_all.at[k],
                down_send.at[k], down_recv.at[k], peer(k),
            )

        def down_own():
            return pltpu.make_async_copy(
                grad_down_ref.at[pl.ds(b * owned, owned)], down_ref_all.at[0], down_sem
            )

        barrier = pltpu.get_barrier_semaphore()
        pl.semaphore_signal(barrier, inc=1, device_id=sibling, device_id_type=MESH)
        for k in range(1, batch_size):
            pl.semaphore_signal(barrier, inc=1, device_id=peer(k), device_id_type=MESH)

        @pl.when(has_left)
        def _():
            pl.semaphore_signal(barrier, inc=1, device_id=at(z - 1), device_id_type=MESH)

        @pl.when(has_right)
        def _():
            pl.semaphore_signal(barrier, inc=1, device_id=at(z + 1), device_id_type=MESH)

        own = pltpu.make_async_copy(x_ref, all_ref.at[z, c], own_sem)
        own.start()
        sum_ref[...] = jnp.zeros_like(sum_ref)
        up_acc[...] = jnp.zeros_like(up_acc)
        down_acc[...] = jnp.zeros_like(down_acc)
        pl.semaphore_wait(
            barrier, batch_size + has_left.astype(jnp.int32) + has_right.astype(jnp.int32)
        )
        own.wait()

        def pass_on(chip, g):
            @pl.when((chip <= z) & has_right)
            def _():
                row_copy(chip, g, 0).start()

            @pl.when((chip >= z) & has_left)
            def _():
                row_copy(chip, g, 1).start()

            row_copy(chip, g, 2).start()

        for g in range(cuts):
            pass_on(z, g)

        def compute(chip, g):
            cot_load = pltpu.make_async_copy(cot_ref.at[chip, :, g], cot_buf, cot_sem)
            cot_load.start()
            row_copy(chip, g, 2).wait_recv()
            x_load = pltpu.make_async_copy(all_ref.at[chip, :, g], x_buf, x_sem)
            x_load.start()
            cot_load.wait()
            grad_hidden = matmul_nt(cot_buf[...].reshape(2 * sub, width), down_ref[...])
            x_load.wait()
            pre_act = matmul(x_buf[...].reshape(2 * sub, width), up_ref[...]) + bias_ref[...]
            hidden, slope = gelu_pair(pre_act)
            hid_buf[...] = hidden.astype(BF16).reshape(2, sub, hid)
            hid_store = pltpu.make_async_copy(hid_buf, hid_ref.at[chip, :, g], hid_sem)
            hid_store.start()
            grad_pre = (grad_hidden * slope).astype(BF16)
            pre_buf[...] = grad_pre.reshape(2, sub, hid)
            pre_store = pltpu.make_async_copy(pre_buf, pre_ref.at[chip, :, g], pre_sem)
            pre_store.start()
            sum_ref[...] += jnp.sum(
                grad_pre.astype(F32).reshape(2 * sub // 8, 8, hid), axis=0
            )
            share = matmul_nt(grad_pre, up_ref[...]).astype(BF16).reshape(2, sub, width)

            @pl.when(c == 0)
            def _():
                mine[chip, g] = share[0]
                give[chip, g] = share[1]

            @pl.when(c == 1)
            def _():
                mine[chip, g] = share[1]
                give[chip, g] = share[0]

            pair_copy(chip, g).start()
            down_acc[...] += matmul_t(
                cot_buf[...].reshape(2 * sub, width), hid_buf[...].reshape(2 * sub, hid)
            ).reshape(tiles, TILE, hid)
            hid_store.wait()
            pre_store.wait()

        def nearest(i):
            edge = jnp.minimum(z, n - 1 - z)
            near = (i + 1) // 2
            inner = jnp.where(i % 2 == 1, z - near, z + near)
            far = i - edge
            outer = jnp.where(z < n - 1 - z, z + far, z - far)
            return jnp.where(i <= 2 * edge, inner, outer)

        def compute_rest(index):
            chip = nearest(index // cuts)
            g = index % cuts
            loads = [
                pltpu.make_async_copy(hid_ref.at[chip, :, g], hid_buf, hid_sem),
                pltpu.make_async_copy(all_ref.at[chip, :, g], x_buf, x_sem),
                pltpu.make_async_copy(pre_ref.at[chip, :, g], pre_buf, pre_sem),
            ]
            for load in loads:
                load.start()
            loads[0].wait()
            hidden = hid_buf[...].reshape(2 * sub, hid)
            stage[...] = matmul(hidden, down_ref[...]).astype(BF16).reshape(2, sub, width)
            for cut in range(cuts):

                @pl.when(g == cut)
                def _():
                    pltpu.make_async_copy(stage, mix_refs[cut].at[chip], mix_sem).start()

            loads[1].wait()
            loads[2].wait()
            up_acc[...] += matmul_t(
                x_buf[...].reshape(2 * sub, width), pre_buf[...].reshape(2 * sub, hid)
            ).reshape(tiles, TILE, hid)
            pltpu.make_async_copy(stage, mix_refs[0].at[chip], mix_sem).wait()

        def add_up(chip, g, e, more):
            part = pl.ds(e * piece, piece)
            total = mine[chip, g, part, :].astype(F32) + pair_in[chip, g, part, :].astype(F32)

            @pl.when(more)
            def _():
                chain_copy(chip, g, e, z).wait_recv()
                mine[chip, g, part, :] = (
                    total + chain_in[chip, g, part, :].astype(F32)
                ).astype(BF16)

            @pl.when(jnp.logical_not(more))
            def _():
                mine[chip, g, part, :] = total.astype(BF16)

        def step(t, carry):
            d = t // cuts
            g = t % cuts

            @pl.when((d > 0) & (z >= d))
            def _():
                row_copy(z - d, g, 0).wait_recv()
                pass_on(z - d, g)

            @pl.when((d > 0) & (z + d < n))
            def _():
                row_copy(z + d, g, 1).wait_recv()
                pass_on(z + d, g)

            def one_side(side, inner):
                chip = z + d * (2 * side - 1)

                @pl.when((chip >= 0) & (chip < n) & (d < n) & ((d > 0) | (side == 0)))
                def _():
                    compute(chip, g)

                return inner

            lax.fori_loop(0, 2, one_side, 0)

            @pl.when(t == (jnp.maximum(z, n - 1 - z) + 1) * cuts - 1)
            def _():
                def put_down(p, inner):
                    grad_down_ref[p] = down_acc[owner_ref[p]].astype(BF16)
                    return inner

                lax.fori_loop(0, tiles, put_down, 0)
                for k in range(1, batch_size):
                    down_copy(k).start()
                down_own().start()

            from_left = jnp.maximum(t - z, 0)
            chip_right = from_left // cuts
            g_right = from_left % cuts

            @pl.when((t >= z) & (chip_right > z) & (chip_right < n))
            def _():
                pair_copy(chip_right, g_right).wait_recv()
                for e in range(pieces):
                    add_up(chip_right, g_right, e, has_left)
                    chain_copy(chip_right, g_right, e, z + 1).start()

            from_right = jnp.maximum(t - (n - 1 - z), 0)
            chip_left = n - 1 - from_right // cuts
            g_left = from_right % cuts

            @pl.when((t >= n - 1 - z) & (chip_left < z) & (chip_left >= 0))
            def _():
                pair_copy(chip_left, g_left).wait_recv()
                for e in range(pieces):
                    add_up(chip_left, g_left, e, has_right)

                    @pl.when(chip_left == z - 1)
                    def _():
                        last_copy(chip_left, g_left, e).start()

                    @pl.when(chip_left < z - 1)
                    def _():
                        chain_copy(chip_left, g_left, e, z - 1).start()

            events = (z >= d).astype(jnp.int32) + (z + d < n).astype(jnp.int32)
            events = jnp.where((d == 0) | (d >= n), 1, events)
            ready = (events < 2) & (carry < total_events)

            @pl.when(ready)
            def _():
                compute_rest(carry)

            return carry + ready.astype(jnp.int32)

        done = lax.fori_loop(0, n * cuts + n - 1, step, 0)

        def left_over(index, carry):
            @pl.when(index >= done)
            def _():
                compute_rest(index)

            return carry

        lax.fori_loop(0, total_events, left_over, 0)

        def put_tile(p, carry):
            grad_up_ref[p] = up_acc[owner_ref[p]].astype(BF16)
            return carry

        lax.fori_loop(0, tiles, put_tile, 0)

        for g in range(cuts):
            pair_copy(z, g).wait_recv()
            out_ref[g] = mine[z, g].astype(F32) + pair_in[z, g].astype(F32)

            @pl.when(has_left)
            def _():
                for e in range(pieces):
                    chain_copy(z, g, e, z).wait_recv()
                out_ref[g] += chain_in[z, g].astype(F32)

            @pl.when(has_right)
            def _():
                for e in range(pieces):
                    last_copy(z, g, e).wait_recv()
                out_ref[g] += right_in[g].astype(F32)

        def finish(chip, carry):
            for g in range(cuts):

                @pl.when((chip <= z) & has_right)
                def _():
                    row_copy(chip, g, 0).wait_send()

                @pl.when((chip >= z) & has_left)
                def _():
                    row_copy(chip, g, 1).wait_send()

                row_copy(chip, g, 2).wait_send()
                pair_copy(chip, g).wait_send()

                @pl.when(chip != z)
                def _():
                    for e in range(pieces):
                        chain_copy(chip, g, e, z).wait_send()

            return carry

        lax.fori_loop(0, n, finish, 0)
        for k in range(1, batch_size):
            down_copy(k).wait()
        down_own().wait()

    dma = pltpu.SemaphoreType.DMA
    vm = pltpu.VMEM
    each = dma((n, cuts))
    shares = vm((n, cuts, sub, width), BF16)
    outs = pl.pallas_call(
        kernel,
        out_shape=(
            jax.ShapeDtypeStruct(block + (width,), BF16),
            jax.ShapeDtypeStruct(block + (hid,), BF16),
            jax.ShapeDtypeStruct(block + (hid,), BF16),
            jax.ShapeDtypeStruct((n, 2, sub, width), BF16),
            jax.ShapeDtypeStruct((n, 2, sub, width), BF16),
            jax.ShapeDtypeStruct((tiles, TILE, hid), BF16),
            jax.ShapeDtypeStruct((batch_size, owned, TILE, hid), BF16),
            jax.ShapeDtypeStruct((cuts, sub, width), F32),
            jax.ShapeDtypeStruct((8, hid), F32),
        ),
        in_specs=[pl.BlockSpec(memory_space=pltpu.SMEM), WHOLE, ANY, WHOLE, WHOLE, WHOLE],
        out_specs=(ANY, ANY, ANY, ANY, ANY, WHOLE, ANY, WHOLE, WHOLE),
        scratch_shapes=[
            vm((2, sub, width), BF16),
            vm((2, sub, width), BF16),
            vm((2, sub, hid), BF16),
            vm((2, sub, hid), BF16),
            shares, shares, shares, shares,
            vm((cuts, sub, width), BF16),
            vm((tiles, TILE, hid), F32),
            vm((tiles, TILE, hid), F32),
            vm((2, sub, width), BF16),
            vm((tiles, TILE, hid), BF16),
            dma, dma, dma, dma, dma, dma,
            each, each, each, each, each,
            each, each, dma((n, cuts, pieces)), dma((n, cuts, pieces)),
            dma((cuts, pieces)),
            dma((batch_size,)), dma((batch_size,)), dma,
        ],
        compiler_params=pltpu.CompilerParams(
            collective_id=3, has_side_effects=True, vmem_limit_bytes=VMEM_LIMIT
        ),
        cost_estimate=pl.CostEstimate(
            flops=12 * n * 2 * tok * width * hid, bytes_accessed=300 * 1024 * 1024, transcendentals=0
        ),
        name="mixer_pass",
    )(
        owner,
        mixer_in.reshape(cuts, sub, width),
        cot_all.reshape(block + (width,)),
        w_up,
        w_down,
        bias_up.reshape(1, hid),
    )
    _, _, _, mix_a, mix_b, grad_up, grad_down, grad_in, bias_sum = outs
    return (
        mix_a.reshape(2 * n * sub, width),
        mix_b.reshape(2 * n * sub, width),
        grad_up.reshape(batch_size, owned * TILE, hid),
        grad_down.reshape(batch_size, owned * TILE, hid),
        grad_in.reshape(tok, width),
        jnp.sum(bias_sum, axis=0),
    )


def attention_forward(queries, key_rows, value_turned, mask, slabs):
    tok, width = queries.shape
    seq_len, head_size = key_rows.shape
    slab = width // slabs
    heads = slab // head_size
    scale = LOG2E / math.sqrt(head_size)

    def kernel(q_ref, k_ref, v_ref, mask_ref, o_ref, log_ref):
        for j in range(heads):
            spot = slice(j * head_size, (j + 1) * head_size)
            scores = matmul_nt(k_ref[...], q_ref[:, spot]) * scale + mask_ref[...]
            highest = jnp.max(scores, axis=0, keepdims=True)
            raised = jnp.exp2(scores - highest)
            total = jnp.sum(raised, axis=0, keepdims=True)
            out = matmul(v_ref[...], raised.astype(BF16)) / total
            o_ref[:, spot] = out.T.astype(BF16)
            log_ref[0, j : j + 1, :] = highest + jnp.log2(total)

    return pl.pallas_call(
        kernel,
        grid=(slabs,),
        out_shape=(
            jax.ShapeDtypeStruct((tok, width), BF16),
            jax.ShapeDtypeStruct((slabs, heads, tok), F32),
        ),
        in_specs=[
            pl.BlockSpec((tok, slab), lambda i: (0, i)),
            pl.BlockSpec((seq_len, head_size), lambda i: (0, 0)),
            pl.BlockSpec((head_size, seq_len), lambda i: (0, 0)),
            pl.BlockSpec((seq_len, tok), lambda i: (0, 0)),
        ],
        out_specs=(
            pl.BlockSpec((tok, slab), lambda i: (0, i)),
            pl.BlockSpec((1, heads, tok), lambda i: (i, 0, 0)),
        ),
        compiler_params=pltpu.CompilerParams(vmem_limit_bytes=VMEM_LIMIT),
        cost_estimate=pl.CostEstimate(
            flops=8 * tok * seq_len * width,
            bytes_accessed=4 * tok * width,
            transcendentals=tok * seq_len * slabs * heads,
        ),
        name="attention_forward",
    )(queries, key_rows, value_turned, mask)


def backward_pass(
    owner, grad_mixer, cotangent, tokens, normed_two, inverse_two, vectors, queries, attended,
    log_totals, key_rows, key_turned, value_rows, mask, w_query_all, w_out_all, w_kv, up_parts,
    batch_size, head_count,
):
    tok, width = tokens.shape
    seq_len, head_size = key_rows.shape
    slab = width // head_count
    heads = slab // head_size
    n = head_count // 2
    tiles = width // TILE
    cols_out = width // batch_size
    half_rows = slab // 2
    kv_cols = 2 * head_size
    kv_rows = width // head_count // batch_size
    ring = batch_size == 4
    scale = LOG2E / math.sqrt(head_size)
    plain_scale = 1.0 / math.sqrt(head_size)
    block = 512 if seq_len % 512 == 0 else seq_len

    def kernel(
        owner_ref, gm_ref, cot_ref, tok_ref, n2_ref, i2_ref, vec_ref, q_ref, att_ref, log_ref,
        k_ref, kt_ref, v_ref, mask_ref, wq_ref, wo_ref, wkv_ref, up_ref,
        tokens_out, query_out, out_out, kv_out, vec_out, up_out,
        branch, wide_tiles, normed_owned, branch_owned, grad_in, wq_buf, wo_buf, dk, dv,
        give, mine, pair_in, land, hop, z_land,
        dkv, dkv_pair, dkv_here, dkv_land,
        kv_part, kv_pair, kv_sum, kv_land, kv_half, kv_zland,
        vec_part, vec_land, vec_sum, vec_bland, up_land,
        gm_sem, n2_sem, cot_sem, free_sem, wq_sem, wo_sem, pair_send, pair_recv, hop_send, hop_recv, land_send, land_recv,
        z_send, z_recv, dkv_s, dkv_r, dkz_s, dkz_r,
        s_pair, r_pair, s_kvb, r_kvb, s_kvz, r_kvz, s_kva, r_kva,
        s_vh, r_vh, s_vb, r_vb, s_va, r_va, s_up, r_up,
    ):
        b = lax.axis_index("batch")
        h = lax.axis_index("head")
        z = h // 2
        c = h % 2
        sibling = {"head": h + 1 - 2 * c}

        def at_chip(r):
            return {"head": lax.rem(z + r, n) * 2 + c}

        def other(d):
            return {"head": lax.rem(h + d, head_count)}

        def peer(k):
            return {"batch": b ^ k}

        def remote(src, dst, send, recv, target):
            return pltpu.make_async_remote_copy(
                src_ref=src, dst_ref=dst, send_sem=send, recv_sem=recv,
                device_id=target, device_id_type=MESH,
            )

        greet([other(d) for d in range(1, head_count)] + [peer(k) for k in range(1, batch_size)])

        up_copies = [
            remote(up_ref, up_land.at[k], s_up.at[k], r_up.at[k], peer(k))
            for k in range(1, batch_size)
        ]
        for copy in up_copies:
            copy.start()

        def slab_at(s):
            chip = lax.rem(z + 1 + s // 2, n)
            return chip * 2 + jnp.where(s % 2 == 0, 1 - c, c)

        def weight_loads(s):
            i = slab_at(s)
            return (
                pltpu.make_async_copy(
                    wq_ref.at[:, lanes(i * slab, slab, slab)], wq_buf, wq_sem
                ),
                pltpu.make_async_copy(
                    wo_ref.at[lanes(i * slab, slab, slab), :], wo_buf, wo_sem
                ),
            )

        norm_loads = (
            pltpu.make_async_copy(gm_ref, tokens_out, gm_sem),
            pltpu.make_async_copy(n2_ref, grad_in, n2_sem),
            pltpu.make_async_copy(cot_ref, branch, cot_sem),
        )
        for load in norm_loads + weight_loads(0):
            load.start()

        def put_vector(row, value):
            for i in range(head_count):
                vec_part[i, row : row + 1, :] = value[:, i * slab : (i + 1) * slab]

        def column_sum(value):
            return jnp.sum(value, axis=0, keepdims=True)

        for load in norm_loads:
            load.wait()
        grad_mix = tokens_out[...]
        normed_two_rows = grad_in[...]
        grad_out_rows = branch[...].astype(F32)
        put_vector(5, column_sum(grad_out_rows))
        grad_resid = grad_out_rows + norm_back(
            grad_mix, normed_two_rows, i2_ref[:, :1], vec_ref[2:3, :]
        )
        put_vector(2, column_sum(grad_mix * normed_two_rows))
        put_vector(3, column_sum(grad_mix))
        tokens_out[...] = grad_resid
        grad_branch = grad_resid.astype(BF16)
        branch[...] = grad_branch

        put_vector(4, column_sum(grad_branch.astype(F32)))

        for p in range(tiles):
            wide_tiles[p] = branch[:, p * TILE : (p + 1) * TILE]

        for p in range(tiles):
            branch_owned[:, p * TILE : (p + 1) * TILE] = wide_tiles[owner_ref[p]]
        normed_one, inverse_one = norm_stats(tok_ref[...].astype(F32))
        normed_in = (normed_one * vec_ref[0:1, :] + vec_ref[1:2, :]).astype(BF16)
        for p in range(tiles):
            wide_tiles[p] = normed_in[:, p * TILE : (p + 1) * TILE]

        for p in range(tiles):
            normed_owned[:, p * TILE : (p + 1) * TILE] = wide_tiles[owner_ref[p]]
        dk[...] = jnp.zeros_like(dk)
        dv[...] = jnp.zeros_like(dv)
        grad_in[...] = jnp.zeros_like(grad_in)

        def pair_copy(q):
            return remote(
                give.at[q % 2], pair_in.at[q % 2], pair_send.at[q], pair_recv.at[q], sibling
            )

        halves = (pl.ds(0, half_rows), pl.ds(half_rows, half_rows))

        def hop_copy(q, k):
            part = halves[1 if k == 1 else 0]
            return remote(
                mine.at[q, b ^ 3, part], hop.at[q, k - 1], hop_send.at[q, k], hop_recv.at[q, k],
                peer(k),
            )

        def land_copy(q, k, which):
            if which is None:
                return remote(
                    mine.at[q, b ^ k], land.at[q, k - 1], land_send.at[q, k, 0],
                    land_recv.at[q, k, 0], peer(k),
                )
            part = halves[which]
            return remote(
                mine.at[q, b ^ k, part], land.at[q, k - 1, part], land_send.at[q, k, which],
                land_recv.at[q, k, which], peer(k),
            )

        def z_copy(q):
            return remote(
                mine.at[q, b], z_land.at[q], z_send.at[q], z_recv.at[q], at_chip(q % n + 1)
            )

        def pair_start(q, value):
            @pl.when(q >= 2)
            def _():
                pair_copy(q - 2).wait_send()
                pl.semaphore_wait(free_sem, 1)

            for k in range(batch_size):
                give[q % 2, k] = value[:, k * cols_out : (k + 1) * cols_out]
            pair_copy(q).start()

        def plane_start(q):
            pair_copy(q).wait_recv()
            mine[q] = (mine[q].astype(F32) + pair_in[q % 2].astype(F32)).astype(BF16)

            @pl.when(q < 2 * n - 2)
            def _():
                pl.semaphore_signal(free_sem, inc=1, device_id=sibling, device_id_type=MESH)

            if ring:
                hop_copy(q, 1).start()
                hop_copy(q, 2).start()
                land_copy(q, 1, 1).start()
                land_copy(q, 2, 0).start()
            else:
                for k in range(1, batch_size):
                    land_copy(q, k, None).start()

        def plane_hop(q):
            if not ring:
                return
            for k in (1, 2):
                hop_copy(q, 3 - k).wait_recv()
                which = 0 if k == 1 else 1
                part = halves[which]
                mine[q, b ^ k, part, :] = (
                    mine[q, b ^ k, part, :].astype(F32) + hop[q, 2 - k].astype(F32)
                ).astype(BF16)
                land_copy(q, k, which).start()

        def plane_end(q):
            total = mine[q, b].astype(F32)
            for k in range(1, 3 if ring else batch_size):
                for which in (0, 1) if ring else (None,):
                    land_copy(q, k, which).wait_recv()
                total += land[q, k - 1].astype(F32)
            mine[q, b] = total.astype(BF16)

            @pl.when(q % n < n - 1)
            def _():
                z_copy(q).start()

        def out_gradient(i):
            att = att_ref[:, lanes(i * slab, slab, slab)]
            return matmul(att.astype(F32).T.astype(BF16), branch_owned[...]).astype(BF16)

        def put_mine(q, value):
            for k in range(batch_size):
                mine[q, k] = value[:, k * cols_out : (k + 1) * cols_out]

        def out_pairs(j, carry):
            pair_start(j, out_gradient(slab_at(2 * j)))
            put_mine(j, out_gradient(slab_at(2 * j + 1)))

            @pl.when(j >= 1)
            def _():
                plane_start(j - 1)

            return carry

        lax.fori_loop(0, n, out_pairs, 0)
        plane_start(n - 1)

        def work(s, carry):
            j = s // 2
            i = slab_at(s)
            cols = lanes(i * slab, slab, slab)

            loads = weight_loads(s)
            loads[1].wait()
            grad_att = matmul_nt(branch[...], wo_buf[...]).astype(BF16)

            @pl.when(s + 1 < head_count)
            def _():
                weight_loads(s + 1)[1].start()

            queries_here = q_ref[:, cols]
            att_here = att_ref[:, cols]
            logs_here = log_ref[i]
            parts = []
            for e in range(heads):
                spot = slice(e * head_size, (e + 1) * head_size)
                query = queries_here[:, spot]
                grad = grad_att[:, spot]
                joint = grad.astype(F32) * att_here[:, spot].astype(F32)
                delta = jnp.sum(joint.T, axis=0, keepdims=True)
                logs = logs_here[e : e + 1, :]
                total = jnp.zeros((head_size, tok), F32)
                for start in range(0, seq_len, block):
                    part = slice(start, start + block)
                    scores = matmul_nt(k_ref[part, :], query) * scale
                    probs = jnp.exp2(scores + (mask_ref[part, :].astype(F32) - logs))
                    grad_probs = matmul_nt(v_ref[part, :], grad)
                    grad_scores = (probs * (grad_probs - delta)).astype(BF16)
                    dv[part, :] += matmul(probs.astype(BF16), grad)
                    dk[part, :] += matmul(grad_scores, query)
                    total += matmul(kt_ref[:, part], grad_scores)
                parts.append(total * plain_scale)
            turned = jnp.concatenate(parts, axis=0) if heads > 1 else parts[0]
            grad_q = turned.T.astype(BF16)
            vec_part[i, 6:7, :] = column_sum(grad_q.astype(F32))
            grad_query = matmul(turned.astype(BF16), normed_owned[...]).astype(BF16)

            @pl.when(s % 2 == 0)
            def _():
                pair_start(n + j, grad_query)

            @pl.when(s % 2 == 1)
            def _():
                put_mine(n + j, grad_query)

            loads[0].wait()
            grad_in[...] += matmul_nt(grad_q, wq_buf[...])

            @pl.when(s + 1 < head_count)
            def _():
                weight_loads(s + 1)[0].start()

            @pl.when(s < n)
            def _():
                plane_hop(s)

            @pl.when((s >= 2) & (s < n + 2))
            def _():
                plane_end(s - 2)

            @pl.when(s % 2 == 1)
            def _():
                plane_start(n + j)

                @pl.when(j >= 1)
                def _():
                    plane_hop(n + j - 1)

                @pl.when(j >= 2)
                def _():
                    plane_end(n + j - 2)

            return carry

        lax.fori_loop(0, head_count, work, 0)

        dkv[:, :, :, :head_size] = (dk[...] * plain_scale).astype(BF16).reshape(n, 2, tok, head_size)
        dkv[:, :, :, head_size:] = dv[...].astype(BF16).reshape(n, 2, tok, head_size)
        dkv_swap = remote(dkv.at[:, 1 - c], dkv_pair, dkv_s, dkv_r, sibling)
        dkv_swap.start()
        dkv_swap.wait_recv()
        for r in range(n):
            dkv_here[r] = (dkv[r, c].astype(F32) + dkv_pair[r].astype(F32)).astype(BF16)
        dkv_copies = [
            remote(
                dkv_here.at[lax.rem(z + r, n)], dkv_land.at[r], dkz_s.at[r], dkz_r.at[r],
                at_chip(r),
            )
            for r in range(1, n)
        ]
        for copy in dkv_copies:
            copy.start()
        normed_one, inverse_one = norm_stats(tok_ref[...].astype(F32))
        normed_in = (normed_one * vec_ref[0:1, :] + vec_ref[1:2, :]).astype(BF16)
        plane_hop(2 * n - 1)
        grad_kv = dkv_here[z].astype(F32)
        for copy in dkv_copies:
            copy.wait_recv()
        for r in range(1, n):
            grad_kv += dkv_land[r].astype(F32)
        grad_kv = grad_kv.astype(BF16)

        kv_part[...] = (
            matmul_t(normed_in, grad_kv)
            .astype(BF16)
            .reshape(n, 2, batch_size, kv_rows, kv_cols)
        )
        pair_kv = remote(kv_part.at[:, 1 - c], kv_pair, s_pair, r_pair, sibling)
        pair_kv.start()

        grad_normed = grad_in[...] + matmul_nt(grad_kv, wkv_ref[...])
        pair_kv.wait_recv()
        for r in range(n):
            kv_sum[r] = (kv_part[r, c].astype(F32) + kv_pair[r].astype(F32)).astype(BF16)
        kv_copies = [
            remote(kv_sum.at[:, b ^ k], kv_land.at[k], s_kvb.at[k], r_kvb.at[k], peer(k))
            for k in range(1, batch_size)
        ]
        for copy in kv_copies:
            copy.start()
        put_vector(0, column_sum(grad_normed * normed_one))
        put_vector(1, column_sum(grad_normed))
        for i in range(head_count):
            vec_part[i, 7:8, :] = jnp.zeros((1, slab), F32)
        vec_part[0, 7:8, :head_size] = column_sum(grad_kv[:, head_size:].astype(F32))
        vec_copies = [
            remote(
                vec_part.at[lax.rem(h + d, head_count)], vec_land.at[d], s_vh.at[d], r_vh.at[d],
                other(d),
            )
            for d in range(1, head_count)
        ]
        for copy in vec_copies:
            copy.start()
        tokens_out[...] += norm_back(grad_normed, normed_one, inverse_one, vec_ref[0:1, :])
        total = vec_part[h]
        for copy in vec_copies:
            copy.wait_recv()
        for d in range(1, head_count):
            total += vec_land[d]
        vec_sum[...] = total
        vec_bcopies = [
            remote(vec_sum, vec_bland.at[k], s_vb.at[k], r_vb.at[k], peer(k))
            for k in range(1, batch_size)
        ]
        for copy in vec_bcopies:
            copy.start()
        up_total = up_ref[...]
        for copy in up_copies:
            copy.wait_recv()
        for k in range(1, batch_size):
            up_total += up_land[k]
        up_out[...] = up_total
        for copy in kv_copies:
            copy.wait_recv()
        kv_total = kv_sum[:, b].astype(F32)
        for k in range(1, batch_size):
            kv_total += kv_land[k].astype(F32)
        kv_half[...] = kv_total.astype(BF16)
        kv_zcopies = [
            remote(
                kv_half.at[lax.rem(z + r, n)], kv_zland.at[r], s_kvz.at[r], r_kvz.at[r], at_chip(r)
            )
            for r in range(1, n)
        ]
        for copy in kv_zcopies:
            copy.start()
        for copy in vec_bcopies:
            copy.wait_recv()
        total = vec_sum[...]
        for k in range(1, batch_size):
            total += vec_bland[k]
        vec_out[h] = total
        vec_acopies = [
            remote(vec_out.at[h], vec_out.at[h], s_va.at[d], r_va.at[d], other(d))
            for d in range(1, head_count)
        ]
        for copy in vec_acopies:
            copy.start()
        for copy in kv_zcopies:
            copy.wait_recv()
        kv_mine = kv_half[z].astype(F32)
        for r in range(1, n):
            kv_mine += kv_zland[r].astype(F32)
        kv_out[b] = kv_mine
        kv_acopies = [
            remote(kv_out.at[b], kv_out.at[b], s_kva.at[k], r_kva.at[k], peer(k))
            for k in range(1, batch_size)
        ]
        for copy in kv_acopies:
            copy.start()

        plane_end(2 * n - 2)
        plane_end(2 * n - 1)
        for first, target in ((0, out_out), (n, query_out)):
            total = mine[first + n - 1, b].astype(F32)
            for r in range(n - 1):
                z_copy(first + r).wait_recv()
                total += z_land[first + r].astype(F32)
            target[0] = total.astype(BF16)
        for copy in vec_acopies + kv_acopies:
            copy.wait_recv()

        for copy in up_copies + [dkv_swap, pair_kv] + dkv_copies + vec_copies + kv_copies:
            copy.wait_send()
        for copy in vec_bcopies + kv_zcopies + vec_acopies + kv_acopies:
            copy.wait_send()
        pair_copy(2 * n - 2).wait_send()
        pair_copy(2 * n - 1).wait_send()

        def finish(q, carry):
            @pl.when(q % n < n - 1)
            def _():
                z_copy(q).wait_send()

            if ring:
                for k in (1, 2):
                    hop_copy(q, k).wait_send()
                    for which in (0, 1):
                        land_copy(q, k, which).wait_send()
            else:
                for k in range(1, batch_size):
                    land_copy(q, k, None).wait_send()
            return carry

        lax.fori_loop(0, 2 * n, finish, 0)

    dma = pltpu.SemaphoreType.DMA
    vm = pltpu.VMEM
    nb, nh = batch_size, head_count
    lands = 2 if ring else nb - 1
    shared = (nb, slab, cols_out)
    return pl.pallas_call(
        kernel,
        out_shape=(
            jax.ShapeDtypeStruct((tok, width), F32),
            jax.ShapeDtypeStruct((1, slab, cols_out), BF16),
            jax.ShapeDtypeStruct((1, slab, cols_out), BF16),
            jax.ShapeDtypeStruct((nb, kv_rows, kv_cols), F32),
            jax.ShapeDtypeStruct((nh, 8, slab), F32),
            jax.ShapeDtypeStruct(up_parts.shape, F32),
        ),
        in_specs=[pl.BlockSpec(memory_space=pltpu.SMEM), ANY, ANY, WHOLE, ANY]
        + [WHOLE] * 9
        + [ANY, ANY, WHOLE, WHOLE],
        out_specs=(WHOLE,) * 6,
        scratch_shapes=[
            vm((tok, width), BF16),
            vm((tiles, tok, TILE), BF16),
            vm((tok, width), BF16),
            vm((tok, width), BF16),
            vm((tok, width), F32),
            vm((width, slab), BF16),
            vm((slab, width), BF16),
            vm((seq_len, head_size), F32),
            vm((seq_len, head_size), F32),
            vm((2,) + shared, BF16),
            vm((2 * n,) + shared, BF16),
            vm((2,) + shared, BF16),
            vm((2 * n, lands, slab, cols_out), BF16),
            vm((2 * n, 2, half_rows, cols_out) if ring else (1, 1, 16, TILE), BF16),
            vm((2 * n, slab, cols_out), BF16),
            vm((n, 2, tok, kv_cols), BF16),
            vm((n, tok, kv_cols), BF16),
            vm((n, tok, kv_cols), BF16),
            vm((n, tok, kv_cols), BF16),
            vm((n, 2, nb, kv_rows, kv_cols), BF16),
            vm((n, nb, kv_rows, kv_cols), BF16),
            vm((n, nb, kv_rows, kv_cols), BF16),
            vm((nb, n, kv_rows, kv_cols), BF16),
            vm((n, kv_rows, kv_cols), BF16),
            vm((n, kv_rows, kv_cols), BF16),
            vm((nh, 8, slab), F32),
            vm((nh, 8, slab), F32),
            vm((8, slab), F32),
            vm((nb, 8, slab), F32),
            vm((nb,) + up_parts.shape, F32),
            dma, dma, dma, pltpu.SemaphoreType.REGULAR, dma, dma,
            dma((2 * n,)), dma((2 * n,)), dma((2 * n, 3)), dma((2 * n, 3)),
            dma((2 * n, nb, 2)), dma((2 * n, nb, 2)), dma((2 * n,)), dma((2 * n,)), dma, dma, dma((n,)), dma((n,)),
            dma, dma, dma((nb,)), dma((nb,)), dma((n,)), dma((n,)), dma((nb,)), dma((nb,)),
            dma((nh,)), dma((nh,)), dma((nb,)), dma((nb,)), dma((nh,)), dma((nh,)),
            dma((nb,)), dma((nb,)),
        ],
        compiler_params=pltpu.CompilerParams(
            collective_id=4, has_side_effects=True, vmem_limit_bytes=VMEM_LIMIT + 2 * 1024 * 1024
        ),
        cost_estimate=pl.CostEstimate(
            flops=20 * tok * seq_len * width + 8 * tok * width * width,
            bytes_accessed=200 * 1024 * 1024,
            transcendentals=tok * seq_len * width // head_size,
        ),
        name="backward_pass",
    )(
        owner, grad_mixer, cotangent, tokens, normed_two, inverse_two, vectors, queries, attended,
        log_totals, key_rows, key_turned, value_rows, mask, w_query_all, w_out_all, w_kv, up_parts,
    )


def split_high(value):
    high = value.astype(BF16)
    return high, (value - high.astype(F32)).astype(BF16)


def matmul_three(first_op, second_op):
    first_high, first_low = split_high(first_op)
    second_high, second_low = split_high(second_op)
    return (
        matmul(first_high, second_high)
        + matmul(first_high, second_low)
        + matmul(first_low, second_high)
    )


def shampoo(
    first, second, first_weight, second_weight, owned, left, right, root_left, root_right, wide_rows,
    per_step,
):
    _, owned_count, columns, _, _ = left.shape

    steps = owned_count // per_step

    def kernel(ids_ref, *refs):
        del ids_ref
        one, two = refs[:2]
        w_one, w_two = refs[2 : 2 + per_step], refs[2 + per_step : 2 + 2 * per_step]
        l_ref, r_ref, p_ref, q_ref, g_out, l_out, r_out, w_out = refs[2 + 2 * per_step :]

        def update(turned):
            shares = two if turned else one
            for p in range(per_step):
                for t in range(columns):
                    wide = slice(p * TILE, (p + 1) * TILE)
                    spot = slice(t * TILE, (t + 1) * TILE)
                    part = (wide, spot) if wide_rows else (spot, wide)
                    grad = shares[(0,) + part].astype(F32)
                    for i in range(1, shares.shape[0]):
                        grad += shares[(i,) + part].astype(F32)
                    if turned == wide_rows:
                        grad = grad.T
                    weight = w_two[p][spot, :] if turned else w_one[p][:, spot]
                    high = grad.astype(BF16)
                    g_out[0, p, t] = grad
                    l_out[0, p, t] = DECAY_RATE * l_ref[0, p, t] + (1.0 - DECAY_RATE) * matmul_nt(
                        high, high
                    )
                    r_out[0, p, t] = DECAY_RATE * r_ref[0, p, t] + (1.0 - DECAY_RATE) * matmul_t(
                        high, high
                    )
                    stepped = matmul_three(p_ref[0, p, t], grad)
                    stepped = matmul_three(stepped, q_ref[0, p, t])
                    w_out[0, p, t] = weight.astype(F32) - MATRIX_RATE * stepped

        @pl.when(pl.program_id(0) == 0)
        def _():
            update(False)

        @pl.when(pl.program_id(0) == 1)
        def _():
            update(True)

    last = steps - 1

    def place_one(m, i):
        return jnp.where(m == 0, i, last)

    def place_two(m, i):
        return jnp.where(m == 1, i, 0)

    def share(array, place):
        if wide_rows:
            return pl.BlockSpec(
                (array.shape[0], per_step * TILE, columns * TILE),
                lambda m, i, ids: (0, place(m, i), 0),
            )
        return pl.BlockSpec(
            (array.shape[0], columns * TILE, per_step * TILE),
            lambda m, i, ids: (0, 0, place(m, i)),
        )

    def weight_one(p):
        return pl.BlockSpec(
            (TILE, columns * TILE), lambda m, i, ids: (ids[place_one(m, i) * per_step + p], 0)
        )

    def weight_two(p):
        return pl.BlockSpec(
            (columns * TILE, TILE), lambda m, i, ids: (0, ids[place_two(m, i) * per_step + p])
        )

    stat = pl.BlockSpec((1, per_step, columns, TILE, TILE), lambda m, i, ids: (m, i, 0, 0, 0))
    shape = jax.ShapeDtypeStruct(left.shape, F32)
    return pl.pallas_call(
        kernel,
        grid_spec=pltpu.PrefetchScalarGridSpec(
            num_scalar_prefetch=1,
            grid=(2, steps),
            in_specs=[share(first, place_one), share(second, place_two)]
            + [weight_one(p) for p in range(per_step)]
            + [weight_two(p) for p in range(per_step)]
            + [stat] * 4,
            out_specs=[stat] * 4,
        ),
        out_shape=[shape] * 4,
        compiler_params=pltpu.CompilerParams(vmem_limit_bytes=VMEM_LIMIT),
        cost_estimate=pl.CostEstimate(
            flops=left.size * TILE * 16, bytes_accessed=left.size * 40, transcendentals=0
        ),
        name="shampoo",
    )(
        owned,
        first,
        second,
        *([first_weight] * per_step),
        *([second_weight] * per_step),
        left,
        right,
        root_left,
        root_right,
    )


def shampoo_update(grad_tiles, left_old, right_old, root_left, root_right, weight_tiles):
    outer_left = jnp.einsum("...ij,...kj->...ik", grad_tiles, grad_tiles, precision=PRECISE)
    outer_right = jnp.einsum("...ji,...jk->...ik", grad_tiles, grad_tiles, precision=PRECISE)
    left_new = DECAY_RATE * left_old + (1.0 - DECAY_RATE) * outer_left
    right_new = DECAY_RATE * right_old + (1.0 - DECAY_RATE) * outer_right
    stepped = jnp.einsum("...ij,...jk->...ik", root_left, grad_tiles, precision=PRECISE)
    stepped = jnp.einsum("...ij,...jk->...ik", stepped, root_right, precision=PRECISE)
    return (grad_tiles, left_new, right_new, weight_tiles - MATRIX_RATE * stepped)


def diagonal_update(gradient, second, current):
    second_new = DECAY_RATE * second + (1.0 - DECAY_RATE) * gradient * gradient
    return (
        gradient,
        second_new,
        current - VECTOR_RATE * gradient / (jnp.sqrt(second_new) + SAFE_ADD),
    )


def gelu_pair(u):
    root = math.sqrt(2.0 / math.pi)
    square = u * u
    turn = jnp.tanh(root * u * (1.0 + 0.044715 * square))
    half = 0.5 * (1.0 + turn)
    slope = half + 0.5 * u * (1.0 - turn * turn) * root * (1.0 + 3.0 * 0.044715 * square)
    return u * half, slope


def body(
    tokens,
    cotangent,
    doc_starts,
    owner,
    vectors,
    bias_query,
    bias_value,
    bias_up,
    w_query,
    w_key,
    w_value,
    w_out,
    w_up,
    w_down,
    attn_left,
    attn_right,
    attn_root_left,
    attn_root_right,
    mixer_left,
    mixer_right,
    mixer_root_left,
    mixer_root_right,
    kv_left,
    kv_right,
    kv_root_left,
    kv_root_right,
    vector_second,
    query_second,
    value_second,
    up_second,
):
    batch_size = lax.axis_size("batch")
    head_count = lax.axis_size("head")
    batch_index = lax.axis_index("batch")
    head_index = lax.axis_index("head")
    tok_dev, width = tokens.shape
    seq_len = tok_dev * head_count
    row_start = head_index * tok_dev
    head_size = w_key.shape[1]
    slab = w_query.shape[1]
    gain_one = vectors[0]
    shift_one = vectors[1]
    bias_down = vectors[5]

    positions = jnp.arange(seq_len, dtype=jnp.int32)
    documents = jnp.sum((doc_starts[0][None, :] <= positions[:, None]).astype(jnp.int32), axis=1)
    row_ids = row_start + jnp.arange(tok_dev, dtype=jnp.int32)
    row_docs = lax.dynamic_slice_in_dim(documents, row_start, tok_dev, 0)
    allowed = (documents[:, None] == row_docs[None, :]) & (positions[:, None] <= row_ids[None, :])
    mask = jnp.where(allowed, 0.0, MASKED).astype(F32)

    w_query_all, w_out_part, bias_all = gather_weights(
        w_query, w_out, bias_query.reshape(1, slab), batch_size, head_count
    )
    w_out_part, cotangent_later, tokens_later = lax.optimization_barrier(
        (w_out_part, cotangent, tokens)
    )
    cot_all = lax.all_gather(cotangent_later, "head", axis=0, tiled=True)
    rows_own = tokens_later.astype(F32)
    normed_one, inverse_one = norm_stats(rows_own)
    normed_in = (normed_one * gain_one + shift_one).astype(BF16)
    w_kv = jnp.concatenate([w_key, w_value], axis=1)
    kv_bias = jnp.concatenate([jnp.zeros_like(bias_value), bias_value])
    kv_own = (matmul(normed_in, w_kv) + kv_bias).astype(BF16)
    w_out_all, kv_all = gather_rest(w_out_part, kv_own, batch_size, head_count)
    key_rows = kv_all[:, :head_size]
    value_rows = kv_all[:, head_size:]

    queries = (matmul(normed_in, w_query_all) + bias_all.reshape(1, width)).astype(BF16)
    attended, log_totals = attention_forward(queries, key_rows, value_rows.T, mask, head_count)
    resid, mixer_in, normed_two, inverse_wide = project_out(
        attended, w_out_all, tokens, vectors
    )

    mix_a, mix_b, grad_up, down_shares, grad_mixer_in, grad_up_bias = mixer_pass(
        mixer_in, cot_all, w_up, w_down, bias_up, owner, batch_size, head_count, 2
    )
    mix_first = lax.psum_scatter(mix_a, "head", scatter_dimension=0, tiled=True)
    up_shares = lax.psum_scatter(grad_up, "batch", scatter_dimension=0, tiled=True)

    kv_rows = width // head_count // batch_size
    grad_tokens, query_share, out_share, kv_total, vector_wide, up_bias_total = backward_pass(
        owner,
        grad_mixer_in,
        cotangent,
        tokens,
        normed_two,
        inverse_wide,
        vectors,
        queries,
        attended,
        log_totals,
        key_rows,
        key_rows.T,
        value_rows,
        mask.astype(BF16),
        w_query_all,
        w_out_all,
        w_kv,
        grad_up_bias.reshape(8, -1),
        batch_size,
        head_count,
    )
    kv_total, mix_first, mix_b = lax.optimization_barrier((kv_total, mix_first, mix_b))
    up_shares, mix_first = lax.optimization_barrier((up_shares, mix_first))
    mix_second = lax.psum_scatter(mix_b, "head", scatter_dimension=0, tiled=True)
    kv_total = kv_total.reshape(batch_size * kv_rows, 2 * head_size)
    up_bias_total = up_bias_total.reshape(-1)
    vector_all = vector_wide.transpose(1, 0, 2).reshape(8, width)
    vector_total = vector_all[:6]
    query_bias_total = lax.dynamic_slice_in_dim(vector_all[6], head_index * slab, slab, 0)
    value_bias_total = vector_all[7, :head_size]

    owned_count = attn_left.shape[1]
    owned = lax.dynamic_slice_in_dim(owner, batch_index * owned_count, owned_count, 0)
    mixer_out = shampoo(
        up_shares,
        down_shares,
        w_up,
        w_down,
        owned,
        mixer_left,
        mixer_right,
        mixer_root_left,
        mixer_root_right,
        True,
        1,
    )
    attn_out = shampoo(
        query_share,
        out_share,
        w_query,
        w_out,
        owned,
        attn_left,
        attn_right,
        attn_root_left,
        attn_root_right,
        False,
        attn_left.shape[1],
    )
    kv_count = width // head_count

    def kv_tiles(matrix):
        return matrix.reshape(kv_count // TILE, TILE, head_size // TILE, TILE).transpose(0, 2, 1, 3)

    kv_slab = lax.dynamic_slice_in_dim(w_kv, head_index * kv_count, kv_count, 0).astype(F32)
    kv_out = shampoo_update(
        jnp.stack([kv_tiles(kv_total[:, :head_size]), kv_tiles(kv_total[:, head_size:])]),
        kv_left,
        kv_right,
        kv_root_left,
        kv_root_right,
        jnp.stack([kv_tiles(kv_slab[:, :head_size]), kv_tiles(kv_slab[:, head_size:])]),
    )
    mix_one = jnp.concatenate([mix_first, mix_second], axis=0)
    output = resid + mix_one.astype(F32) + bias_down
    vec_out = diagonal_update(vector_total, vector_second, vectors)
    query_out = diagonal_update(query_bias_total, query_second, bias_query)
    value_out = diagonal_update(value_bias_total, value_second, bias_value)
    up_out = diagonal_update(up_bias_total, up_second, bias_up)
    return (
        output,
        grad_tokens,
        vec_out[0],
        vec_out[1][2:],
        vec_out[1][:2],
        vec_out[2],
        query_out[0],
        query_out[1],
        query_out[2],
        value_out[0],
        value_out[1],
        value_out[2],
        up_out[0],
        up_out[1],
        up_out[2],
        attn_out[0],
        attn_out[1],
        attn_out[2],
        attn_out[3],
        mixer_out[0],
        mixer_out[1],
        mixer_out[2],
        mixer_out[3],
        kv_out[0],
        kv_out[1],
        kv_out[2],
        kv_out[3],
    )


def solution(mesh):
    rows = P(("batch", "head"), None)
    whole = P()
    head = P("head")
    tiles = P(None, "batch", "head", None, None)
    kv_tiles = P(None, "head", None, None, None)
    in_specs = (
        rows,
        rows,
        P("batch", None),
        whole,
        whole,
        head,
        whole,
        head,
        P(None, "head"),
        whole,
        whole,
        P("head", None),
        P(None, "head"),
        P("head", None),
        *([tiles] * 8),
        *([kv_tiles] * 4),
        whole,
        head,
        whole,
        head,
    )
    out_specs = (
        rows,
        rows,
        *([whole] * 4),
        *([head] * 3),
        *([whole] * 3),
        *([head] * 3),
        *([tiles] * 8),
        *([kv_tiles] * 4),
    )
    return jax.shard_map(body, mesh=mesh, in_specs=in_specs, out_specs=out_specs, check_vma=False)
```

```python
from functools import partial
import math

import jax
import jax.numpy as jnp
from jax import lax
from jax.experimental import pallas as pl
from jax.experimental.pallas import tpu as pltpu
from jax.sharding import PartitionSpec as P

EPSILON = 1e-05
DECAY_RATE = 0.5
MATRIX_RATE = 0.01
VECTOR_RATE = 0.1
SAFE_ADD = 1e-08
PRECISE = lax.Precision.HIGHEST
LOG2E = math.log2(math.e)
MASKED = -1e30
TILE = 128
MESH = pl.DeviceIdType.MESH
BF16 = jnp.bfloat16
F32 = jnp.float32
VMEM_LIMIT = 60 * 1024 * 1024
ANY = pl.BlockSpec(memory_space=pl.ANY)
WHOLE = pl.BlockSpec(memory_space=pltpu.VMEM)


def matmul(first_op, second_op):
    return jnp.dot(first_op, second_op, preferred_element_type=F32)


def matmul_t(first_op, second_op):
    return lax.dot_general(
        first_op, second_op, (((0,), (0,)), ((), ())), preferred_element_type=F32
    )


def matmul_nt(first_op, second_op):
    return lax.dot_general(
        first_op, second_op, (((1,), (1,)), ((), ())), preferred_element_type=F32
    )


def norm_stats(rows_in):
    mean_row = jnp.mean(rows_in, axis=-1, keepdims=True)
    centered = rows_in - mean_row
    variance = jnp.mean(centered * centered, axis=-1, keepdims=True)
    inverse = lax.rsqrt(variance + EPSILON)
    return (centered * inverse, inverse)


def norm_back(grad_out, normed, inverse, gain):
    scaled = grad_out * gain
    mean_one = jnp.mean(scaled, axis=-1, keepdims=True)
    mean_two = jnp.mean(scaled * normed, axis=-1, keepdims=True)
    return inverse * (scaled - mean_one - normed * mean_two)


def lanes(start, size, unit):
    return pl.ds(pl.multiple_of(start, unit), size)


def greet(targets):
    barrier = pltpu.get_barrier_semaphore()
    for target in targets:
        pl.semaphore_signal(barrier, inc=1, device_id=target, device_id_type=MESH)
    pl.semaphore_wait(barrier, len(targets))


def gather_tools(batch_size, head_count):
    chips = head_count // 2
    b = lax.axis_index("batch")
    h = lax.axis_index("head")
    z = h // 2
    c = h % 2

    def at(chip):
        return {"head": chip * 2 + c}

    def peer(k):
        return {"batch": b ^ k}

    def remote(src, dst, send, recv, target):
        return pltpu.make_async_remote_copy(
            src_ref=src,
            dst_ref=dst,
            send_sem=send,
            recv_sem=recv,
            device_id=target,
            device_id_type=MESH,
        )

    others = [lax.rem(z + i, chips) for i in range(1, chips)]
    return b, h, z, c, {"head": h + 1 - 2 * c}, at, peer, remote, others


def plane_exchange(place, tools, sems, batch_size):
    b, _, _, _, sibling, _, peer, remote, others = tools
    xs, xr, fs, fr, cs, cr = sems
    ring = batch_size == 4
    direct = (1, 2) if ring else tuple(range(1, batch_size))

    def hop(k, chip):
        spot = place(b, chip)
        return remote(spot, spot, xs.at[k, chip], xr.at[k, chip], peer(k))

    def half(k, chip):
        spot = place(b ^ k, chip, k - 1)
        return remote(spot, spot, fs.at[k, chip], fr.at[k, chip], peer(3 - k))

    def side(k, chip):
        spot = place(b ^ k, chip)
        return remote(spot, spot, cs.at[k, chip], cr.at[k, chip], sibling)

    def start(chip):
        for k in direct:
            hop(k, chip).start()
        side(0, chip).start()

    def turn():
        for chip in others:
            for k in direct:
                hop(k, chip).wait_recv()
                if ring:
                    half(k, chip).start()
                side(k, chip).start()

    def close():
        if ring:
            for chip in others:
                for k in direct:
                    half(k, chip).wait_recv()
                side(3, chip).start()

    def finish():
        for chip in others:
            for k in range(batch_size):
                side(k, chip).wait()
            for k in direct:
                hop(k, chip).wait_send()
                if ring:
                    half(k, chip).wait_send()

    return start, turn, close, finish


def place_rows(w_all, rows, core, batch_size):
    def place(quarter, chip, half=None):
        part = rows // batch_size
        if half is not None:
            part = part // 2
            quarter = quarter * 2 + half
        return w_all.at[lanes((chip * 2 + core) * rows + quarter * part, part, part), :]

    return place


def gather_weights(w_query, w_out, bias_local, batch_size, head_count):
    rows, cols = w_query.shape
    chips = head_count // 2

    def kernel(
        q_ref, w_ref, bias_ref, q_all, w_all, bias_all, loc, right, left, line, ys, yr, sides_s,
        sides_r, xs, xr, fs, fr, cs, cr, bs, br,
    ):
        tools = gather_tools(batch_size, head_count)
        b, h, z, c, sibling, at, peer, remote, others = tools
        has_left = z > 0
        has_right = z < chips - 1

        def other(d):
            return {"head": lax.rem(h + d, head_count)}

        def place_query(quarter, chip, half=None):
            part = rows // batch_size
            if half is not None:
                part = part // 2
                quarter = quarter * 2 + half
            head = chip * 2 + c
            return q_all.at[lanes(quarter * part, part, part), lanes(head * cols, cols, cols)]

        places = (place_query, place_rows(w_all, cols, c, batch_size))
        greet([other(d) for d in range(1, head_count)] + [peer(k) for k in range(1, batch_size)])
        own = (q_all.at[:, lanes(h * cols, cols, cols)], w_all.at[lanes(h * cols, cols, cols), :])
        q_part, w_part = rows // batch_size, cols // batch_size
        mine = (
            q_ref.at[lanes(b * q_part, q_part, q_part), :],
            w_ref.at[lanes(b * w_part, w_part, w_part), :],
        )

        def z_copy(m, chip, to_right, src=None):
            spot = places[m](b, chip)
            src = spot if src is None else src
            if to_right:
                return remote(src, spot, right.at[m, chip], line.at[m, chip], at(z + 1))
            return remote(src, spot, left.at[m, chip], line.at[m, chip], at(z - 1))

        def z_first(m):
            @pl.when(has_right)
            def _():
                z_copy(m, z, True, mine[m]).start()

            @pl.when(has_left)
            def _():
                z_copy(m, z, False, mine[m]).start()

        def z_steps(m, d, then):
            @pl.when(z >= d)
            def _():
                z_copy(m, z - d, True).wait_recv()

                @pl.when(has_right)
                def _():
                    z_copy(m, z - d, True).start()

                then(z - d)

            @pl.when(z + d < chips)
            def _():
                z_copy(m, z + d, False).wait_recv()

                @pl.when(has_left)
                def _():
                    z_copy(m, z + d, False).start()

                then(z + d)

        z_first(0)
        locals_ = [
            pltpu.make_async_copy(src, own[m], loc.at[m]) for m, src in enumerate((q_ref, w_ref))
        ]
        slices = [
            remote(src, own[m], ys.at[m], yr.at[m], sibling) for m, src in enumerate((q_ref, w_ref))
        ]
        biases = [
            remote(bias_ref, bias_all.at[h], bs.at[d], br.at[d], other(d))
            for d in range(1, head_count)
        ]
        bias_own = pltpu.make_async_copy(bias_ref, bias_all.at[h], bs.at[0])
        for copy in locals_ + slices + biases + [bias_own]:
            copy.start()

        start, turn, close, finish = plane_exchange(
            place_query, tools, (xs, xr, fs, fr, cs, cr), batch_size
        )

        def side(chip):
            spot = places[1](b, chip)
            return remote(spot, spot, sides_s.at[chip], sides_r.at[chip], sibling)

        for d in range(1, chips):
            z_steps(0, d, start)
            if d == 1:
                z_first(1)
        turn()
        for d in range(1, chips):
            z_steps(1, d, lambda chip: side(chip).start())
        close()
        finish()
        for chip in others:
            side(chip).wait()
        for m in range(2):

            @pl.when(has_right)
            def _():
                z_copy(m, z, True, mine[m]).wait_send()

            @pl.when(has_left)
            def _():
                z_copy(m, z, False, mine[m]).wait_send()

            for d in range(1, chips):

                @pl.when((z >= d) & has_right)
                def _():
                    z_copy(m, z - d, True).wait_send()

                @pl.when((z + d < chips) & has_left)
                def _():
                    z_copy(m, z + d, False).wait_send()

        for copy in locals_ + slices + biases + [bias_own]:
            copy.wait()

    dma = pltpu.SemaphoreType.DMA
    hop = dma((batch_size, chips))
    two = dma((2, chips))
    return pl.pallas_call(
        kernel,
        out_shape=(
            jax.ShapeDtypeStruct((rows, cols * head_count), w_query.dtype),
            jax.ShapeDtypeStruct((cols * head_count, w_out.shape[1]), w_out.dtype),
            jax.ShapeDtypeStruct((head_count, 1, cols), F32),
        ),
        in_specs=[WHOLE] * 3,
        out_specs=(ANY,) * 3,
        scratch_shapes=[
            dma((2,)), two, two, two, dma((2,)), dma((2,)), dma((chips,)), dma((chips,)),
            hop, hop, hop, hop, hop, hop, dma((head_count,)), dma((head_count,)),
        ],
        compiler_params=pltpu.CompilerParams(collective_id=0, has_side_effects=True),
        cost_estimate=pl.CostEstimate(
            flops=0, bytes_accessed=120 * 1024 * 1024, transcendentals=0
        ),
        name="gather_weights",
    )(w_query, w_out, bias_local)


def gather_rest(w_all, kv_own, batch_size, head_count):
    chips = head_count // 2
    rows = w_all.shape[0] // head_count
    tok, kv_cols = kv_own.shape

    def kernel(
        in_ref, kv_ref, w_ref, kv_all, xs, xr, fs, fr, cs, cr, own_sem, zs, zr, ss, sr
    ):
        del in_ref
        tools = gather_tools(batch_size, head_count)
        _, h, z, c, sibling, at, peer, remote, others = tools
        greet([sibling] + [at(chip) for chip in others] + [peer(k) for k in range(1, batch_size)])

        def place(chip):
            return kv_all.at[lanes((chip * 2 + c) * tok, tok, tok), :]

        own = pltpu.make_async_copy(kv_ref, place(z), own_sem)
        own.start()

        def away(i):
            return remote(kv_ref, place(z), zs.at[i], zr.at[i], at(others[i]))

        def side(chip):
            src = kv_ref if chip is z else place(chip)
            return remote(src, place(chip), ss.at[chip], sr.at[chip], sibling)

        for i in range(chips - 1):
            away(i).start()
        side(z).start()
        start, turn, close, finish = plane_exchange(
            place_rows(w_ref, rows, c, batch_size), tools, (xs, xr, fs, fr, cs, cr), batch_size
        )
        for chip in others:
            start(chip)
        turn()
        for i in range(chips - 1):
            away(i).wait_recv()
            side(others[chips - 2 - i]).start()
        close()
        finish()
        side(z).wait()
        for i in range(chips - 1):
            side(others[i]).wait()
            away(i).wait_send()
        own.wait()

    dma = pltpu.SemaphoreType.DMA
    hop = dma((batch_size, chips))
    line = dma((chips,))
    return pl.pallas_call(
        kernel,
        out_shape=(
            jax.ShapeDtypeStruct(w_all.shape, w_all.dtype),
            jax.ShapeDtypeStruct((head_count * tok, kv_cols), kv_own.dtype),
        ),
        in_specs=[ANY, WHOLE],
        out_specs=(ANY, ANY),
        scratch_shapes=[hop] * 6 + [dma, line, line, line, line],
        input_output_aliases={0: 0},
        compiler_params=pltpu.CompilerParams(collective_id=5, has_side_effects=True),
        cost_estimate=pl.CostEstimate(
            flops=0, bytes_accessed=100 * 1024 * 1024, transcendentals=0
        ),
        name="gather_rest",
    )(w_all, kv_own)


def project_out(attended, weight, tokens, vectors):
    tok, width = attended.shape

    def kernel(att_ref, tok_ref, vec_ref, w_ref, resid_ref, mixer_ref, normed_ref, inverse_ref):
        resid = matmul(att_ref[...], w_ref[...]) + vec_ref[4:5, :] + tok_ref[...].astype(F32)
        normed, inverse = norm_stats(resid)
        resid_ref[...] = resid
        normed_ref[...] = normed
        inverse_ref[...] = jnp.broadcast_to(inverse, inverse_ref.shape)
        mixer_ref[...] = (normed * vec_ref[2:3, :] + vec_ref[3:4, :]).astype(BF16)

    return pl.pallas_call(
        kernel,
        out_shape=(
            jax.ShapeDtypeStruct((tok, width), F32),
            jax.ShapeDtypeStruct((tok, width), BF16),
            jax.ShapeDtypeStruct((tok, width), F32),
            jax.ShapeDtypeStruct((tok, TILE), F32),
        ),
        in_specs=[WHOLE] * 4,
        out_specs=(WHOLE,) * 4,
        compiler_params=pltpu.CompilerParams(vmem_limit_bytes=VMEM_LIMIT),
        cost_estimate=pl.CostEstimate(
            flops=2 * tok * width * width, bytes_accessed=14 * width * width, transcendentals=0
        ),
        name="project_out",
    )(attended, tokens, vectors, weight)


def mixer_pass(mixer_in, cot_all, w_up, w_down, bias_up, owner, batch_size, head_count, cuts):
    tok, width = mixer_in.shape
    hid = w_up.shape[1]
    n = head_count // 2
    sub = tok // cuts
    block = (n, 2, cuts, sub)
    tiles = width // TILE
    owned = tiles // batch_size
    total_events = n * cuts
    pieces = 2
    piece = sub // pieces

    def kernel(
        owner_ref, x_ref, cot_ref, up_ref, down_ref, bias_ref,
        all_ref, hid_ref, pre_ref, mix_a_ref, mix_b_ref, grad_up_ref, down_ref_all, out_ref,
        sum_ref,
        x_buf, cot_buf, hid_buf, pre_buf, mine, give, pair_in, chain_in, right_in,
        up_acc, down_acc, stage, grad_down_ref,
        own_sem, x_sem, cot_sem, hid_sem, pre_sem, mix_sem,
        right_send, left_send, side_send, side_recv, line_recv,
        pair_send, pair_recv, chain_send, chain_recv, last_recv, down_send, down_recv, down_sem,
    ):
        mix_refs = (mix_a_ref, mix_b_ref)
        h = lax.axis_index("head")
        z = h // 2
        c = h % 2
        has_left = z > 0
        has_right = z < n - 1

        def at(chip):
            return {"head": chip * 2 + c}

        sibling = {"head": h + 1 - 2 * c}

        def remote(src, dst, send, recv, target):
            return pltpu.make_async_remote_copy(
                src_ref=src, dst_ref=dst, send_sem=send, recv_sem=recv,
                device_id=target, device_id_type=MESH,
            )

        def row_copy(chip, g, way):
            spot = all_ref.at[chip, c, g]
            if way == 0:
                return remote(spot, spot, right_send.at[chip, g], line_recv.at[chip, g], at(z + 1))
            if way == 1:
                return remote(spot, spot, left_send.at[chip, g], line_recv.at[chip, g], at(z - 1))
            return remote(spot, spot, side_send.at[chip, g], side_recv.at[chip, g], sibling)

        def pair_copy(chip, g):
            return remote(
                give.at[chip, g], pair_in.at[chip, g], pair_send.at[chip, g],
                pair_recv.at[chip, g], sibling,
            )

        def chain_copy(chip, g, e, target):
            part = pl.ds(e * piece, piece)
            return remote(
                mine.at[chip, g, part], chain_in.at[chip, g, part], chain_send.at[chip, g, e],
                chain_recv.at[chip, g, e], at(target),
            )

        def last_copy(chip, g, e):
            part = pl.ds(e * piece, piece)
            return remote(
                mine.at[chip, g, part], right_in.at[g, part], chain_send.at[chip, g, e],
                last_recv.at[g, e], at(z - 1),
            )

        b = lax.axis_index("batch")

        def peer(k):
            return {"batch": b ^ k}

        def down_copy(k):
            return remote(
                grad_down_ref.at[pl.ds((b ^ k) * owned, owned)], down_ref_all.at[k],
                down_send.at[k], down_recv.at[k], peer(k),
            )

        def down_own():
            return pltpu.make_async_copy(
                grad_down_ref.at[pl.ds(b * owned, owned)], down_ref_all.at[0], down_sem
            )

        barrier = pltpu.get_barrier_semaphore()
        pl.semaphore_signal(barrier, inc=1, device_id=sibling, device_id_type=MESH)
        for k in range(1, batch_size):
            pl.semaphore_signal(barrier, inc=1, device_id=peer(k), device_id_type=MESH)

        @pl.when(has_left)
        def _():
            pl.semaphore_signal(barrier, inc=1, device_id=at(z - 1), device_id_type=MESH)

        @pl.when(has_right)
        def _():
            pl.semaphore_signal(barrier, inc=1, device_id=at(z + 1), device_id_type=MESH)

        own = pltpu.make_async_copy(x_ref, all_ref.at[z, c], own_sem)
        own.start()
        sum_ref[...] = jnp.zeros_like(sum_ref)
        up_acc[...] = jnp.zeros_like(up_acc)
        down_acc[...] = jnp.zeros_like(down_acc)
        pl.semaphore_wait(
            barrier, batch_size + has_left.astype(jnp.int32) + has_right.astype(jnp.int32)
        )
        own.wait()

        def pass_on(chip, g):
            @pl.when((chip <= z) & has_right)
            def _():
                row_copy(chip, g, 0).start()

            @pl.when((chip >= z) & has_left)
            def _():
                row_copy(chip, g, 1).start()

            row_copy(chip, g, 2).start()

        for g in range(cuts):
            pass_on(z, g)

        def compute(chip, g):
            cot_load = pltpu.make_async_copy(cot_ref.at[chip, :, g], cot_buf, cot_sem)
            cot_load.start()
            row_copy(chip, g, 2).wait_recv()
            x_load = pltpu.make_async_copy(all_ref.at[chip, :, g], x_buf, x_sem)
            x_load.start()
            cot_load.wait()
            grad_hidden = matmul_nt(cot_buf[...].reshape(2 * sub, width), down_ref[...])
            x_load.wait()
            pre_act = matmul(x_buf[...].reshape(2 * sub, width), up_ref[...]) + bias_ref[...]
            hidden, slope = gelu_pair(pre_act)
            hid_buf[...] = hidden.astype(BF16).reshape(2, sub, hid)
            hid_store = pltpu.make_async_copy(hid_buf, hid_ref.at[chip, :, g], hid_sem)
            hid_store.start()
            grad_pre = (grad_hidden * slope).astype(BF16)
            pre_buf[...] = grad_pre.reshape(2, sub, hid)
            pre_store = pltpu.make_async_copy(pre_buf, pre_ref.at[chip, :, g], pre_sem)
            pre_store.start()
            sum_ref[...] += jnp.sum(
                grad_pre.astype(F32).reshape(2 * sub // 8, 8, hid), axis=0
            )
            share = matmul_nt(grad_pre, up_ref[...]).astype(BF16).reshape(2, sub, width)

            @pl.when(c == 0)
            def _():
                mine[chip, g] = share[0]
                give[chip, g] = share[1]

            @pl.when(c == 1)
            def _():
                mine[chip, g] = share[1]
                give[chip, g] = share[0]

            pair_copy(chip, g).start()
            down_acc[...] += matmul_t(
                cot_buf[...].reshape(2 * sub, width), hid_buf[...].reshape(2 * sub, hid)
            ).reshape(tiles, TILE, hid)
            hid_store.wait()
            pre_store.wait()

        def nearest(i):
            edge = jnp.minimum(z, n - 1 - z)
            near = (i + 1) // 2
            inner = jnp.where(i % 2 == 1, z - near, z + near)
            far = i - edge
            outer = jnp.where(z < n - 1 - z, z + far, z - far)
            return jnp.where(i <= 2 * edge, inner, outer)

        def compute_rest(index):
            chip = nearest(index // cuts)
            g = index % cuts
            loads = [
                pltpu.make_async_copy(hid_ref.at[chip, :, g], hid_buf, hid_sem),
                pltpu.make_async_copy(all_ref.at[chip, :, g], x_buf, x_sem),
                pltpu.make_async_copy(pre_ref.at[chip, :, g], pre_buf, pre_sem),
            ]
            for load in loads:
                load.start()
            loads[0].wait()
            hidden = hid_buf[...].reshape(2 * sub, hid)
            stage[...] = matmul(hidden, down_ref[...]).astype(BF16).reshape(2, sub, width)
            for cut in range(cuts):

                @pl.when(g == cut)
                def _():
                    pltpu.make_async_copy(stage, mix_refs[cut].at[chip], mix_sem).start()

            loads[1].wait()
            loads[2].wait()
            up_acc[...] += matmul_t(
                x_buf[...].reshape(2 * sub, width), pre_buf[...].reshape(2 * sub, hid)
            ).reshape(tiles, TILE, hid)
            pltpu.make_async_copy(stage, mix_refs[0].at[chip], mix_sem).wait()

        def add_up(chip, g, e, more):
            part = pl.ds(e * piece, piece)
            total = mine[chip, g, part, :].astype(F32) + pair_in[chip, g, part, :].astype(F32)

            @pl.when(more)
            def _():
                chain_copy(chip, g, e, z).wait_recv()
                mine[chip, g, part, :] = (
                    total + chain_in[chip, g, part, :].astype(F32)
                ).astype(BF16)

            @pl.when(jnp.logical_not(more))
            def _():
                mine[chip, g, part, :] = total.astype(BF16)

        def step(t, carry):
            d = t // cuts
            g = t % cuts

            @pl.when((d > 0) & (z >= d))
            def _():
                row_copy(z - d, g, 0).wait_recv()
                pass_on(z - d, g)

            @pl.when((d > 0) & (z + d < n))
            def _():
                row_copy(z + d, g, 1).wait_recv()
                pass_on(z + d, g)

            def one_side(side, inner):
                chip = z + d * (2 * side - 1)

                @pl.when((chip >= 0) & (chip < n) & (d < n) & ((d > 0) | (side == 0)))
                def _():
                    compute(chip, g)

                return inner

            lax.fori_loop(0, 2, one_side, 0)

            @pl.when(t == (jnp.maximum(z, n - 1 - z) + 1) * cuts - 1)
            def _():
                def put_down(p, inner):
                    grad_down_ref[p] = down_acc[owner_ref[p]].astype(BF16)
                    return inner

                lax.fori_loop(0, tiles, put_down, 0)
                for k in range(1, batch_size):
                    down_copy(k).start()
                down_own().start()

            from_left = jnp.maximum(t - z, 0)
            chip_right = from_left // cuts
            g_right = from_left % cuts

            @pl.when((t >= z) & (chip_right > z) & (chip_right < n))
            def _():
                pair_copy(chip_right, g_right).wait_recv()
                for e in range(pieces):
                    add_up(chip_right, g_right, e, has_left)
                    chain_copy(chip_right, g_right, e, z + 1).start()

            from_right = jnp.maximum(t - (n - 1 - z), 0)
            chip_left = n - 1 - from_right // cuts
            g_left = from_right % cuts

            @pl.when((t >= n - 1 - z) & (chip_left < z) & (chip_left >= 0))
            def _():
                pair_copy(chip_left, g_left).wait_recv()
                for e in range(pieces):
                    add_up(chip_left, g_left, e, has_right)

                    @pl.when(chip_left == z - 1)
                    def _():
                        last_copy(chip_left, g_left, e).start()

                    @pl.when(chip_left < z - 1)
                    def _():
                        chain_copy(chip_left, g_left, e, z - 1).start()

            events = (z >= d).astype(jnp.int32) + (z + d < n).astype(jnp.int32)
            events = jnp.where((d == 0) | (d >= n), 1, events)
            ready = (events < 2) & (carry < total_events)

            @pl.when(ready)
            def _():
                compute_rest(carry)

            return carry + ready.astype(jnp.int32)

        done = lax.fori_loop(0, n * cuts + n - 1, step, 0)

        def left_over(index, carry):
            @pl.when(index >= done)
            def _():
                compute_rest(index)

            return carry

        lax.fori_loop(0, total_events, left_over, 0)

        def put_tile(p, carry):
            grad_up_ref[p] = up_acc[owner_ref[p]].astype(BF16)
            return carry

        lax.fori_loop(0, tiles, put_tile, 0)

        for g in range(cuts):
            pair_copy(z, g).wait_recv()
            out_ref[g] = mine[z, g].astype(F32) + pair_in[z, g].astype(F32)

            @pl.when(has_left)
            def _():
                for e in range(pieces):
                    chain_copy(z, g, e, z).wait_recv()
                out_ref[g] += chain_in[z, g].astype(F32)

            @pl.when(has_right)
            def _():
                for e in range(pieces):
                    last_copy(z, g, e).wait_recv()
                out_ref[g] += right_in[g].astype(F32)

        def finish(chip, carry):
            for g in range(cuts):

                @pl.when((chip <= z) & has_right)
                def _():
                    row_copy(chip, g, 0).wait_send()

                @pl.when((chip >= z) & has_left)
                def _():
                    row_copy(chip, g, 1).wait_send()

                row_copy(chip, g, 2).wait_send()
                pair_copy(chip, g).wait_send()

                @pl.when(chip != z)
                def _():
                    for e in range(pieces):
                        chain_copy(chip, g, e, z).wait_send()

            return carry

        lax.fori_loop(0, n, finish, 0)
        for k in range(1, batch_size):
            down_copy(k).wait()
        down_own().wait()

    dma = pltpu.SemaphoreType.DMA
    vm = pltpu.VMEM
    each = dma((n, cuts))
    shares = vm((n, cuts, sub, width), BF16)
    outs = pl.pallas_call(
        kernel,
        out_shape=(
            jax.ShapeDtypeStruct(block + (width,), BF16),
            jax.ShapeDtypeStruct(block + (hid,), BF16),
            jax.ShapeDtypeStruct(block + (hid,), BF16),
            jax.ShapeDtypeStruct((n, 2, sub, width), BF16),
            jax.ShapeDtypeStruct((n, 2, sub, width), BF16),
            jax.ShapeDtypeStruct((tiles, TILE, hid), BF16),
            jax.ShapeDtypeStruct((batch_size, owned, TILE, hid), BF16),
            jax.ShapeDtypeStruct((cuts, sub, width), F32),
            jax.ShapeDtypeStruct((8, hid), F32),
        ),
        in_specs=[pl.BlockSpec(memory_space=pltpu.SMEM), WHOLE, ANY, WHOLE, WHOLE, WHOLE],
        out_specs=(ANY, ANY, ANY, ANY, ANY, WHOLE, ANY, WHOLE, WHOLE),
        scratch_shapes=[
            vm((2, sub, width), BF16),
            vm((2, sub, width), BF16),
            vm((2, sub, hid), BF16),
            vm((2, sub, hid), BF16),
            shares, shares, shares, shares,
            vm((cuts, sub, width), BF16),
            vm((tiles, TILE, hid), F32),
            vm((tiles, TILE, hid), F32),
            vm((2, sub, width), BF16),
            vm((tiles, TILE, hid), BF16),
            dma, dma, dma, dma, dma, dma,
            each, each, each, each, each,
            each, each, dma((n, cuts, pieces)), dma((n, cuts, pieces)),
            dma((cuts, pieces)),
            dma((batch_size,)), dma((batch_size,)), dma,
        ],
        compiler_params=pltpu.CompilerParams(
            collective_id=3, has_side_effects=True, vmem_limit_bytes=VMEM_LIMIT
        ),
        cost_estimate=pl.CostEstimate(
            flops=12 * n * 2 * tok * width * hid, bytes_accessed=300 * 1024 * 1024, transcendentals=0
        ),
        name="mixer_pass",
    )(
        owner,
        mixer_in.reshape(cuts, sub, width),
        cot_all.reshape(block + (width,)),
        w_up,
        w_down,
        bias_up.reshape(1, hid),
    )
    _, _, _, mix_a, mix_b, grad_up, grad_down, grad_in, bias_sum = outs
    return (
        mix_a.reshape(2 * n * sub, width),
        mix_b.reshape(2 * n * sub, width),
        grad_up.reshape(batch_size, owned * TILE, hid),
        grad_down.reshape(batch_size, owned * TILE, hid),
        grad_in.reshape(tok, width),
        jnp.sum(bias_sum, axis=0),
    )


def attention_forward(queries, kv_all, mask, slabs):
    tok, width = queries.shape
    seq_len, head_size = kv_all.shape[0], kv_all.shape[1] // 2
    slab = width // slabs
    heads = slab // head_size
    scale = LOG2E / math.sqrt(head_size)

    def kernel(q_ref, k_ref, v_ref, mask_ref, o_ref, log_ref, turned):
        @pl.when(pl.program_id(0) == 0)
        def _():
            turned[...] = v_ref[...].astype(F32).T.astype(BF16)

        for j in range(heads):
            spot = slice(j * head_size, (j + 1) * head_size)
            scores = matmul_nt(k_ref[...], q_ref[:, spot]) * scale + mask_ref[...]
            highest = jnp.max(scores, axis=0, keepdims=True)
            raised = jnp.exp2(scores - highest)
            total = jnp.sum(raised, axis=0, keepdims=True)
            out = matmul(turned[...], raised.astype(BF16)) / total
            o_ref[:, spot] = out.T.astype(BF16)
            log_ref[0, j : j + 1, :] = highest + jnp.log2(total)

    return pl.pallas_call(
        kernel,
        grid=(slabs,),
        out_shape=(
            jax.ShapeDtypeStruct((tok, width), BF16),
            jax.ShapeDtypeStruct((slabs, heads, tok), F32),
        ),
        in_specs=[
            pl.BlockSpec((tok, slab), lambda i: (0, i)),
            pl.BlockSpec((seq_len, head_size), lambda i: (0, 0)),
            pl.BlockSpec((seq_len, head_size), lambda i: (0, 1)),
            pl.BlockSpec((seq_len, tok), lambda i: (0, 0)),
        ],
        out_specs=(
            pl.BlockSpec((tok, slab), lambda i: (0, i)),
            pl.BlockSpec((1, heads, tok), lambda i: (i, 0, 0)),
        ),
        scratch_shapes=[pltpu.VMEM((head_size, seq_len), BF16)],
        compiler_params=pltpu.CompilerParams(vmem_limit_bytes=VMEM_LIMIT),
        cost_estimate=pl.CostEstimate(
            flops=8 * tok * seq_len * width,
            bytes_accessed=4 * tok * width,
            transcendentals=tok * seq_len * slabs * heads,
        ),
        name="attention_forward",
    )(queries, kv_all, kv_all, mask)


def backward_pass(
    owner, grad_mixer, cotangent, tokens, normed_two, inverse_two, vectors, queries, attended,
    log_totals, kv_all, mask, w_query_all, w_out_all, w_kv, up_parts,
    batch_size, head_count,
):
    tok, width = tokens.shape
    seq_len, head_size = kv_all.shape[0], kv_all.shape[1] // 2
    slab = width // head_count
    heads = slab // head_size
    n = head_count // 2
    tiles = width // TILE
    cols_out = width // batch_size
    half_rows = slab // 2
    kv_cols = 2 * head_size
    kv_rows = width // head_count // batch_size
    ring = batch_size == 4
    scale = LOG2E / math.sqrt(head_size)
    plain_scale = 1.0 / math.sqrt(head_size)
    block = 512 if seq_len % 512 == 0 else seq_len

    def kernel(
        owner_ref, gm_ref, cot_ref, tok_ref, n2_ref, i2_ref, vec_ref, q_ref, att_ref, log_ref,
        keys_ref, mask_ref, wq_ref, wo_ref, wkv_ref, up_ref,
        tokens_out, query_out, out_out, kv_out, vec_out, up_out,
        branch, kt_ref, wide_tiles, normed_owned, branch_owned, grad_in, wq_buf, wo_buf, dk, dv,
        give, mine, pair_in, land, hop, z_land,
        dkv, dkv_pair, dkv_here, dkv_land,
        kv_part, kv_pair, kv_sum, kv_land, kv_half, kv_zland,
        vec_part, vec_land, vec_sum, vec_bland, up_land,
        gm_sem, n2_sem, cot_sem, free_sem, wq_sem, wo_sem, pair_send, pair_recv, hop_send, hop_recv, land_send, land_recv,
        z_send, z_recv, dkv_s, dkv_r, dkz_s, dkz_r,
        s_pair, r_pair, s_kvb, r_kvb, s_kvz, r_kvz, s_kva, r_kva,
        s_vh, r_vh, s_vb, r_vb, s_va, r_va, s_up, r_up,
    ):
        b = lax.axis_index("batch")
        h = lax.axis_index("head")
        z = h // 2
        c = h % 2
        sibling = {"head": h + 1 - 2 * c}

        def at_chip(r):
            return {"head": lax.rem(z + r, n) * 2 + c}

        def other(d):
            return {"head": lax.rem(h + d, head_count)}

        def peer(k):
            return {"batch": b ^ k}

        def remote(src, dst, send, recv, target):
            return pltpu.make_async_remote_copy(
                src_ref=src, dst_ref=dst, send_sem=send, recv_sem=recv,
                device_id=target, device_id_type=MESH,
            )

        greet([other(d) for d in range(1, head_count)] + [peer(k) for k in range(1, batch_size)])

        up_copies = [
            remote(up_ref, up_land.at[k], s_up.at[k], r_up.at[k], peer(k))
            for k in range(1, batch_size)
        ]
        for copy in up_copies:
            copy.start()

        def slab_at(s):
            chip = lax.rem(z + 1 + s // 2, n)
            return chip * 2 + jnp.where(s % 2 == 0, 1 - c, c)

        def weight_loads(s):
            i = slab_at(s)
            return (
                pltpu.make_async_copy(
                    wq_ref.at[:, lanes(i * slab, slab, slab)], wq_buf, wq_sem
                ),
                pltpu.make_async_copy(
                    wo_ref.at[lanes(i * slab, slab, slab), :], wo_buf, wo_sem
                ),
            )

        norm_loads = (
            pltpu.make_async_copy(gm_ref, tokens_out, gm_sem),
            pltpu.make_async_copy(n2_ref, grad_in, n2_sem),
            pltpu.make_async_copy(cot_ref, branch, cot_sem),
        )
        for load in norm_loads + weight_loads(0):
            load.start()

        def put_vector(row, value):
            for i in range(head_count):
                vec_part[i, row : row + 1, :] = value[:, i * slab : (i + 1) * slab]

        def column_sum(value):
            return jnp.sum(value, axis=0, keepdims=True)

        for load in norm_loads:
            load.wait()
        grad_mix = tokens_out[...]
        normed_two_rows = grad_in[...]
        grad_out_rows = branch[...].astype(F32)
        put_vector(5, column_sum(grad_out_rows))
        grad_resid = grad_out_rows + norm_back(
            grad_mix, normed_two_rows, i2_ref[:, :1], vec_ref[2:3, :]
        )
        put_vector(2, column_sum(grad_mix * normed_two_rows))
        put_vector(3, column_sum(grad_mix))
        tokens_out[...] = grad_resid
        grad_branch = grad_resid.astype(BF16)
        branch[...] = grad_branch

        put_vector(4, column_sum(grad_branch.astype(F32)))

        for p in range(tiles):
            wide_tiles[p] = branch[:, p * TILE : (p + 1) * TILE]

        for p in range(tiles):
            branch_owned[:, p * TILE : (p + 1) * TILE] = wide_tiles[owner_ref[p]]
        normed_one, inverse_one = norm_stats(tok_ref[...].astype(F32))
        normed_in = (normed_one * vec_ref[0:1, :] + vec_ref[1:2, :]).astype(BF16)
        for p in range(tiles):
            wide_tiles[p] = normed_in[:, p * TILE : (p + 1) * TILE]

        for p in range(tiles):
            normed_owned[:, p * TILE : (p + 1) * TILE] = wide_tiles[owner_ref[p]]
        kt_ref[...] = keys_ref[:, :head_size].astype(F32).T.astype(BF16)
        dk[...] = jnp.zeros_like(dk)
        dv[...] = jnp.zeros_like(dv)
        grad_in[...] = jnp.zeros_like(grad_in)

        def pair_copy(q):
            return remote(
                give.at[q % 2], pair_in.at[q % 2], pair_send.at[q], pair_recv.at[q], sibling
            )

        halves = (pl.ds(0, half_rows), pl.ds(half_rows, half_rows))

        def hop_copy(q, k):
            part = halves[1 if k == 1 else 0]
            return remote(
                mine.at[q, b ^ 3, part], hop.at[q, k - 1], hop_send.at[q, k], hop_recv.at[q, k],
                peer(k),
            )

        def land_copy(q, k, which):
            if which is None:
                return remote(
                    mine.at[q, b ^ k], land.at[q, k - 1], land_send.at[q, k, 0],
                    land_recv.at[q, k, 0], peer(k),
                )
            part = halves[which]
            return remote(
                mine.at[q, b ^ k, part], land.at[q, k - 1, part], land_send.at[q, k, which],
                land_recv.at[q, k, which], peer(k),
            )

        def z_copy(q):
            return remote(
                mine.at[q, b], z_land.at[q], z_send.at[q], z_recv.at[q], at_chip(q % n + 1)
            )

        def pair_start(q, value):
            @pl.when(q >= 2)
            def _():
                pair_copy(q - 2).wait_send()
                pl.semaphore_wait(free_sem, 1)

            for k in range(batch_size):
                give[q % 2, k] = value[:, k * cols_out : (k + 1) * cols_out]
            pair_copy(q).start()

        def plane_start(q):
            pair_copy(q).wait_recv()
            mine[q] = (mine[q].astype(F32) + pair_in[q % 2].astype(F32)).astype(BF16)

            @pl.when(q < 2 * n - 2)
            def _():
                pl.semaphore_signal(free_sem, inc=1, device_id=sibling, device_id_type=MESH)

            if ring:
                hop_copy(q, 1).start()
                hop_copy(q, 2).start()
                land_copy(q, 1, 1).start()
                land_copy(q, 2, 0).start()
            else:
                for k in range(1, batch_size):
                    land_copy(q, k, None).start()

        def plane_hop(q):
            if not ring:
                return
            for k in (1, 2):
                hop_copy(q, 3 - k).wait_recv()
                which = 0 if k == 1 else 1
                part = halves[which]
                mine[q, b ^ k, part, :] = (
                    mine[q, b ^ k, part, :].astype(F32) + hop[q, 2 - k].astype(F32)
                ).astype(BF16)
                land_copy(q, k, which).start()

        def plane_end(q):
            total = mine[q, b].astype(F32)
            for k in range(1, 3 if ring else batch_size):
                for which in (0, 1) if ring else (None,):
                    land_copy(q, k, which).wait_recv()
                total += land[q, k - 1].astype(F32)
            mine[q, b] = total.astype(BF16)

            @pl.when(q % n < n - 1)
            def _():
                z_copy(q).start()

        def out_gradient(i):
            att = att_ref[:, lanes(i * slab, slab, slab)]
            return matmul(att.astype(F32).T.astype(BF16), branch_owned[...]).astype(BF16)

        def put_mine(q, value):
            for k in range(batch_size):
                mine[q, k] = value[:, k * cols_out : (k + 1) * cols_out]

        def out_pairs(j, carry):
            pair_start(j, out_gradient(slab_at(2 * j)))
            put_mine(j, out_gradient(slab_at(2 * j + 1)))

            @pl.when(j >= 1)
            def _():
                plane_start(j - 1)

            return carry

        lax.fori_loop(0, n, out_pairs, 0)
        plane_start(n - 1)

        def work(s, carry):
            j = s // 2
            i = slab_at(s)
            cols = lanes(i * slab, slab, slab)

            loads = weight_loads(s)
            loads[1].wait()
            grad_att = matmul_nt(branch[...], wo_buf[...]).astype(BF16)

            @pl.when(s + 1 < head_count)
            def _():
                weight_loads(s + 1)[1].start()

            queries_here = q_ref[:, cols]
            att_here = att_ref[:, cols]
            logs_here = log_ref[i]
            parts = []
            for e in range(heads):
                spot = slice(e * head_size, (e + 1) * head_size)
                query = queries_here[:, spot]
                grad = grad_att[:, spot]
                joint = grad.astype(F32) * att_here[:, spot].astype(F32)
                delta = jnp.sum(joint.T, axis=0, keepdims=True)
                logs = logs_here[e : e + 1, :]
                total = jnp.zeros((head_size, tok), F32)
                for start in range(0, seq_len, block):
                    part = slice(start, start + block)
                    scores = matmul_nt(keys_ref[part, :head_size], query) * scale
                    probs = jnp.exp2(scores + (mask_ref[part, :].astype(F32) - logs))
                    grad_probs = matmul_nt(keys_ref[part, head_size:], grad)
                    grad_scores = (probs * (grad_probs - delta)).astype(BF16)
                    dv[part, :] += matmul(probs.astype(BF16), grad)
                    dk[part, :] += matmul(grad_scores, query)
                    total += matmul(kt_ref[:, part], grad_scores)
                parts.append(total * plain_scale)
            turned = jnp.concatenate(parts, axis=0) if heads > 1 else parts[0]
            grad_q = turned.T.astype(BF16)
            vec_part[i, 6:7, :] = column_sum(grad_q.astype(F32))
            grad_query = matmul(turned.astype(BF16), normed_owned[...]).astype(BF16)

            @pl.when(s % 2 == 0)
            def _():
                pair_start(n + j, grad_query)

            @pl.when(s % 2 == 1)
            def _():
                put_mine(n + j, grad_query)

            loads[0].wait()
            grad_in[...] += matmul_nt(grad_q, wq_buf[...])

            @pl.when(s + 1 < head_count)
            def _():
                weight_loads(s + 1)[0].start()

            @pl.when(s < n)
            def _():
                plane_hop(s)

            @pl.when((s >= 2) & (s < n + 2))
            def _():
                plane_end(s - 2)

            @pl.when(s % 2 == 1)
            def _():
                plane_start(n + j)

                @pl.when(j >= 1)
                def _():
                    plane_hop(n + j - 1)

                @pl.when(j >= 2)
                def _():
                    plane_end(n + j - 2)

            return carry

        lax.fori_loop(0, head_count, work, 0)

        dkv[:, :, :, :head_size] = (dk[...] * plain_scale).astype(BF16).reshape(n, 2, tok, head_size)
        dkv[:, :, :, head_size:] = dv[...].astype(BF16).reshape(n, 2, tok, head_size)
        dkv_swap = remote(dkv.at[:, 1 - c], dkv_pair, dkv_s, dkv_r, sibling)
        dkv_swap.start()
        dkv_swap.wait_recv()
        for r in range(n):
            dkv_here[r] = (dkv[r, c].astype(F32) + dkv_pair[r].astype(F32)).astype(BF16)
        dkv_copies = [
            remote(
                dkv_here.at[lax.rem(z + r, n)], dkv_land.at[r], dkz_s.at[r], dkz_r.at[r],
                at_chip(r),
            )
            for r in range(1, n)
        ]
        for copy in dkv_copies:
            copy.start()
        normed_one, inverse_one = norm_stats(tok_ref[...].astype(F32))
        normed_in = (normed_one * vec_ref[0:1, :] + vec_ref[1:2, :]).astype(BF16)
        plane_hop(2 * n - 1)
        grad_kv = dkv_here[z].astype(F32)
        for copy in dkv_copies:
            copy.wait_recv()
        for r in range(1, n):
            grad_kv += dkv_land[r].astype(F32)
        grad_kv = grad_kv.astype(BF16)

        kv_part[...] = (
            matmul_t(normed_in, grad_kv)
            .astype(BF16)
            .reshape(n, 2, batch_size, kv_rows, kv_cols)
        )
        pair_kv = remote(kv_part.at[:, 1 - c], kv_pair, s_pair, r_pair, sibling)
        pair_kv.start()

        grad_normed = grad_in[...] + matmul_nt(grad_kv, wkv_ref[...])
        pair_kv.wait_recv()
        for r in range(n):
            kv_sum[r] = (kv_part[r, c].astype(F32) + kv_pair[r].astype(F32)).astype(BF16)
        kv_copies = [
            remote(kv_sum.at[:, b ^ k], kv_land.at[k], s_kvb.at[k], r_kvb.at[k], peer(k))
            for k in range(1, batch_size)
        ]
        for copy in kv_copies:
            copy.start()
        put_vector(0, column_sum(grad_normed * normed_one))
        put_vector(1, column_sum(grad_normed))
        for i in range(head_count):
            vec_part[i, 7:8, :] = jnp.zeros((1, slab), F32)
        vec_part[0, 7:8, :head_size] = column_sum(grad_kv[:, head_size:].astype(F32))
        vec_copies = [
            remote(
                vec_part.at[lax.rem(h + d, head_count)], vec_land.at[d], s_vh.at[d], r_vh.at[d],
                other(d),
            )
            for d in range(1, head_count)
        ]
        for copy in vec_copies:
            copy.start()
        tokens_out[...] += norm_back(grad_normed, normed_one, inverse_one, vec_ref[0:1, :])
        total = vec_part[h]
        for copy in vec_copies:
            copy.wait_recv()
        for d in range(1, head_count):
            total += vec_land[d]
        vec_sum[...] = total
        vec_bcopies = [
            remote(vec_sum, vec_bland.at[k], s_vb.at[k], r_vb.at[k], peer(k))
            for k in range(1, batch_size)
        ]
        for copy in vec_bcopies:
            copy.start()
        up_total = up_ref[...]
        for copy in up_copies:
            copy.wait_recv()
        for k in range(1, batch_size):
            up_total += up_land[k]
        up_out[...] = up_total
        for copy in kv_copies:
            copy.wait_recv()
        kv_total = kv_sum[:, b].astype(F32)
        for k in range(1, batch_size):
            kv_total += kv_land[k].astype(F32)
        kv_half[...] = kv_total.astype(BF16)
        kv_zcopies = [
            remote(
                kv_half.at[lax.rem(z + r, n)], kv_zland.at[r], s_kvz.at[r], r_kvz.at[r], at_chip(r)
            )
            for r in range(1, n)
        ]
        for copy in kv_zcopies:
            copy.start()
        for copy in vec_bcopies:
            copy.wait_recv()
        total = vec_sum[...]
        for k in range(1, batch_size):
            total += vec_bland[k]
        vec_out[h] = total
        vec_acopies = [
            remote(vec_out.at[h], vec_out.at[h], s_va.at[d], r_va.at[d], other(d))
            for d in range(1, head_count)
        ]
        for copy in vec_acopies:
            copy.start()
        for copy in kv_zcopies:
            copy.wait_recv()
        kv_mine = kv_half[z].astype(F32)
        for r in range(1, n):
            kv_mine += kv_zland[r].astype(F32)
        kv_out[b] = kv_mine
        kv_acopies = [
            remote(kv_out.at[b], kv_out.at[b], s_kva.at[k], r_kva.at[k], peer(k))
            for k in range(1, batch_size)
        ]
        for copy in kv_acopies:
            copy.start()

        plane_end(2 * n - 2)
        plane_end(2 * n - 1)
        for first, target in ((0, out_out), (n, query_out)):
            total = mine[first + n - 1, b].astype(F32)
            for r in range(n - 1):
                z_copy(first + r).wait_recv()
                total += z_land[first + r].astype(F32)
            target[0] = total.astype(BF16)
        for copy in vec_acopies + kv_acopies:
            copy.wait_recv()

        for copy in up_copies + [dkv_swap, pair_kv] + dkv_copies + vec_copies + kv_copies:
            copy.wait_send()
        for copy in vec_bcopies + kv_zcopies + vec_acopies + kv_acopies:
            copy.wait_send()
        pair_copy(2 * n - 2).wait_send()
        pair_copy(2 * n - 1).wait_send()

        def finish(q, carry):
            @pl.when(q % n < n - 1)
            def _():
                z_copy(q).wait_send()

            if ring:
                for k in (1, 2):
                    hop_copy(q, k).wait_send()
                    for which in (0, 1):
                        land_copy(q, k, which).wait_send()
            else:
                for k in range(1, batch_size):
                    land_copy(q, k, None).wait_send()
            return carry

        lax.fori_loop(0, 2 * n, finish, 0)

    dma = pltpu.SemaphoreType.DMA
    vm = pltpu.VMEM
    nb, nh = batch_size, head_count
    lands = 2 if ring else nb - 1
    shared = (nb, slab, cols_out)
    return pl.pallas_call(
        kernel,
        out_shape=(
            jax.ShapeDtypeStruct((tok, width), F32),
            jax.ShapeDtypeStruct((1, slab, cols_out), BF16),
            jax.ShapeDtypeStruct((1, slab, cols_out), BF16),
            jax.ShapeDtypeStruct((nb, kv_rows, kv_cols), F32),
            jax.ShapeDtypeStruct((nh, 8, slab), F32),
            jax.ShapeDtypeStruct(up_parts.shape, F32),
        ),
        in_specs=[pl.BlockSpec(memory_space=pltpu.SMEM), ANY, ANY, WHOLE, ANY]
        + [WHOLE] * 7
        + [ANY, ANY, WHOLE, WHOLE],
        out_specs=(WHOLE,) * 6,
        scratch_shapes=[
            vm((tok, width), BF16),
            vm((head_size, seq_len), BF16),
            vm((tiles, tok, TILE), BF16),
            vm((tok, width), BF16),
            vm((tok, width), BF16),
            vm((tok, width), F32),
            vm((width, slab), BF16),
            vm((slab, width), BF16),
            vm((seq_len, head_size), F32),
            vm((seq_len, head_size), F32),
            vm((2,) + shared, BF16),
            vm((2 * n,) + shared, BF16),
            vm((2,) + shared, BF16),
            vm((2 * n, lands, slab, cols_out), BF16),
            vm((2 * n, 2, half_rows, cols_out) if ring else (1, 1, 16, TILE), BF16),
            vm((2 * n, slab, cols_out), BF16),
            vm((n, 2, tok, kv_cols), BF16),
            vm((n, tok, kv_cols), BF16),
            vm((n, tok, kv_cols), BF16),
            vm((n, tok, kv_cols), BF16),
            vm((n, 2, nb, kv_rows, kv_cols), BF16),
            vm((n, nb, kv_rows, kv_cols), BF16),
            vm((n, nb, kv_rows, kv_cols), BF16),
            vm((nb, n, kv_rows, kv_cols), BF16),
            vm((n, kv_rows, kv_cols), BF16),
            vm((n, kv_rows, kv_cols), BF16),
            vm((nh, 8, slab), F32),
            vm((nh, 8, slab), F32),
            vm((8, slab), F32),
            vm((nb, 8, slab), F32),
            vm((nb,) + up_parts.shape, F32),
            dma, dma, dma, pltpu.SemaphoreType.REGULAR, dma, dma,
            dma((2 * n,)), dma((2 * n,)), dma((2 * n, 3)), dma((2 * n, 3)),
            dma((2 * n, nb, 2)), dma((2 * n, nb, 2)), dma((2 * n,)), dma((2 * n,)), dma, dma, dma((n,)), dma((n,)),
            dma, dma, dma((nb,)), dma((nb,)), dma((n,)), dma((n,)), dma((nb,)), dma((nb,)),
            dma((nh,)), dma((nh,)), dma((nb,)), dma((nb,)), dma((nh,)), dma((nh,)),
            dma((nb,)), dma((nb,)),
        ],
        compiler_params=pltpu.CompilerParams(
            collective_id=4, has_side_effects=True, vmem_limit_bytes=VMEM_LIMIT + 2 * 1024 * 1024
        ),
        cost_estimate=pl.CostEstimate(
            flops=20 * tok * seq_len * width + 8 * tok * width * width,
            bytes_accessed=200 * 1024 * 1024,
            transcendentals=tok * seq_len * width // head_size,
        ),
        name="backward_pass",
    )(
        owner, grad_mixer, cotangent, tokens, normed_two, inverse_two, vectors, queries, attended,
        log_totals, kv_all, mask, w_query_all, w_out_all, w_kv, up_parts,
    )


def split_high(value):
    high = value.astype(BF16)
    return high, (value - high.astype(F32)).astype(BF16)


def matmul_three(first_op, second_op):
    first_high, first_low = split_high(first_op)
    second_high, second_low = split_high(second_op)
    return (
        matmul(first_high, second_high)
        + matmul(first_high, second_low)
        + matmul(first_low, second_high)
    )


def shampoo(
    first, second, first_weight, second_weight, owned, left, right, root_left, root_right, wide_rows,
    per_step,
):
    _, owned_count, columns, _, _ = left.shape

    steps = owned_count // per_step

    def kernel(ids_ref, *refs):
        del ids_ref
        one, two = refs[:2]
        w_one, w_two = refs[2 : 2 + per_step], refs[2 + per_step : 2 + 2 * per_step]
        l_ref, r_ref, p_ref, q_ref, g_out, l_out, r_out, w_out = refs[2 + 2 * per_step :]

        def update(turned):
            shares = two if turned else one
            tiles = [(p, t) for p in range(per_step) for t in range(columns)]
            group = 4 if len(tiles) % 4 == 0 else 1
            for first in range(0, len(tiles), group):
                here = tiles[first : first + group]
                grads = []
                for p, t in here:
                    wide = slice(p * TILE, (p + 1) * TILE)
                    spot = slice(t * TILE, (t + 1) * TILE)
                    part = (wide, spot) if wide_rows else (spot, wide)
                    grad = shares[(0,) + part].astype(F32)
                    for i in range(1, shares.shape[0]):
                        grad += shares[(i,) + part].astype(F32)
                    grads.append(grad.T if turned == wide_rows else grad)
                highs = [grad.astype(BF16) for grad in grads]
                halfway = [matmul_three(p_ref[0, p, t], g) for (p, t), g in zip(here, grads)]
                lefts = [matmul_nt(high, high) for high in highs]
                steps_here = [matmul_three(m, q_ref[0, p, t]) for (p, t), m in zip(here, halfway)]
                rights = [matmul_t(high, high) for high in highs]
                for i, (p, t) in enumerate(here):
                    spot = slice(t * TILE, (t + 1) * TILE)
                    weight = w_two[p][spot, :] if turned else w_one[p][:, spot]
                    g_out[0, p, t] = grads[i]
                    l_out[0, p, t] = (
                        DECAY_RATE * l_ref[0, p, t] + (1.0 - DECAY_RATE) * lefts[i]
                    )
                    r_out[0, p, t] = (
                        DECAY_RATE * r_ref[0, p, t] + (1.0 - DECAY_RATE) * rights[i]
                    )
                    w_out[0, p, t] = weight.astype(F32) - MATRIX_RATE * steps_here[i]

        @pl.when(pl.program_id(0) == 0)
        def _():
            update(False)

        @pl.when(pl.program_id(0) == 1)
        def _():
            update(True)

    last = steps - 1

    def place_one(m, i):
        return jnp.where(m == 0, i, last)

    def place_two(m, i):
        return jnp.where(m == 1, i, 0)

    def share(array, place):
        if wide_rows:
            return pl.BlockSpec(
                (array.shape[0], per_step * TILE, columns * TILE),
                lambda m, i, ids: (0, place(m, i), 0),
            )
        return pl.BlockSpec(
            (array.shape[0], columns * TILE, per_step * TILE),
            lambda m, i, ids: (0, 0, place(m, i)),
        )

    def weight_one(p):
        return pl.BlockSpec(
            (TILE, columns * TILE), lambda m, i, ids: (ids[place_one(m, i) * per_step + p], 0)
        )

    def weight_two(p):
        return pl.BlockSpec(
            (columns * TILE, TILE), lambda m, i, ids: (0, ids[place_two(m, i) * per_step + p])
        )

    stat = pl.BlockSpec((1, per_step, columns, TILE, TILE), lambda m, i, ids: (m, i, 0, 0, 0))
    shape = jax.ShapeDtypeStruct(left.shape, F32)
    return pl.pallas_call(
        kernel,
        grid_spec=pltpu.PrefetchScalarGridSpec(
            num_scalar_prefetch=1,
            grid=(2, steps),
            in_specs=[share(first, place_one), share(second, place_two)]
            + [weight_one(p) for p in range(per_step)]
            + [weight_two(p) for p in range(per_step)]
            + [stat] * 4,
            out_specs=[stat] * 4,
        ),
        out_shape=[shape] * 4,
        compiler_params=pltpu.CompilerParams(vmem_limit_bytes=VMEM_LIMIT),
        cost_estimate=pl.CostEstimate(
            flops=left.size * TILE * 16, bytes_accessed=left.size * 40, transcendentals=0
        ),
        name="shampoo",
    )(
        owned,
        first,
        second,
        *([first_weight] * per_step),
        *([second_weight] * per_step),
        left,
        right,
        root_left,
        root_right,
    )


def shampoo_update(grad_tiles, left_old, right_old, root_left, root_right, weight_tiles):
    outer_left = jnp.einsum("...ij,...kj->...ik", grad_tiles, grad_tiles, precision=PRECISE)
    outer_right = jnp.einsum("...ji,...jk->...ik", grad_tiles, grad_tiles, precision=PRECISE)
    left_new = DECAY_RATE * left_old + (1.0 - DECAY_RATE) * outer_left
    right_new = DECAY_RATE * right_old + (1.0 - DECAY_RATE) * outer_right
    stepped = jnp.einsum("...ij,...jk->...ik", root_left, grad_tiles, precision=PRECISE)
    stepped = jnp.einsum("...ij,...jk->...ik", stepped, root_right, precision=PRECISE)
    return (grad_tiles, left_new, right_new, weight_tiles - MATRIX_RATE * stepped)


def diagonal_update(gradient, second, current):
    second_new = DECAY_RATE * second + (1.0 - DECAY_RATE) * gradient * gradient
    return (
        gradient,
        second_new,
        current - VECTOR_RATE * gradient / (jnp.sqrt(second_new) + SAFE_ADD),
    )


def gelu_pair(u):
    root = math.sqrt(2.0 / math.pi)
    square = u * u
    turn = jnp.tanh(root * u * (1.0 + 0.044715 * square))
    half = 0.5 * (1.0 + turn)
    slope = half + 0.5 * u * (1.0 - turn * turn) * root * (1.0 + 3.0 * 0.044715 * square)
    return u * half, slope


def body(
    tokens,
    cotangent,
    doc_starts,
    owner,
    vectors,
    bias_query,
    bias_value,
    bias_up,
    w_query,
    w_key,
    w_value,
    w_out,
    w_up,
    w_down,
    attn_left,
    attn_right,
    attn_root_left,
    attn_root_right,
    mixer_left,
    mixer_right,
    mixer_root_left,
    mixer_root_right,
    kv_left,
    kv_right,
    kv_root_left,
    kv_root_right,
    vector_second,
    query_second,
    value_second,
    up_second,
):
    batch_size = lax.axis_size("batch")
    head_count = lax.axis_size("head")
    batch_index = lax.axis_index("batch")
    head_index = lax.axis_index("head")
    tok_dev, width = tokens.shape
    seq_len = tok_dev * head_count
    row_start = head_index * tok_dev
    head_size = w_key.shape[1]
    slab = w_query.shape[1]
    gain_one = vectors[0]
    shift_one = vectors[1]
    bias_down = vectors[5]

    positions = jnp.arange(seq_len, dtype=jnp.int32)
    documents = jnp.sum((doc_starts[0][None, :] <= positions[:, None]).astype(jnp.int32), axis=1)
    row_ids = row_start + jnp.arange(tok_dev, dtype=jnp.int32)
    row_docs = lax.dynamic_slice_in_dim(documents, row_start, tok_dev, 0)
    allowed = (documents[:, None] == row_docs[None, :]) & (positions[:, None] <= row_ids[None, :])
    mask = jnp.where(allowed, 0.0, MASKED).astype(F32)

    w_query_all, w_out_part, bias_all = gather_weights(
        w_query, w_out, bias_query.reshape(1, slab), batch_size, head_count
    )
    w_out_part, cotangent_later, tokens_later = lax.optimization_barrier(
        (w_out_part, cotangent, tokens)
    )
    cot_all = lax.all_gather(cotangent_later, "head", axis=0, tiled=True)
    rows_own = tokens_later.astype(F32)
    normed_one, inverse_one = norm_stats(rows_own)
    normed_in = (normed_one * gain_one + shift_one).astype(BF16)
    w_kv = jnp.concatenate([w_key, w_value], axis=1)
    kv_bias = jnp.concatenate([jnp.zeros_like(bias_value), bias_value])
    kv_own = (matmul(normed_in, w_kv) + kv_bias).astype(BF16)
    w_out_all, kv_all = gather_rest(w_out_part, kv_own, batch_size, head_count)

    queries = (matmul(normed_in, w_query_all) + bias_all.reshape(1, width)).astype(BF16)
    attended, log_totals = attention_forward(queries, kv_all, mask, head_count)
    resid, mixer_in, normed_two, inverse_wide = project_out(
        attended, w_out_all, tokens, vectors
    )

    mix_a, mix_b, grad_up, down_shares, grad_mixer_in, grad_up_bias = mixer_pass(
        mixer_in, cot_all, w_up, w_down, bias_up, owner, batch_size, head_count, 2
    )
    mix_first = lax.psum_scatter(mix_a, "head", scatter_dimension=0, tiled=True)
    up_shares = lax.psum_scatter(grad_up, "batch", scatter_dimension=0, tiled=True)

    kv_rows = width // head_count // batch_size
    grad_tokens, query_share, out_share, kv_total, vector_wide, up_bias_total = backward_pass(
        owner,
        grad_mixer_in,
        cotangent,
        tokens,
        normed_two,
        inverse_wide,
        vectors,
        queries,
        attended,
        log_totals,
        kv_all,
        mask.astype(BF16),
        w_query_all,
        w_out_all,
        w_kv,
        grad_up_bias.reshape(8, -1),
        batch_size,
        head_count,
    )
    kv_total, mix_first = lax.optimization_barrier((kv_total, mix_first))
    up_shares, mix_first = lax.optimization_barrier((up_shares, mix_first))
    mix_second = lax.psum_scatter(mix_b, "head", scatter_dimension=0, tiled=True)
    kv_total = kv_total.reshape(batch_size * kv_rows, 2 * head_size)
    up_bias_total = up_bias_total.reshape(-1)
    vector_all = vector_wide.transpose(1, 0, 2).reshape(8, width)
    vector_total = vector_all[:6]
    query_bias_total = lax.dynamic_slice_in_dim(vector_all[6], head_index * slab, slab, 0)
    value_bias_total = vector_all[7, :head_size]

    owned_count = attn_left.shape[1]
    owned = lax.dynamic_slice_in_dim(owner, batch_index * owned_count, owned_count, 0)
    mixer_out = shampoo(
        up_shares,
        down_shares,
        w_up,
        w_down,
        owned,
        mixer_left,
        mixer_right,
        mixer_root_left,
        mixer_root_right,
        True,
        2 if owned_count % 2 == 0 else 1,
    )
    attn_out = shampoo(
        query_share,
        out_share,
        w_query,
        w_out,
        owned,
        attn_left,
        attn_right,
        attn_root_left,
        attn_root_right,
        False,
        attn_left.shape[1],
    )
    kv_count = width // head_count

    def kv_tiles(matrix):
        return matrix.reshape(kv_count // TILE, TILE, head_size // TILE, TILE).transpose(0, 2, 1, 3)

    kv_slab = lax.dynamic_slice_in_dim(w_kv, head_index * kv_count, kv_count, 0).astype(F32)
    kv_out = shampoo_update(
        jnp.stack([kv_tiles(kv_total[:, :head_size]), kv_tiles(kv_total[:, head_size:])]),
        kv_left,
        kv_right,
        kv_root_left,
        kv_root_right,
        jnp.stack([kv_tiles(kv_slab[:, :head_size]), kv_tiles(kv_slab[:, head_size:])]),
    )
    _, mix_second = lax.optimization_barrier((mixer_out[0], mix_second))
    mix_one = jnp.concatenate([mix_first, mix_second], axis=0)
    output = resid + mix_one.astype(F32) + bias_down
    vec_out = diagonal_update(vector_total, vector_second, vectors)
    query_out = diagonal_update(query_bias_total, query_second, bias_query)
    value_out = diagonal_update(value_bias_total, value_second, bias_value)
    up_out = diagonal_update(up_bias_total, up_second, bias_up)
    return (
        output,
        grad_tokens,
        vec_out[0],
        vec_out[1][2:],
        vec_out[1][:2],
        vec_out[2],
        query_out[0],
        query_out[1],
        query_out[2],
        value_out[0],
        value_out[1],
        value_out[2],
        up_out[0],
        up_out[1],
        up_out[2],
        attn_out[0],
        attn_out[1],
        attn_out[2],
        attn_out[3],
        mixer_out[0],
        mixer_out[1],
        mixer_out[2],
        mixer_out[3],
        kv_out[0],
        kv_out[1],
        kv_out[2],
        kv_out[3],
    )


def solution(mesh):
    rows = P(("batch", "head"), None)
    whole = P()
    head = P("head")
    tiles = P(None, "batch", "head", None, None)
    kv_tiles = P(None, "head", None, None, None)
    in_specs = (
        rows,
        rows,
        P("batch", None),
        whole,
        whole,
        head,
        whole,
        head,
        P(None, "head"),
        whole,
        whole,
        P("head", None),
        P(None, "head"),
        P("head", None),
        *([tiles] * 8),
        *([kv_tiles] * 4),
        whole,
        head,
        whole,
        head,
    )
    out_specs = (
        rows,
        rows,
        *([whole] * 4),
        *([head] * 3),
        *([whole] * 3),
        *([head] * 3),
        *([tiles] * 8),
        *([kv_tiles] * 4),
    )
    return jax.shard_map(body, mesh=mesh, in_specs=in_specs, out_specs=out_specs, check_vma=False)
```

```python
from functools import partial
import math

import jax
import jax.numpy as jnp
from jax import lax
from jax.experimental import pallas as pl
from jax.experimental.pallas import tpu as pltpu
from jax.sharding import PartitionSpec as P

EPSILON = 1e-05
DECAY_RATE = 0.5
MATRIX_RATE = 0.01
VECTOR_RATE = 0.1
SAFE_ADD = 1e-08
PRECISE = lax.Precision.HIGHEST
LOG2E = math.log2(math.e)
MASKED = -1e30
TILE = 128
MESH = pl.DeviceIdType.MESH
BF16 = jnp.bfloat16
F32 = jnp.float32
VMEM_LIMIT = 60 * 1024 * 1024
ANY = pl.BlockSpec(memory_space=pl.ANY)
WHOLE = pl.BlockSpec(memory_space=pltpu.VMEM)


def matmul(first_op, second_op):
    return jnp.dot(first_op, second_op, preferred_element_type=F32)


def matmul_t(first_op, second_op):
    return lax.dot_general(
        first_op, second_op, (((0,), (0,)), ((), ())), preferred_element_type=F32
    )


def matmul_nt(first_op, second_op):
    return lax.dot_general(
        first_op, second_op, (((1,), (1,)), ((), ())), preferred_element_type=F32
    )


def norm_stats(rows_in):
    mean_row = jnp.mean(rows_in, axis=-1, keepdims=True)
    centered = rows_in - mean_row
    variance = jnp.mean(centered * centered, axis=-1, keepdims=True)
    inverse = lax.rsqrt(variance + EPSILON)
    return (centered * inverse, inverse)


def norm_back(grad_out, normed, inverse, gain):
    scaled = grad_out * gain
    mean_one = jnp.mean(scaled, axis=-1, keepdims=True)
    mean_two = jnp.mean(scaled * normed, axis=-1, keepdims=True)
    return inverse * (scaled - mean_one - normed * mean_two)


def lanes(start, size, unit):
    return pl.ds(pl.multiple_of(start, unit), size)


def greet(targets):
    barrier = pltpu.get_barrier_semaphore()
    for target in targets:
        pl.semaphore_signal(barrier, inc=1, device_id=target, device_id_type=MESH)
    pl.semaphore_wait(barrier, len(targets))


def gather_tools(batch_size, head_count):
    chips = head_count // 2
    b = lax.axis_index("batch")
    h = lax.axis_index("head")
    z = h // 2
    c = h % 2

    def at(chip):
        return {"head": chip * 2 + c}

    def peer(k):
        return {"batch": b ^ k}

    def remote(src, dst, send, recv, target):
        return pltpu.make_async_remote_copy(
            src_ref=src,
            dst_ref=dst,
            send_sem=send,
            recv_sem=recv,
            device_id=target,
            device_id_type=MESH,
        )

    others = [lax.rem(z + i, chips) for i in range(1, chips)]
    return b, h, z, c, {"head": h + 1 - 2 * c}, at, peer, remote, others


def plane_exchange(place, tools, sems, batch_size):
    b, _, _, _, sibling, _, peer, remote, others = tools
    xs, xr, fs, fr, cs, cr = sems
    ring = batch_size == 4
    direct = (1, 2) if ring else tuple(range(1, batch_size))

    def hop(k, chip):
        spot = place(b, chip)
        return remote(spot, spot, xs.at[k, chip], xr.at[k, chip], peer(k))

    def half(k, chip):
        spot = place(b ^ k, chip, k - 1)
        return remote(spot, spot, fs.at[k, chip], fr.at[k, chip], peer(3 - k))

    def side(k, chip):
        spot = place(b ^ k, chip)
        return remote(spot, spot, cs.at[k, chip], cr.at[k, chip], sibling)

    def start(chip):
        for k in direct:
            hop(k, chip).start()
        side(0, chip).start()

    def turn():
        for chip in others:
            for k in direct:
                hop(k, chip).wait_recv()
                if ring:
                    half(k, chip).start()
                side(k, chip).start()

    def close():
        if ring:
            for chip in others:
                for k in direct:
                    half(k, chip).wait_recv()
                side(3, chip).start()

    def finish():
        for chip in others:
            for k in range(batch_size):
                side(k, chip).wait()
            for k in direct:
                hop(k, chip).wait_send()
                if ring:
                    half(k, chip).wait_send()

    return start, turn, close, finish


def place_rows(w_all, rows, core, batch_size):
    def place(quarter, chip, half=None):
        part = rows // batch_size
        if half is not None:
            part = part // 2
            quarter = quarter * 2 + half
        return w_all.at[lanes((chip * 2 + core) * rows + quarter * part, part, part), :]

    return place


def gather_weights(w_query, w_out, bias_local, batch_size, head_count):
    rows, cols = w_query.shape
    chips = head_count // 2

    def kernel(
        q_ref, w_ref, bias_ref, q_all, w_all, bias_all, loc, right, left, line, ys, yr, sides_s,
        sides_r, xs, xr, fs, fr, cs, cr, bs, br,
    ):
        tools = gather_tools(batch_size, head_count)
        b, h, z, c, sibling, at, peer, remote, others = tools
        has_left = z > 0
        has_right = z < chips - 1

        def other(d):
            return {"head": lax.rem(h + d, head_count)}

        def place_query(quarter, chip, half=None):
            part = rows // batch_size
            if half is not None:
                part = part // 2
                quarter = quarter * 2 + half
            head = chip * 2 + c
            return q_all.at[lanes(quarter * part, part, part), lanes(head * cols, cols, cols)]

        places = (place_query, place_rows(w_all, cols, c, batch_size))
        greet([other(d) for d in range(1, head_count)] + [peer(k) for k in range(1, batch_size)])
        own = (q_all.at[:, lanes(h * cols, cols, cols)], w_all.at[lanes(h * cols, cols, cols), :])
        q_part, w_part = rows // batch_size, cols // batch_size
        mine = (
            q_ref.at[lanes(b * q_part, q_part, q_part), :],
            w_ref.at[lanes(b * w_part, w_part, w_part), :],
        )

        def z_copy(m, chip, to_right, src=None):
            spot = places[m](b, chip)
            src = spot if src is None else src
            if to_right:
                return remote(src, spot, right.at[m, chip], line.at[m, chip], at(z + 1))
            return remote(src, spot, left.at[m, chip], line.at[m, chip], at(z - 1))

        def z_first(m):
            @pl.when(has_right)
            def _():
                z_copy(m, z, True, mine[m]).start()

            @pl.when(has_left)
            def _():
                z_copy(m, z, False, mine[m]).start()

        def z_steps(m, d, then):
            @pl.when(z >= d)
            def _():
                z_copy(m, z - d, True).wait_recv()

                @pl.when(has_right)
                def _():
                    z_copy(m, z - d, True).start()

                then(z - d)

            @pl.when(z + d < chips)
            def _():
                z_copy(m, z + d, False).wait_recv()

                @pl.when(has_left)
                def _():
                    z_copy(m, z + d, False).start()

                then(z + d)

        z_first(0)
        locals_ = [
            pltpu.make_async_copy(src, own[m], loc.at[m]) for m, src in enumerate((q_ref, w_ref))
        ]
        slices = [
            remote(src, own[m], ys.at[m], yr.at[m], sibling) for m, src in enumerate((q_ref, w_ref))
        ]
        biases = [
            remote(bias_ref, bias_all.at[h], bs.at[d], br.at[d], other(d))
            for d in range(1, head_count)
        ]
        bias_own = pltpu.make_async_copy(bias_ref, bias_all.at[h], bs.at[0])
        for copy in locals_ + slices + biases + [bias_own]:
            copy.start()

        start, turn, close, finish = plane_exchange(
            place_query, tools, (xs, xr, fs, fr, cs, cr), batch_size
        )

        def side(chip):
            spot = places[1](b, chip)
            return remote(spot, spot, sides_s.at[chip], sides_r.at[chip], sibling)

        for d in range(1, chips):
            z_steps(0, d, start)
            if d == 1:
                z_first(1)
        turn()
        for d in range(1, chips):
            z_steps(1, d, lambda chip: side(chip).start())
        close()
        finish()
        for chip in others:
            side(chip).wait()
        for m in range(2):

            @pl.when(has_right)
            def _():
                z_copy(m, z, True, mine[m]).wait_send()

            @pl.when(has_left)
            def _():
                z_copy(m, z, False, mine[m]).wait_send()

            for d in range(1, chips):

                @pl.when((z >= d) & has_right)
                def _():
                    z_copy(m, z - d, True).wait_send()

                @pl.when((z + d < chips) & has_left)
                def _():
                    z_copy(m, z + d, False).wait_send()

        for copy in locals_ + slices + biases + [bias_own]:
            copy.wait()

    dma = pltpu.SemaphoreType.DMA
    hop = dma((batch_size, chips))
    two = dma((2, chips))
    return pl.pallas_call(
        kernel,
        out_shape=(
            jax.ShapeDtypeStruct((rows, cols * head_count), w_query.dtype),
            jax.ShapeDtypeStruct((cols * head_count, w_out.shape[1]), w_out.dtype),
            jax.ShapeDtypeStruct((head_count, 1, cols), F32),
        ),
        in_specs=[WHOLE] * 3,
        out_specs=(ANY,) * 3,
        scratch_shapes=[
            dma((2,)), two, two, two, dma((2,)), dma((2,)), dma((chips,)), dma((chips,)),
            hop, hop, hop, hop, hop, hop, dma((head_count,)), dma((head_count,)),
        ],
        compiler_params=pltpu.CompilerParams(collective_id=0, has_side_effects=True),
        cost_estimate=pl.CostEstimate(
            flops=0, bytes_accessed=120 * 1024 * 1024, transcendentals=0
        ),
        name="gather_weights",
    )(w_query, w_out, bias_local)


def gather_rest(w_all, kv_own, batch_size, head_count):
    chips = head_count // 2
    rows = w_all.shape[0] // head_count
    tok, kv_cols = kv_own.shape

    def kernel(
        in_ref, kv_ref, w_ref, kv_all, xs, xr, fs, fr, cs, cr, own_sem, zs, zr, ss, sr
    ):
        del in_ref
        tools = gather_tools(batch_size, head_count)
        _, h, z, c, sibling, at, peer, remote, others = tools
        greet([sibling] + [at(chip) for chip in others] + [peer(k) for k in range(1, batch_size)])

        def place(chip):
            return kv_all.at[lanes((chip * 2 + c) * tok, tok, tok), :]

        own = pltpu.make_async_copy(kv_ref, place(z), own_sem)
        own.start()

        def away(i):
            return remote(kv_ref, place(z), zs.at[i], zr.at[i], at(others[i]))

        def side(chip):
            src = kv_ref if chip is z else place(chip)
            return remote(src, place(chip), ss.at[chip], sr.at[chip], sibling)

        for i in range(chips - 1):
            away(i).start()
        side(z).start()
        start, turn, close, finish = plane_exchange(
            place_rows(w_ref, rows, c, batch_size), tools, (xs, xr, fs, fr, cs, cr), batch_size
        )
        for chip in others:
            start(chip)
        turn()
        for i in range(chips - 1):
            away(i).wait_recv()
            side(others[chips - 2 - i]).start()
        close()
        finish()
        side(z).wait()
        for i in range(chips - 1):
            side(others[i]).wait()
            away(i).wait_send()
        own.wait()

    dma = pltpu.SemaphoreType.DMA
    hop = dma((batch_size, chips))
    line = dma((chips,))
    return pl.pallas_call(
        kernel,
        out_shape=(
            jax.ShapeDtypeStruct(w_all.shape, w_all.dtype),
            jax.ShapeDtypeStruct((head_count * tok, kv_cols), kv_own.dtype),
        ),
        in_specs=[ANY, WHOLE],
        out_specs=(ANY, ANY),
        scratch_shapes=[hop] * 6 + [dma, line, line, line, line],
        input_output_aliases={0: 0},
        compiler_params=pltpu.CompilerParams(collective_id=5, has_side_effects=True),
        cost_estimate=pl.CostEstimate(
            flops=0, bytes_accessed=100 * 1024 * 1024, transcendentals=0
        ),
        name="gather_rest",
    )(w_all, kv_own)


def project_out(attended, weight, tokens, vectors):
    tok, width = attended.shape

    def kernel(att_ref, tok_ref, vec_ref, w_ref, resid_ref, mixer_ref, normed_ref, inverse_ref):
        resid = matmul(att_ref[...], w_ref[...]) + vec_ref[4:5, :] + tok_ref[...].astype(F32)
        normed, inverse = norm_stats(resid)
        resid_ref[...] = resid
        normed_ref[...] = normed
        inverse_ref[...] = jnp.broadcast_to(inverse, inverse_ref.shape)
        mixer_ref[...] = (normed * vec_ref[2:3, :] + vec_ref[3:4, :]).astype(BF16)

    return pl.pallas_call(
        kernel,
        out_shape=(
            jax.ShapeDtypeStruct((tok, width), F32),
            jax.ShapeDtypeStruct((tok, width), BF16),
            jax.ShapeDtypeStruct((tok, width), F32),
            jax.ShapeDtypeStruct((tok, TILE), F32),
        ),
        in_specs=[WHOLE] * 4,
        out_specs=(WHOLE,) * 4,
        compiler_params=pltpu.CompilerParams(vmem_limit_bytes=VMEM_LIMIT),
        cost_estimate=pl.CostEstimate(
            flops=2 * tok * width * width, bytes_accessed=14 * width * width, transcendentals=0
        ),
        name="project_out",
    )(attended, tokens, vectors, weight)


def mixer_pass(mixer_in, cot_all, w_up, w_down, bias_up, owner, batch_size, head_count, cuts):
    tok, width = mixer_in.shape
    hid = w_up.shape[1]
    n = head_count // 2
    sub = tok // cuts
    block = (n, 2, cuts, sub)
    tiles = width // TILE
    owned = tiles // batch_size
    total_events = n * cuts
    pieces = 4
    piece = sub // pieces

    def kernel(
        owner_ref, x_ref, cot_ref, up_ref, down_ref, bias_ref,
        all_ref, hid_ref, pre_ref, mix_a_ref, mix_b_ref, grad_up_ref, down_ref_all, out_ref,
        sum_ref,
        x_buf, cot_buf, hid_buf, pre_buf, mine, give, pair_in, chain_in, right_in,
        up_acc, down_acc, stage, grad_down_ref,
        own_sem, x_sem, cot_sem, hid_sem, pre_sem, mix_sem,
        right_send, left_send, side_send, side_recv, line_recv,
        pair_send, pair_recv, chain_send, chain_recv, last_recv, down_send, down_recv, down_sem,
    ):
        mix_refs = (mix_a_ref, mix_b_ref)
        h = lax.axis_index("head")
        z = h // 2
        c = h % 2
        has_left = z > 0
        has_right = z < n - 1

        def at(chip):
            return {"head": chip * 2 + c}

        sibling = {"head": h + 1 - 2 * c}

        def remote(src, dst, send, recv, target):
            return pltpu.make_async_remote_copy(
                src_ref=src, dst_ref=dst, send_sem=send, recv_sem=recv,
                device_id=target, device_id_type=MESH,
            )

        def row_copy(chip, g, way):
            spot = all_ref.at[chip, c, g]
            if way == 0:
                return remote(spot, spot, right_send.at[chip, g], line_recv.at[chip, g], at(z + 1))
            if way == 1:
                return remote(spot, spot, left_send.at[chip, g], line_recv.at[chip, g], at(z - 1))
            return remote(spot, spot, side_send.at[chip, g], side_recv.at[chip, g], sibling)

        def pair_copy(chip, g):
            return remote(
                give.at[chip, g], pair_in.at[chip, g], pair_send.at[chip, g],
                pair_recv.at[chip, g], sibling,
            )

        def chain_copy(chip, g, e, target):
            part = pl.ds(e * piece, piece)
            return remote(
                mine.at[chip, g, part], chain_in.at[chip, g, part], chain_send.at[chip, g, e],
                chain_recv.at[chip, g, e], at(target),
            )

        def last_copy(chip, g, e):
            part = pl.ds(e * piece, piece)
            return remote(
                mine.at[chip, g, part], right_in.at[g, part], chain_send.at[chip, g, e],
                last_recv.at[g, e], at(z - 1),
            )

        b = lax.axis_index("batch")

        def peer(k):
            return {"batch": b ^ k}

        def down_copy(k):
            return remote(
                grad_down_ref.at[pl.ds((b ^ k) * owned, owned)], down_ref_all.at[k],
                down_send.at[k], down_recv.at[k], peer(k),
            )

        def down_own():
            return pltpu.make_async_copy(
                grad_down_ref.at[pl.ds(b * owned, owned)], down_ref_all.at[0], down_sem
            )

        barrier = pltpu.get_barrier_semaphore()
        pl.semaphore_signal(barrier, inc=1, device_id=sibling, device_id_type=MESH)
        for k in range(1, batch_size):
            pl.semaphore_signal(barrier, inc=1, device_id=peer(k), device_id_type=MESH)

        @pl.when(has_left)
        def _():
            pl.semaphore_signal(barrier, inc=1, device_id=at(z - 1), device_id_type=MESH)

        @pl.when(has_right)
        def _():
            pl.semaphore_signal(barrier, inc=1, device_id=at(z + 1), device_id_type=MESH)

        own = pltpu.make_async_copy(x_ref, all_ref.at[z, c], own_sem)
        own.start()
        sum_ref[...] = jnp.zeros_like(sum_ref)
        up_acc[...] = jnp.zeros_like(up_acc)
        down_acc[...] = jnp.zeros_like(down_acc)
        pl.semaphore_wait(
            barrier, batch_size + has_left.astype(jnp.int32) + has_right.astype(jnp.int32)
        )
        own.wait()

        def pass_on(chip, g):
            @pl.when((chip <= z) & has_right)
            def _():
                row_copy(chip, g, 0).start()

            @pl.when((chip >= z) & has_left)
            def _():
                row_copy(chip, g, 1).start()

            row_copy(chip, g, 2).start()

        for g in range(cuts):
            pass_on(z, g)

        def compute(chip, g):
            cot_load = pltpu.make_async_copy(cot_ref.at[chip, :, g], cot_buf, cot_sem)
            cot_load.start()
            row_copy(chip, g, 2).wait_recv()
            x_load = pltpu.make_async_copy(all_ref.at[chip, :, g], x_buf, x_sem)
            x_load.start()
            cot_load.wait()
            grad_hidden = matmul_nt(cot_buf[...].reshape(2 * sub, width), down_ref[...])
            x_load.wait()
            pre_act = matmul(x_buf[...].reshape(2 * sub, width), up_ref[...]) + bias_ref[...]
            hidden, slope = gelu_pair(pre_act)
            hid_buf[...] = hidden.astype(BF16).reshape(2, sub, hid)
            hid_store = pltpu.make_async_copy(hid_buf, hid_ref.at[chip, :, g], hid_sem)
            hid_store.start()
            grad_pre = (grad_hidden * slope).astype(BF16)
            pre_buf[...] = grad_pre.reshape(2, sub, hid)
            pre_store = pltpu.make_async_copy(pre_buf, pre_ref.at[chip, :, g], pre_sem)
            pre_store.start()
            sum_ref[...] += jnp.sum(
                grad_pre.astype(F32).reshape(2 * sub // 8, 8, hid), axis=0
            )
            share = matmul_nt(grad_pre, up_ref[...]).astype(BF16).reshape(2, sub, width)

            @pl.when(c == 0)
            def _():
                mine[chip, g] = share[0]
                give[chip, g] = share[1]

            @pl.when(c == 1)
            def _():
                mine[chip, g] = share[1]
                give[chip, g] = share[0]

            pair_copy(chip, g).start()
            down_acc[...] += matmul_t(
                cot_buf[...].reshape(2 * sub, width), hid_buf[...].reshape(2 * sub, hid)
            ).reshape(tiles, TILE, hid)
            hid_store.wait()
            pre_store.wait()

        def nearest(i):
            edge = jnp.minimum(z, n - 1 - z)
            near = (i + 1) // 2
            inner = jnp.where(i % 2 == 1, z - near, z + near)
            far = i - edge
            outer = jnp.where(z < n - 1 - z, z + far, z - far)
            return jnp.where(i <= 2 * edge, inner, outer)

        def compute_rest(index):
            chip = nearest(index // cuts)
            g = index % cuts
            loads = [
                pltpu.make_async_copy(hid_ref.at[chip, :, g], hid_buf, hid_sem),
                pltpu.make_async_copy(all_ref.at[chip, :, g], x_buf, x_sem),
                pltpu.make_async_copy(pre_ref.at[chip, :, g], pre_buf, pre_sem),
            ]
            for load in loads:
                load.start()
            loads[0].wait()
            hidden = hid_buf[...].reshape(2 * sub, hid)
            stage[...] = matmul(hidden, down_ref[...]).astype(BF16).reshape(2, sub, width)
            for cut in range(cuts):

                @pl.when(g == cut)
                def _():
                    pltpu.make_async_copy(stage, mix_refs[cut].at[chip], mix_sem).start()

            loads[1].wait()
            loads[2].wait()
            up_acc[...] += matmul_t(
                x_buf[...].reshape(2 * sub, width), pre_buf[...].reshape(2 * sub, hid)
            ).reshape(tiles, TILE, hid)
            pltpu.make_async_copy(stage, mix_refs[0].at[chip], mix_sem).wait()

        def add_up(chip, g, e, more):
            part = pl.ds(e * piece, piece)
            total = mine[chip, g, part, :].astype(F32) + pair_in[chip, g, part, :].astype(F32)

            @pl.when(more)
            def _():
                chain_copy(chip, g, e, z).wait_recv()
                mine[chip, g, part, :] = (
                    total + chain_in[chip, g, part, :].astype(F32)
                ).astype(BF16)

            @pl.when(jnp.logical_not(more))
            def _():
                mine[chip, g, part, :] = total.astype(BF16)

        def step(t, carry):
            d = t // cuts
            g = t % cuts

            @pl.when((d > 0) & (z >= d))
            def _():
                row_copy(z - d, g, 0).wait_recv()
                pass_on(z - d, g)

            @pl.when((d > 0) & (z + d < n))
            def _():
                row_copy(z + d, g, 1).wait_recv()
                pass_on(z + d, g)

            def one_side(side, inner):
                chip = z + d * (2 * side - 1)

                @pl.when((chip >= 0) & (chip < n) & (d < n) & ((d > 0) | (side == 0)))
                def _():
                    compute(chip, g)

                return inner

            lax.fori_loop(0, 2, one_side, 0)

            @pl.when(t == (jnp.maximum(z, n - 1 - z) + 1) * cuts - 1)
            def _():
                def put_down(p, inner):
                    grad_down_ref[p] = down_acc[owner_ref[p]].astype(BF16)
                    return inner

                lax.fori_loop(0, tiles, put_down, 0)
                for k in range(1, batch_size):
                    down_copy(k).start()
                down_own().start()

            from_left = jnp.maximum(t - z, 0)
            chip_right = from_left // cuts
            g_right = from_left % cuts

            @pl.when((t >= z) & (chip_right > z) & (chip_right < n))
            def _():
                pair_copy(chip_right, g_right).wait_recv()
                for e in range(pieces):
                    add_up(chip_right, g_right, e, has_left)
                    chain_copy(chip_right, g_right, e, z + 1).start()

            from_right = jnp.maximum(t - (n - 1 - z), 0)
            chip_left = n - 1 - from_right // cuts
            g_left = from_right % cuts

            @pl.when((t >= n - 1 - z) & (chip_left < z) & (chip_left >= 0))
            def _():
                pair_copy(chip_left, g_left).wait_recv()
                for e in range(pieces):
                    add_up(chip_left, g_left, e, has_right)

                    @pl.when(chip_left == z - 1)
                    def _():
                        last_copy(chip_left, g_left, e).start()

                    @pl.when(chip_left < z - 1)
                    def _():
                        chain_copy(chip_left, g_left, e, z - 1).start()

            events = (z >= d).astype(jnp.int32) + (z + d < n).astype(jnp.int32)
            events = jnp.where((d == 0) | (d >= n), 1, events)
            ready = (events < 2) & (carry < total_events)

            @pl.when(ready)
            def _():
                compute_rest(carry)

            return carry + ready.astype(jnp.int32)

        done = lax.fori_loop(0, n * cuts + n - 1, step, 0)

        def left_over(index, carry):
            @pl.when(index >= done)
            def _():
                compute_rest(index)

            return carry

        lax.fori_loop(0, total_events, left_over, 0)

        def put_tile(p, carry):
            grad_up_ref[p] = up_acc[owner_ref[p]].astype(BF16)
            return carry

        lax.fori_loop(0, tiles, put_tile, 0)

        for g in range(cuts):
            pair_copy(z, g).wait_recv()
            out_ref[g] = mine[z, g].astype(F32) + pair_in[z, g].astype(F32)

            @pl.when(has_left)
            def _():
                for e in range(pieces):
                    chain_copy(z, g, e, z).wait_recv()
                out_ref[g] += chain_in[z, g].astype(F32)

            @pl.when(has_right)
            def _():
                for e in range(pieces):
                    last_copy(z, g, e).wait_recv()
                out_ref[g] += right_in[g].astype(F32)

        def finish(chip, carry):
            for g in range(cuts):

                @pl.when((chip <= z) & has_right)
                def _():
                    row_copy(chip, g, 0).wait_send()

                @pl.when((chip >= z) & has_left)
                def _():
                    row_copy(chip, g, 1).wait_send()

                row_copy(chip, g, 2).wait_send()
                pair_copy(chip, g).wait_send()

                @pl.when(chip != z)
                def _():
                    for e in range(pieces):
                        chain_copy(chip, g, e, z).wait_send()

            return carry

        lax.fori_loop(0, n, finish, 0)
        for k in range(1, batch_size):
            down_copy(k).wait()
        down_own().wait()

    dma = pltpu.SemaphoreType.DMA
    vm = pltpu.VMEM
    each = dma((n, cuts))
    shares = vm((n, cuts, sub, width), BF16)
    outs = pl.pallas_call(
        kernel,
        out_shape=(
            jax.ShapeDtypeStruct(block + (width,), BF16),
            jax.ShapeDtypeStruct(block + (hid,), BF16),
            jax.ShapeDtypeStruct(block + (hid,), BF16),
            jax.ShapeDtypeStruct((n, 2, sub, width), BF16),
            jax.ShapeDtypeStruct((n, 2, sub, width), BF16),
            jax.ShapeDtypeStruct((tiles, TILE, hid), BF16),
            jax.ShapeDtypeStruct((batch_size, owned, TILE, hid), BF16),
            jax.ShapeDtypeStruct((cuts, sub, width), F32),
            jax.ShapeDtypeStruct((8, hid), F32),
        ),
        in_specs=[pl.BlockSpec(memory_space=pltpu.SMEM), WHOLE, ANY, WHOLE, WHOLE, WHOLE],
        out_specs=(ANY, ANY, ANY, ANY, ANY, WHOLE, ANY, WHOLE, WHOLE),
        scratch_shapes=[
            vm((2, sub, width), BF16),
            vm((2, sub, width), BF16),
            vm((2, sub, hid), BF16),
            vm((2, sub, hid), BF16),
            shares, shares, shares, shares,
            vm((cuts, sub, width), BF16),
            vm((tiles, TILE, hid), F32),
            vm((tiles, TILE, hid), F32),
            vm((2, sub, width), BF16),
            vm((tiles, TILE, hid), BF16),
            dma, dma, dma, dma, dma, dma,
            each, each, each, each, each,
            each, each, dma((n, cuts, pieces)), dma((n, cuts, pieces)),
            dma((cuts, pieces)),
            dma((batch_size,)), dma((batch_size,)), dma,
        ],
        compiler_params=pltpu.CompilerParams(
            collective_id=3, has_side_effects=True, vmem_limit_bytes=VMEM_LIMIT
        ),
        cost_estimate=pl.CostEstimate(
            flops=12 * n * 2 * tok * width * hid, bytes_accessed=300 * 1024 * 1024, transcendentals=0
        ),
        name="mixer_pass",
    )(
        owner,
        mixer_in.reshape(cuts, sub, width),
        cot_all.reshape(block + (width,)),
        w_up,
        w_down,
        bias_up.reshape(1, hid),
    )
    _, _, _, mix_a, mix_b, grad_up, grad_down, grad_in, bias_sum = outs
    return (
        mix_a.reshape(2 * n * sub, width),
        mix_b.reshape(2 * n * sub, width),
        grad_up.reshape(batch_size, owned * TILE, hid),
        grad_down.reshape(batch_size, owned * TILE, hid),
        grad_in.reshape(tok, width),
        jnp.sum(bias_sum, axis=0),
    )


def attention_forward(queries, kv_all, mask, slabs):
    tok, width = queries.shape
    seq_len, head_size = kv_all.shape[0], kv_all.shape[1] // 2
    slab = width // slabs
    heads = slab // head_size
    scale = LOG2E / math.sqrt(head_size)

    def kernel(q_ref, k_ref, v_ref, mask_ref, o_ref, log_ref, turned):
        @pl.when(pl.program_id(0) == 0)
        def _():
            turned[...] = v_ref[...].astype(F32).T.astype(BF16)

        for j in range(heads):
            spot = slice(j * head_size, (j + 1) * head_size)
            scores = matmul_nt(k_ref[...], q_ref[:, spot]) * scale + mask_ref[...]
            highest = jnp.max(scores, axis=0, keepdims=True)
            raised = jnp.exp2(scores - highest)
            total = jnp.sum(raised, axis=0, keepdims=True)
            out = matmul(turned[...], raised.astype(BF16)) / total
            o_ref[:, spot] = out.T.astype(BF16)
            log_ref[0, j : j + 1, :] = highest + jnp.log2(total)

    return pl.pallas_call(
        kernel,
        grid=(slabs,),
        out_shape=(
            jax.ShapeDtypeStruct((tok, width), BF16),
            jax.ShapeDtypeStruct((slabs, heads, tok), F32),
        ),
        in_specs=[
            pl.BlockSpec((tok, slab), lambda i: (0, i)),
            pl.BlockSpec((seq_len, head_size), lambda i: (0, 0)),
            pl.BlockSpec((seq_len, head_size), lambda i: (0, 1)),
            pl.BlockSpec((seq_len, tok), lambda i: (0, 0)),
        ],
        out_specs=(
            pl.BlockSpec((tok, slab), lambda i: (0, i)),
            pl.BlockSpec((1, heads, tok), lambda i: (i, 0, 0)),
        ),
        scratch_shapes=[pltpu.VMEM((head_size, seq_len), BF16)],
        compiler_params=pltpu.CompilerParams(vmem_limit_bytes=VMEM_LIMIT),
        cost_estimate=pl.CostEstimate(
            flops=8 * tok * seq_len * width,
            bytes_accessed=4 * tok * width,
            transcendentals=tok * seq_len * slabs * heads,
        ),
        name="attention_forward",
    )(queries, kv_all, kv_all, mask)


def backward_pass(
    owner, grad_mixer, cotangent, tokens, normed_two, inverse_two, vectors, queries, attended,
    log_totals, kv_all, mask, w_query_all, w_out_all, w_kv, up_parts,
    batch_size, head_count,
):
    tok, width = tokens.shape
    seq_len, head_size = kv_all.shape[0], kv_all.shape[1] // 2
    slab = width // head_count
    heads = slab // head_size
    n = head_count // 2
    tiles = width // TILE
    cols_out = width // batch_size
    half_rows = slab // 2
    kv_cols = 2 * head_size
    kv_rows = width // head_count // batch_size
    ring = batch_size == 4
    scale = LOG2E / math.sqrt(head_size)
    plain_scale = 1.0 / math.sqrt(head_size)
    block = 512 if seq_len % 512 == 0 else seq_len

    def kernel(
        owner_ref, gm_ref, cot_ref, tok_ref, n2_ref, i2_ref, vec_ref, q_ref, att_ref, log_ref,
        keys_ref, mask_ref, wq_ref, wo_ref, wkv_ref, up_ref,
        tokens_out, query_out, out_out, kv_out, vec_out, up_out,
        branch, kt_ref, wide_tiles, normed_owned, branch_owned, grad_in, wq_buf, wo_buf, dk, dv,
        give, mine, pair_in, land, hop, z_land,
        dkv, dkv_pair, dkv_here, dkv_land,
        kv_part, kv_pair, kv_sum, kv_land, kv_half, kv_zland,
        vec_part, vec_land, vec_sum, vec_bland, up_land,
        gm_sem, n2_sem, cot_sem, free_sem, wq_sem, wo_sem, pair_send, pair_recv, hop_send, hop_recv, land_send, land_recv,
        z_send, z_recv, dkv_s, dkv_r, dkz_s, dkz_r,
        s_pair, r_pair, s_kvb, r_kvb, s_kvz, r_kvz, s_kva, r_kva,
        s_vh, r_vh, s_vb, r_vb, s_va, r_va, s_up, r_up,
    ):
        b = lax.axis_index("batch")
        h = lax.axis_index("head")
        z = h // 2
        c = h % 2
        sibling = {"head": h + 1 - 2 * c}

        def at_chip(r):
            return {"head": lax.rem(z + r, n) * 2 + c}

        def other(d):
            return {"head": lax.rem(h + d, head_count)}

        def peer(k):
            return {"batch": b ^ k}

        def remote(src, dst, send, recv, target):
            return pltpu.make_async_remote_copy(
                src_ref=src, dst_ref=dst, send_sem=send, recv_sem=recv,
                device_id=target, device_id_type=MESH,
            )

        greet([other(d) for d in range(1, head_count)] + [peer(k) for k in range(1, batch_size)])

        up_copies = [
            remote(up_ref, up_land.at[k], s_up.at[k], r_up.at[k], peer(k))
            for k in range(1, batch_size)
        ]
        for copy in up_copies:
            copy.start()

        def slab_at(s):
            chip = lax.rem(z + 1 + s // 2, n)
            return chip * 2 + jnp.where(s % 2 == 0, 1 - c, c)

        def weight_loads(s):
            i = slab_at(s)
            return (
                pltpu.make_async_copy(
                    wq_ref.at[:, lanes(i * slab, slab, slab)], wq_buf, wq_sem
                ),
                pltpu.make_async_copy(
                    wo_ref.at[lanes(i * slab, slab, slab), :], wo_buf, wo_sem
                ),
            )

        norm_loads = (
            pltpu.make_async_copy(gm_ref, tokens_out, gm_sem),
            pltpu.make_async_copy(n2_ref, grad_in, n2_sem),
            pltpu.make_async_copy(cot_ref, branch, cot_sem),
        )
        for load in norm_loads + weight_loads(0):
            load.start()

        def put_vector(row, value):
            for i in range(head_count):
                vec_part[i, row : row + 1, :] = value[:, i * slab : (i + 1) * slab]

        def column_sum(value):
            return jnp.sum(value, axis=0, keepdims=True)

        for load in norm_loads:
            load.wait()
        grad_mix = tokens_out[...]
        normed_two_rows = grad_in[...]
        grad_out_rows = branch[...].astype(F32)
        put_vector(5, column_sum(grad_out_rows))
        grad_resid = grad_out_rows + norm_back(
            grad_mix, normed_two_rows, i2_ref[:, :1], vec_ref[2:3, :]
        )
        put_vector(2, column_sum(grad_mix * normed_two_rows))
        put_vector(3, column_sum(grad_mix))
        tokens_out[...] = grad_resid
        grad_branch = grad_resid.astype(BF16)
        branch[...] = grad_branch

        put_vector(4, column_sum(grad_branch.astype(F32)))

        for p in range(tiles):
            wide_tiles[p] = branch[:, p * TILE : (p + 1) * TILE]

        for p in range(tiles):
            branch_owned[:, p * TILE : (p + 1) * TILE] = wide_tiles[owner_ref[p]]
        normed_one, inverse_one = norm_stats(tok_ref[...].astype(F32))
        normed_in = (normed_one * vec_ref[0:1, :] + vec_ref[1:2, :]).astype(BF16)
        for p in range(tiles):
            wide_tiles[p] = normed_in[:, p * TILE : (p + 1) * TILE]

        for p in range(tiles):
            normed_owned[:, p * TILE : (p + 1) * TILE] = wide_tiles[owner_ref[p]]
        kt_ref[...] = keys_ref[:, :head_size].astype(F32).T.astype(BF16)
        dk[...] = jnp.zeros_like(dk)
        dv[...] = jnp.zeros_like(dv)
        grad_in[...] = jnp.zeros_like(grad_in)

        def pair_copy(q):
            return remote(
                give.at[q % 2], pair_in.at[q % 2], pair_send.at[q], pair_recv.at[q], sibling
            )

        halves = (pl.ds(0, half_rows), pl.ds(half_rows, half_rows))

        def hop_copy(q, k):
            part = halves[1 if k == 1 else 0]
            return remote(
                mine.at[q, b ^ 3, part], hop.at[q, k - 1], hop_send.at[q, k], hop_recv.at[q, k],
                peer(k),
            )

        def land_copy(q, k, which):
            if which is None:
                return remote(
                    mine.at[q, b ^ k], land.at[q, k - 1], land_send.at[q, k, 0],
                    land_recv.at[q, k, 0], peer(k),
                )
            part = halves[which]
            return remote(
                mine.at[q, b ^ k, part], land.at[q, k - 1, part], land_send.at[q, k, which],
                land_recv.at[q, k, which], peer(k),
            )

        def z_copy(q):
            return remote(
                mine.at[q, b], z_land.at[q], z_send.at[q], z_recv.at[q], at_chip(q % n + 1)
            )

        def pair_start(q, value):
            @pl.when(q >= 2)
            def _():
                pair_copy(q - 2).wait_send()
                pl.semaphore_wait(free_sem, 1)

            for k in range(batch_size):
                give[q % 2, k] = value[:, k * cols_out : (k + 1) * cols_out]
            pair_copy(q).start()

        def plane_start(q):
            pair_copy(q).wait_recv()
            mine[q] = (mine[q].astype(F32) + pair_in[q % 2].astype(F32)).astype(BF16)

            @pl.when(q < 2 * n - 2)
            def _():
                pl.semaphore_signal(free_sem, inc=1, device_id=sibling, device_id_type=MESH)

            if ring:
                hop_copy(q, 1).start()
                hop_copy(q, 2).start()
                land_copy(q, 1, 1).start()
                land_copy(q, 2, 0).start()
            else:
                for k in range(1, batch_size):
                    land_copy(q, k, None).start()

        def plane_hop(q):
            if not ring:
                return
            for k in (1, 2):
                hop_copy(q, 3 - k).wait_recv()
                which = 0 if k == 1 else 1
                part = halves[which]
                mine[q, b ^ k, part, :] = (
                    mine[q, b ^ k, part, :].astype(F32) + hop[q, 2 - k].astype(F32)
                ).astype(BF16)
                land_copy(q, k, which).start()

        def plane_end(q):
            total = mine[q, b].astype(F32)
            for k in range(1, 3 if ring else batch_size):
                for which in (0, 1) if ring else (None,):
                    land_copy(q, k, which).wait_recv()
                total += land[q, k - 1].astype(F32)
            mine[q, b] = total.astype(BF16)

            @pl.when(q % n < n - 1)
            def _():
                z_copy(q).start()

        def out_gradient(i):
            att = att_ref[:, lanes(i * slab, slab, slab)]
            return matmul(att.astype(F32).T.astype(BF16), branch_owned[...]).astype(BF16)

        def put_mine(q, value):
            for k in range(batch_size):
                mine[q, k] = value[:, k * cols_out : (k + 1) * cols_out]

        def out_pairs(j, carry):
            pair_start(j, out_gradient(slab_at(2 * j)))
            put_mine(j, out_gradient(slab_at(2 * j + 1)))

            @pl.when(j >= 1)
            def _():
                plane_start(j - 1)

            return carry

        lax.fori_loop(0, n, out_pairs, 0)
        plane_start(n - 1)

        def work(s, carry):
            j = s // 2
            i = slab_at(s)
            cols = lanes(i * slab, slab, slab)

            loads = weight_loads(s)
            loads[1].wait()
            grad_att = matmul_nt(branch[...], wo_buf[...]).astype(BF16)

            @pl.when(s + 1 < head_count)
            def _():
                weight_loads(s + 1)[1].start()

            queries_here = q_ref[:, cols]
            att_here = att_ref[:, cols]
            logs_here = log_ref[i]
            parts = []
            for e in range(heads):
                spot = slice(e * head_size, (e + 1) * head_size)
                query = queries_here[:, spot]
                grad = grad_att[:, spot]
                joint = grad.astype(F32) * att_here[:, spot].astype(F32)
                delta = jnp.sum(joint.T, axis=0, keepdims=True)
                logs = logs_here[e : e + 1, :]
                total = jnp.zeros((head_size, tok), F32)
                for start in range(0, seq_len, block):
                    part = slice(start, start + block)
                    scores = matmul_nt(keys_ref[part, :head_size], query) * scale
                    probs = jnp.exp2(scores + (mask_ref[part, :].astype(F32) - logs))
                    grad_probs = matmul_nt(keys_ref[part, head_size:], grad)
                    grad_scores = (probs * (grad_probs - delta)).astype(BF16)
                    dv[part, :] += matmul(probs.astype(BF16), grad)
                    dk[part, :] += matmul(grad_scores, query)
                    total += matmul(kt_ref[:, part], grad_scores)
                parts.append(total * plain_scale)
            turned = jnp.concatenate(parts, axis=0) if heads > 1 else parts[0]
            grad_q = turned.T.astype(BF16)
            vec_part[i, 6:7, :] = column_sum(grad_q.astype(F32))
            grad_query = matmul(turned.astype(BF16), normed_owned[...]).astype(BF16)

            @pl.when(s % 2 == 0)
            def _():
                pair_start(n + j, grad_query)

            @pl.when(s % 2 == 1)
            def _():
                put_mine(n + j, grad_query)

            loads[0].wait()
            grad_in[...] += matmul_nt(grad_q, wq_buf[...])

            @pl.when(s + 1 < head_count)
            def _():
                weight_loads(s + 1)[0].start()

            @pl.when(s < n)
            def _():
                plane_hop(s)

            @pl.when((s >= 2) & (s < n + 2))
            def _():
                plane_end(s - 2)

            @pl.when(s % 2 == 1)
            def _():
                plane_start(n + j)

                @pl.when(j >= 1)
                def _():
                    plane_hop(n + j - 1)

                @pl.when(j >= 2)
                def _():
                    plane_end(n + j - 2)

            return carry

        lax.fori_loop(0, head_count, work, 0)

        dkv[:, :, :, :head_size] = (dk[...] * plain_scale).astype(BF16).reshape(n, 2, tok, head_size)
        dkv[:, :, :, head_size:] = dv[...].astype(BF16).reshape(n, 2, tok, head_size)
        dkv_swap = remote(dkv.at[:, 1 - c], dkv_pair, dkv_s, dkv_r, sibling)
        dkv_swap.start()
        dkv_swap.wait_recv()
        for r in range(n):
            dkv_here[r] = (dkv[r, c].astype(F32) + dkv_pair[r].astype(F32)).astype(BF16)
        dkv_copies = [
            remote(
                dkv_here.at[lax.rem(z + r, n)], dkv_land.at[r], dkz_s.at[r], dkz_r.at[r],
                at_chip(r),
            )
            for r in range(1, n)
        ]
        for copy in dkv_copies:
            copy.start()
        normed_one, inverse_one = norm_stats(tok_ref[...].astype(F32))
        normed_in = (normed_one * vec_ref[0:1, :] + vec_ref[1:2, :]).astype(BF16)
        plane_hop(2 * n - 1)
        grad_kv = dkv_here[z].astype(F32)
        for copy in dkv_copies:
            copy.wait_recv()
        for r in range(1, n):
            grad_kv += dkv_land[r].astype(F32)
        grad_kv = grad_kv.astype(BF16)

        kv_part[...] = (
            matmul_t(normed_in, grad_kv)
            .astype(BF16)
            .reshape(n, 2, batch_size, kv_rows, kv_cols)
        )
        pair_kv = remote(kv_part.at[:, 1 - c], kv_pair, s_pair, r_pair, sibling)
        pair_kv.start()

        grad_normed = grad_in[...] + matmul_nt(grad_kv, wkv_ref[...])
        pair_kv.wait_recv()
        for r in range(n):
            kv_sum[r] = (kv_part[r, c].astype(F32) + kv_pair[r].astype(F32)).astype(BF16)
        kv_copies = [
            remote(kv_sum.at[:, b ^ k], kv_land.at[k], s_kvb.at[k], r_kvb.at[k], peer(k))
            for k in range(1, batch_size)
        ]
        for copy in kv_copies:
            copy.start()
        put_vector(0, column_sum(grad_normed * normed_one))
        put_vector(1, column_sum(grad_normed))
        for i in range(head_count):
            vec_part[i, 7:8, :] = jnp.zeros((1, slab), F32)
        vec_part[0, 7:8, :head_size] = column_sum(grad_kv[:, head_size:].astype(F32))
        vec_copies = [
            remote(
                vec_part.at[lax.rem(h + d, head_count)], vec_land.at[d], s_vh.at[d], r_vh.at[d],
                other(d),
            )
            for d in range(1, head_count)
        ]
        for copy in vec_copies:
            copy.start()
        tokens_out[...] += norm_back(grad_normed, normed_one, inverse_one, vec_ref[0:1, :])
        total = vec_part[h]
        for copy in vec_copies:
            copy.wait_recv()
        for d in range(1, head_count):
            total += vec_land[d]
        vec_sum[...] = total
        vec_bcopies = [
            remote(vec_sum, vec_bland.at[k], s_vb.at[k], r_vb.at[k], peer(k))
            for k in range(1, batch_size)
        ]
        for copy in vec_bcopies:
            copy.start()
        up_total = up_ref[...]
        for copy in up_copies:
            copy.wait_recv()
        for k in range(1, batch_size):
            up_total += up_land[k]
        up_out[...] = up_total
        for copy in kv_copies:
            copy.wait_recv()
        kv_total = kv_sum[:, b].astype(F32)
        for k in range(1, batch_size):
            kv_total += kv_land[k].astype(F32)
        kv_half[...] = kv_total.astype(BF16)
        kv_zcopies = [
            remote(
                kv_half.at[lax.rem(z + r, n)], kv_zland.at[r], s_kvz.at[r], r_kvz.at[r], at_chip(r)
            )
            for r in range(1, n)
        ]
        for copy in kv_zcopies:
            copy.start()
        for copy in vec_bcopies:
            copy.wait_recv()
        total = vec_sum[...]
        for k in range(1, batch_size):
            total += vec_bland[k]
        vec_out[h] = total
        vec_acopies = [
            remote(vec_out.at[h], vec_out.at[h], s_va.at[d], r_va.at[d], other(d))
            for d in range(1, head_count)
        ]
        for copy in vec_acopies:
            copy.start()
        for copy in kv_zcopies:
            copy.wait_recv()
        kv_mine = kv_half[z].astype(F32)
        for r in range(1, n):
            kv_mine += kv_zland[r].astype(F32)
        kv_out[b] = kv_mine
        kv_acopies = [
            remote(kv_out.at[b], kv_out.at[b], s_kva.at[k], r_kva.at[k], peer(k))
            for k in range(1, batch_size)
        ]
        for copy in kv_acopies:
            copy.start()

        plane_end(2 * n - 2)
        plane_end(2 * n - 1)
        for first, target in ((0, out_out), (n, query_out)):
            total = mine[first + n - 1, b].astype(F32)
            for r in range(n - 1):
                z_copy(first + r).wait_recv()
                total += z_land[first + r].astype(F32)
            target[0] = total.astype(BF16)
        for copy in vec_acopies + kv_acopies:
            copy.wait_recv()

        for copy in up_copies + [dkv_swap, pair_kv] + dkv_copies + vec_copies + kv_copies:
            copy.wait_send()
        for copy in vec_bcopies + kv_zcopies + vec_acopies + kv_acopies:
            copy.wait_send()
        pair_copy(2 * n - 2).wait_send()
        pair_copy(2 * n - 1).wait_send()

        def finish(q, carry):
            @pl.when(q % n < n - 1)
            def _():
                z_copy(q).wait_send()

            if ring:
                for k in (1, 2):
                    hop_copy(q, k).wait_send()
                    for which in (0, 1):
                        land_copy(q, k, which).wait_send()
            else:
                for k in range(1, batch_size):
                    land_copy(q, k, None).wait_send()
            return carry

        lax.fori_loop(0, 2 * n, finish, 0)

    dma = pltpu.SemaphoreType.DMA
    vm = pltpu.VMEM
    nb, nh = batch_size, head_count
    lands = 2 if ring else nb - 1
    shared = (nb, slab, cols_out)
    return pl.pallas_call(
        kernel,
        out_shape=(
            jax.ShapeDtypeStruct((tok, width), F32),
            jax.ShapeDtypeStruct((1, slab, cols_out), BF16),
            jax.ShapeDtypeStruct((1, slab, cols_out), BF16),
            jax.ShapeDtypeStruct((nb, kv_rows, kv_cols), F32),
            jax.ShapeDtypeStruct((nh, 8, slab), F32),
            jax.ShapeDtypeStruct(up_parts.shape, F32),
        ),
        in_specs=[pl.BlockSpec(memory_space=pltpu.SMEM), ANY, ANY, WHOLE, ANY]
        + [WHOLE] * 7
        + [ANY, ANY, WHOLE, WHOLE],
        out_specs=(WHOLE,) * 6,
        scratch_shapes=[
            vm((tok, width), BF16),
            vm((head_size, seq_len), BF16),
            vm((tiles, tok, TILE), BF16),
            vm((tok, width), BF16),
            vm((tok, width), BF16),
            vm((tok, width), F32),
            vm((width, slab), BF16),
            vm((slab, width), BF16),
            vm((seq_len, head_size), F32),
            vm((seq_len, head_size), F32),
            vm((2,) + shared, BF16),
            vm((2 * n,) + shared, BF16),
            vm((2,) + shared, BF16),
            vm((2 * n, lands, slab, cols_out), BF16),
            vm((2 * n, 2, half_rows, cols_out) if ring else (1, 1, 16, TILE), BF16),
            vm((2 * n, slab, cols_out), BF16),
            vm((n, 2, tok, kv_cols), BF16),
            vm((n, tok, kv_cols), BF16),
            vm((n, tok, kv_cols), BF16),
            vm((n, tok, kv_cols), BF16),
            vm((n, 2, nb, kv_rows, kv_cols), BF16),
            vm((n, nb, kv_rows, kv_cols), BF16),
            vm((n, nb, kv_rows, kv_cols), BF16),
            vm((nb, n, kv_rows, kv_cols), BF16),
            vm((n, kv_rows, kv_cols), BF16),
            vm((n, kv_rows, kv_cols), BF16),
            vm((nh, 8, slab), F32),
            vm((nh, 8, slab), F32),
            vm((8, slab), F32),
            vm((nb, 8, slab), F32),
            vm((nb,) + up_parts.shape, F32),
            dma, dma, dma, pltpu.SemaphoreType.REGULAR, dma, dma,
            dma((2 * n,)), dma((2 * n,)), dma((2 * n, 3)), dma((2 * n, 3)),
            dma((2 * n, nb, 2)), dma((2 * n, nb, 2)), dma((2 * n,)), dma((2 * n,)), dma, dma, dma((n,)), dma((n,)),
            dma, dma, dma((nb,)), dma((nb,)), dma((n,)), dma((n,)), dma((nb,)), dma((nb,)),
            dma((nh,)), dma((nh,)), dma((nb,)), dma((nb,)), dma((nh,)), dma((nh,)),
            dma((nb,)), dma((nb,)),
        ],
        compiler_params=pltpu.CompilerParams(
            collective_id=4, has_side_effects=True, vmem_limit_bytes=VMEM_LIMIT + 2 * 1024 * 1024
        ),
        cost_estimate=pl.CostEstimate(
            flops=20 * tok * seq_len * width + 8 * tok * width * width,
            bytes_accessed=200 * 1024 * 1024,
            transcendentals=tok * seq_len * width // head_size,
        ),
        name="backward_pass",
    )(
        owner, grad_mixer, cotangent, tokens, normed_two, inverse_two, vectors, queries, attended,
        log_totals, kv_all, mask, w_query_all, w_out_all, w_kv, up_parts,
    )


def split_high(value):
    high = value.astype(BF16)
    return high, (value - high.astype(F32)).astype(BF16)


def matmul_three(first_op, second_op):
    first_high, first_low = split_high(first_op)
    second_high, second_low = split_high(second_op)
    return (
        matmul(first_high, second_high)
        + matmul(first_high, second_low)
        + matmul(first_low, second_high)
    )


def shampoo(
    first, second, first_weight, second_weight, owned, left, right, root_left, root_right, wide_rows,
    per_step,
):
    _, owned_count, columns, _, _ = left.shape

    steps = owned_count // per_step

    def kernel(ids_ref, *refs):
        del ids_ref
        one, two = refs[:2]
        w_one, w_two = refs[2 : 2 + per_step], refs[2 + per_step : 2 + 2 * per_step]
        l_ref, r_ref, p_ref, q_ref, g_out, l_out, r_out, w_out = refs[2 + 2 * per_step :]

        def update(turned):
            shares = two if turned else one
            tiles = [(p, t) for p in range(per_step) for t in range(columns)]
            group = 4 if len(tiles) % 4 == 0 else 1
            for first in range(0, len(tiles), group):
                here = tiles[first : first + group]
                grads = []
                for p, t in here:
                    wide = slice(p * TILE, (p + 1) * TILE)
                    spot = slice(t * TILE, (t + 1) * TILE)
                    part = (wide, spot) if wide_rows else (spot, wide)
                    grad = shares[(0,) + part].astype(F32)
                    for i in range(1, shares.shape[0]):
                        grad += shares[(i,) + part].astype(F32)
                    grads.append(grad.T if turned == wide_rows else grad)
                highs = [grad.astype(BF16) for grad in grads]
                halfway = [matmul_three(p_ref[0, p, t], g) for (p, t), g in zip(here, grads)]
                lefts = [matmul_nt(high, high) for high in highs]
                steps_here = [matmul_three(m, q_ref[0, p, t]) for (p, t), m in zip(here, halfway)]
                rights = [matmul_t(high, high) for high in highs]
                for i, (p, t) in enumerate(here):
                    spot = slice(t * TILE, (t + 1) * TILE)
                    weight = w_two[p][spot, :] if turned else w_one[p][:, spot]
                    g_out[0, p, t] = grads[i]
                    l_out[0, p, t] = (
                        DECAY_RATE * l_ref[0, p, t] + (1.0 - DECAY_RATE) * lefts[i]
                    )
                    r_out[0, p, t] = (
                        DECAY_RATE * r_ref[0, p, t] + (1.0 - DECAY_RATE) * rights[i]
                    )
                    w_out[0, p, t] = weight.astype(F32) - MATRIX_RATE * steps_here[i]

        @pl.when(pl.program_id(0) == 0)
        def _():
            update(False)

        @pl.when(pl.program_id(0) == 1)
        def _():
            update(True)

    last = steps - 1

    def place_one(m, i):
        return jnp.where(m == 0, i, last)

    def place_two(m, i):
        return jnp.where(m == 1, i, 0)

    def share(array, place):
        if wide_rows:
            return pl.BlockSpec(
                (array.shape[0], per_step * TILE, columns * TILE),
                lambda m, i, ids: (0, place(m, i), 0),
            )
        return pl.BlockSpec(
            (array.shape[0], columns * TILE, per_step * TILE),
            lambda m, i, ids: (0, 0, place(m, i)),
        )

    def weight_one(p):
        return pl.BlockSpec(
            (TILE, columns * TILE), lambda m, i, ids: (ids[place_one(m, i) * per_step + p], 0)
        )

    def weight_two(p):
        return pl.BlockSpec(
            (columns * TILE, TILE), lambda m, i, ids: (0, ids[place_two(m, i) * per_step + p])
        )

    stat = pl.BlockSpec((1, per_step, columns, TILE, TILE), lambda m, i, ids: (m, i, 0, 0, 0))
    shape = jax.ShapeDtypeStruct(left.shape, F32)
    return pl.pallas_call(
        kernel,
        grid_spec=pltpu.PrefetchScalarGridSpec(
            num_scalar_prefetch=1,
            grid=(2, steps),
            in_specs=[share(first, place_one), share(second, place_two)]
            + [weight_one(p) for p in range(per_step)]
            + [weight_two(p) for p in range(per_step)]
            + [stat] * 4,
            out_specs=[stat] * 4,
        ),
        out_shape=[shape] * 4,
        compiler_params=pltpu.CompilerParams(vmem_limit_bytes=VMEM_LIMIT),
        cost_estimate=pl.CostEstimate(
            flops=left.size * TILE * 16, bytes_accessed=left.size * 40, transcendentals=0
        ),
        name="shampoo",
    )(
        owned,
        first,
        second,
        *([first_weight] * per_step),
        *([second_weight] * per_step),
        left,
        right,
        root_left,
        root_right,
    )


def shampoo_update(grad_tiles, left_old, right_old, root_left, root_right, weight_tiles):
    outer_left = jnp.einsum("...ij,...kj->...ik", grad_tiles, grad_tiles, precision=PRECISE)
    outer_right = jnp.einsum("...ji,...jk->...ik", grad_tiles, grad_tiles, precision=PRECISE)
    left_new = DECAY_RATE * left_old + (1.0 - DECAY_RATE) * outer_left
    right_new = DECAY_RATE * right_old + (1.0 - DECAY_RATE) * outer_right
    stepped = jnp.einsum("...ij,...jk->...ik", root_left, grad_tiles, precision=PRECISE)
    stepped = jnp.einsum("...ij,...jk->...ik", stepped, root_right, precision=PRECISE)
    return (grad_tiles, left_new, right_new, weight_tiles - MATRIX_RATE * stepped)


def diagonal_update(gradient, second, current):
    second_new = DECAY_RATE * second + (1.0 - DECAY_RATE) * gradient * gradient
    return (
        gradient,
        second_new,
        current - VECTOR_RATE * gradient / (jnp.sqrt(second_new) + SAFE_ADD),
    )


def gelu_pair(u):
    root = math.sqrt(2.0 / math.pi)
    square = u * u
    turn = jnp.tanh(root * u * (1.0 + 0.044715 * square))
    half = 0.5 * (1.0 + turn)
    slope = half + 0.5 * u * (1.0 - turn * turn) * root * (1.0 + 3.0 * 0.044715 * square)
    return u * half, slope


def body(
    tokens,
    cotangent,
    doc_starts,
    owner,
    vectors,
    bias_query,
    bias_value,
    bias_up,
    w_query,
    w_key,
    w_value,
    w_out,
    w_up,
    w_down,
    attn_left,
    attn_right,
    attn_root_left,
    attn_root_right,
    mixer_left,
    mixer_right,
    mixer_root_left,
    mixer_root_right,
    kv_left,
    kv_right,
    kv_root_left,
    kv_root_right,
    vector_second,
    query_second,
    value_second,
    up_second,
):
    batch_size = lax.axis_size("batch")
    head_count = lax.axis_size("head")
    batch_index = lax.axis_index("batch")
    head_index = lax.axis_index("head")
    tok_dev, width = tokens.shape
    seq_len = tok_dev * head_count
    row_start = head_index * tok_dev
    head_size = w_key.shape[1]
    slab = w_query.shape[1]
    gain_one = vectors[0]
    shift_one = vectors[1]
    bias_down = vectors[5]

    positions = jnp.arange(seq_len, dtype=jnp.int32)
    documents = jnp.sum((doc_starts[0][None, :] <= positions[:, None]).astype(jnp.int32), axis=1)
    row_ids = row_start + jnp.arange(tok_dev, dtype=jnp.int32)
    row_docs = lax.dynamic_slice_in_dim(documents, row_start, tok_dev, 0)
    allowed = (documents[:, None] == row_docs[None, :]) & (positions[:, None] <= row_ids[None, :])
    mask = jnp.where(allowed, 0.0, MASKED).astype(F32)

    w_query_all, w_out_part, bias_all = gather_weights(
        w_query, w_out, bias_query.reshape(1, slab), batch_size, head_count
    )
    w_out_part, cotangent_later, tokens_later = lax.optimization_barrier(
        (w_out_part, cotangent, tokens)
    )
    cot_all = lax.all_gather(cotangent_later, "head", axis=0, tiled=True)
    rows_own = tokens_later.astype(F32)
    normed_one, inverse_one = norm_stats(rows_own)
    normed_in = (normed_one * gain_one + shift_one).astype(BF16)
    w_kv = jnp.concatenate([w_key, w_value], axis=1)
    kv_bias = jnp.concatenate([jnp.zeros_like(bias_value), bias_value])
    kv_own = (matmul(normed_in, w_kv) + kv_bias).astype(BF16)
    w_out_all, kv_all = gather_rest(w_out_part, kv_own, batch_size, head_count)

    queries = (matmul(normed_in, w_query_all) + bias_all.reshape(1, width)).astype(BF16)
    attended, log_totals = attention_forward(queries, kv_all, mask, head_count)
    resid, mixer_in, normed_two, inverse_wide = project_out(
        attended, w_out_all, tokens, vectors
    )

    mix_a, mix_b, grad_up, down_shares, grad_mixer_in, grad_up_bias = mixer_pass(
        mixer_in, cot_all, w_up, w_down, bias_up, owner, batch_size, head_count, 2
    )
    mix_first = lax.psum_scatter(mix_a, "head", scatter_dimension=0, tiled=True)
    up_shares = lax.psum_scatter(grad_up, "batch", scatter_dimension=0, tiled=True)

    kv_rows = width // head_count // batch_size
    grad_tokens, query_share, out_share, kv_total, vector_wide, up_bias_total = backward_pass(
        owner,
        grad_mixer_in,
        cotangent,
        tokens,
        normed_two,
        inverse_wide,
        vectors,
        queries,
        attended,
        log_totals,
        kv_all,
        mask.astype(BF16),
        w_query_all,
        w_out_all,
        w_kv,
        grad_up_bias.reshape(8, -1),
        batch_size,
        head_count,
    )
    kv_total, mix_first = lax.optimization_barrier((kv_total, mix_first))
    up_shares, mix_first = lax.optimization_barrier((up_shares, mix_first))
    mix_second = lax.psum_scatter(mix_b, "head", scatter_dimension=0, tiled=True)
    kv_total = kv_total.reshape(batch_size * kv_rows, 2 * head_size)
    up_bias_total = up_bias_total.reshape(-1)
    vector_all = vector_wide.transpose(1, 0, 2).reshape(8, width)
    vector_total = vector_all[:6]
    query_bias_total = lax.dynamic_slice_in_dim(vector_all[6], head_index * slab, slab, 0)
    value_bias_total = vector_all[7, :head_size]

    owned_count = attn_left.shape[1]
    owned = lax.dynamic_slice_in_dim(owner, batch_index * owned_count, owned_count, 0)
    mixer_out = shampoo(
        up_shares,
        down_shares,
        w_up,
        w_down,
        owned,
        mixer_left,
        mixer_right,
        mixer_root_left,
        mixer_root_right,
        True,
        2 if owned_count % 2 == 0 else 1,
    )
    attn_out = shampoo(
        query_share,
        out_share,
        w_query,
        w_out,
        owned,
        attn_left,
        attn_right,
        attn_root_left,
        attn_root_right,
        False,
        attn_left.shape[1],
    )
    kv_count = width // head_count

    def kv_tiles(matrix):
        return matrix.reshape(kv_count // TILE, TILE, head_size // TILE, TILE).transpose(0, 2, 1, 3)

    kv_slab = lax.dynamic_slice_in_dim(w_kv, head_index * kv_count, kv_count, 0).astype(F32)
    kv_out = shampoo_update(
        jnp.stack([kv_tiles(kv_total[:, :head_size]), kv_tiles(kv_total[:, head_size:])]),
        kv_left,
        kv_right,
        kv_root_left,
        kv_root_right,
        jnp.stack([kv_tiles(kv_slab[:, :head_size]), kv_tiles(kv_slab[:, head_size:])]),
    )
    _, mix_second = lax.optimization_barrier((mixer_out[0], mix_second))
    mix_one = jnp.concatenate([mix_first, mix_second], axis=0)
    output = resid + mix_one.astype(F32) + bias_down
    vec_out = diagonal_update(vector_total, vector_second, vectors)
    query_out = diagonal_update(query_bias_total, query_second, bias_query)
    value_out = diagonal_update(value_bias_total, value_second, bias_value)
    up_out = diagonal_update(up_bias_total, up_second, bias_up)
    return (
        output,
        grad_tokens,
        vec_out[0],
        vec_out[1][2:],
        vec_out[1][:2],
        vec_out[2],
        query_out[0],
        query_out[1],
        query_out[2],
        value_out[0],
        value_out[1],
        value_out[2],
        up_out[0],
        up_out[1],
        up_out[2],
        attn_out[0],
        attn_out[1],
        attn_out[2],
        attn_out[3],
        mixer_out[0],
        mixer_out[1],
        mixer_out[2],
        mixer_out[3],
        kv_out[0],
        kv_out[1],
        kv_out[2],
        kv_out[3],
    )


def solution(mesh):
    rows = P(("batch", "head"), None)
    whole = P()
    head = P("head")
    tiles = P(None, "batch", "head", None, None)
    kv_tiles = P(None, "head", None, None, None)
    in_specs = (
        rows,
        rows,
        P("batch", None),
        whole,
        whole,
        head,
        whole,
        head,
        P(None, "head"),
        whole,
        whole,
        P("head", None),
        P(None, "head"),
        P("head", None),
        *([tiles] * 8),
        *([kv_tiles] * 4),
        whole,
        head,
        whole,
        head,
    )
    out_specs = (
        rows,
        rows,
        *([whole] * 4),
        *([head] * 3),
        *([whole] * 3),
        *([head] * 3),
        *([tiles] * 8),
        *([kv_tiles] * 4),
    )
    return jax.shard_map(body, mesh=mesh, in_specs=in_specs, out_specs=out_specs, check_vma=False)
```
